32 devices in a mesh: dp: 4 (over y, x), mp: 8 (over z, core).
Axes of the slice: x: 2, y: 2, z: 4, core: 2. Of those that a mesh axis runs over, the one named last changes fastest.
Arguments:
- tokens: bfloat16 [16384, 1024], P(('dp', 'mp')), may hold values from -6 to 6
- cotangent: bfloat16 [16384, 1024], P(('dp', 'mp')), may hold values from -6 to 6
- first_gain: float32 [1024], P(('dp', 'mp')), may hold values from 0.5 to 1.5
- second_gain: float32 [1024], P(('dp', 'mp')), may hold values from 0.5 to 1.5
- w_query: float32 [1024, 1024], P(('dp', 'mp')), may hold values from -0.1875 to 0.1875
- w_key: float32 [1024, 1024], P(('dp', 'mp')), may hold values from -0.1875 to 0.1875
- w_value: float32 [1024, 1024], P(('dp', 'mp')), may hold values from -0.1875 to 0.1875
- w_out: float32 [1024, 1024], P(('dp', 'mp')), may hold values from -2 to 2
- w_up: float32 [1024, 4096], P(('dp', 'mp')), may hold values from -0.1875 to 0.1875
- w_down: float32 [4096, 1024], P(None, ('dp', 'mp')), may hold values from -0.09375 to 0.09375
- state_rate: float32 [1024, 16], P('mp', 'dp'), may hold values from 0 to 1, as said below
- state_in: float32 [1024, 16], P('mp', 'dp'), may hold values from -1.25 to 1.25
- state_out: float32 [1024, 16], P('mp', 'dp'), may hold values from -0.3125 to 0.3125
- state_bank: float32 [4, 1024, 16], P('dp', 'mp'), may hold values from -24 to 24
- prev_link: int32 [4], replicated, may hold values from 0 to 3, each once
Outputs:
- mixed: bfloat16 [16384, 1024], P(('dp', 'mp'))
- grad_tokens: bfloat16 [16384, 1024], P(('dp', 'mp'))
- grad_first_gain: float32 [1024], P(('dp', 'mp'))
- grad_second_gain: float32 [1024], P(('dp', 'mp'))
- grad_w_query: float32 [1024, 1024], P(('dp', 'mp'))
- grad_w_key: float32 [1024, 1024], P(('dp', 'mp'))
- grad_w_value: float32 [1024, 1024], P(('dp', 'mp'))
- grad_w_out: float32 [1024, 1024], P(('dp', 'mp'))
- grad_w_up: float32 [1024, 4096], P('dp', 'mp')
- grad_w_down: float32 [4096, 1024], P('mp', 'dp')
- grad_state_rate: float32 [1024, 16], P('mp', 'dp')
- grad_state_in: float32 [1024, 16], P('mp', 'dp')
- grad_state_out: float32 [1024, 16], P('mp', 'dp')
- grad_state_bank: float32 [4, 1024, 16], P('dp', 'mp')
The draws below stay inside these ranges and needn't reach their ends.
Inputs may be any that keep to these rules, and one draw needn't show every extreme that they name: `state_rate`: rates per channel and state entry, between 0.3 / 4096 and 1 / 30. `prev_link`: every row of state_bank is named once.
All inputs are finite; a program needn't handle non-finite values.
Results may differ from the reference program's by a relative error of at most 0.013.
Values may be sent and summed in bfloat16 or wider, within the bound.
No kernel may reach another device: no remote copies, remote signals or barrier semaphores. Data moves between devices by JAX's collectives and lax.ppermute only.
A program may use at most 256 MiB of HBM per device.

```python
import math
import jax
import jax.numpy as jnp
from jax import lax

D = 1024
H = 8
HD = 128
FF = 4096
NS = 16
LEN = 4096
BLK = 512
CTX = 128
SEG = 128
WINDOWS = 4
TOKENS = 16384


def draw_state_rate(key, part):
    key = jax.random.fold_in(key, 11)
    pick_key, slow_key, fast_key = jax.random.split(key, 3)
    share = 0.5
    slow_mask = jax.random.uniform(pick_key, (D, 1)) < share
    slow_rate = jnp.exp(jax.random.uniform(slow_key, (D, NS), minval=math.log(0.3 / LEN), maxval=math.log(2.0 / LEN)))
    fast_rate = jnp.exp(jax.random.uniform(fast_key, (D, NS), minval=math.log(2.0 / LEN), maxval=math.log(1.0 / 30.0)))
    return jnp.where(slow_mask, slow_rate, fast_rate).astype(jnp.float32)


def level_of(rng, extent, cuts, smallest, top_value):
    level, own = 1.0, jax.random.fold_in(rng, 6)
    for position, parts in cuts:
        heights = jnp.exp(jax.random.uniform(jax.random.fold_in(own, position), (parts,), jnp.float32, smallest / len(cuts), top_value / len(cuts)))
        level = level * jnp.repeat(heights, extent[position] // parts).reshape([-1 if axis == position else 1 for axis in range(len(extent))])
    return level


def gaussian(stream_key, dims, width, reach, pieces=(), held_as=jnp.bfloat16):
    array = jax.random.normal(stream_key, dims, jnp.float32) * width
    if len(pieces) > 0:
        array = level_of(stream_key, dims, pieces, -0.22, 0.18) * array
    return jnp.clip(array, min=-reach, max=reach).astype(held_as)


def setup_inputs(seed: int = 0) -> dict:
    arg_keys = jax.random.split(jax.random.key(seed), 16)
    tokens = gaussian(arg_keys[0], (TOKENS, D), 1.0, 6.0, ((0, 32),))
    cotangent = gaussian(arg_keys[1], (TOKENS, D), 1.0, 6.0, ((0, 32),))
    first_gain = jnp.clip(1.0 + 0.1 * jax.random.normal(arg_keys[2], (D,), jnp.float32), 0.5, 1.5)
    second_gain = jnp.clip(1.0 + 0.1 * jax.random.normal(arg_keys[3], (D,), jnp.float32), 0.5, 1.5)
    w_query = gaussian(arg_keys[4], (D, D), D ** -0.5, 0.1875, ((0, 32),), jnp.float32)
    w_key = gaussian(arg_keys[5], (D, D), D ** -0.5, 0.1875, ((0, 32),), jnp.float32)
    w_value = gaussian(arg_keys[6], (D, D), D ** -0.5, 0.1875, ((0, 32),), jnp.float32)
    w_out = gaussian(arg_keys[7], (D, D), (D // 128) ** -0.5, 2.0, ((0, 32),), jnp.float32)
    w_up = gaussian(arg_keys[8], (D, FF), D ** -0.5, 0.1875, ((0, 32),), jnp.float32)
    w_down = gaussian(arg_keys[9], (FF, D), FF ** -0.5, 0.09375, ((1, 32),), jnp.float32)
    state_rate = draw_state_rate(jax.random.fold_in(arg_keys[15], 71), 0)
    state_in = gaussian(arg_keys[11], (D, NS), 0.2, 1.25, ((0, 8), (1, 4)), jnp.float32)
    state_out = gaussian(arg_keys[12], (D, NS), 0.05, 0.3125, ((0, 8), (1, 4)), jnp.float32)
    state_bank = gaussian(arg_keys[13], (WINDOWS, D, NS), 4.0, 24.0, ((0, 4), (1, 8)), jnp.float32)
    prev_link = jax.random.permutation(arg_keys[14], WINDOWS).astype(jnp.int32)
    return {"tokens": tokens, "cotangent": cotangent, "first_gain": first_gain, "second_gain": second_gain, "w_query": w_query, "w_key": w_key, "w_value": w_value, "w_out": w_out, "w_up": w_up, "w_down": w_down, "state_rate": state_rate, "state_in": state_in, "state_out": state_out, "state_bank": state_bank, "prev_link": prev_link}


@jax.custom_vjp
def low(v):
    return lax.optimization_barrier(v.astype(jnp.bfloat16)).astype(jnp.float32)

@jax.custom_vjp
def low_back(v):
    return v

def low_keep(v):
    return (low(v), None)

def low_pass(kept, grad):
    return (grad,)

def back_keep(v):
    return (v, None)

def back_low(kept, grad):
    return (low(grad),)
low.defvjp(low_keep, low_pass)
low_back.defvjp(back_keep, back_low)
precise = lax.Precision.HIGHEST

def layer_norm(values, gain):
    center = values - lax.optimization_barrier(jnp.mean(values, axis=-1, keepdims=True))
    spread = lax.optimization_barrier(jnp.mean(center * center, axis=-1, keepdims=True))
    return center * lax.rsqrt(spread + 1e-05) * gain

def recurrence(inputs, rate, gain_in, gain_out, initial):
    windows = inputs.shape[0]
    channels = inputs.shape[2]
    counts = LEN // SEG
    offsets = jnp.arange(SEG, dtype=jnp.int32)
    powers = jnp.exp(-rate[None, :, :] * offsets.astype(jnp.float32)[:, None, None])
    shifted = powers * jnp.exp(-rate)[None]
    kernel = jnp.einsum('tcn,cn->tc', powers, gain_in * gain_out, precision=precise)
    lag_steps = offsets[:, None] - offsets[None, :]
    selector = (lag_steps[:, :, None] == offsets[None, None, :]).astype(jnp.float32)
    toeplitz = jnp.einsum('tsk,kc->tsc', selector, kernel, precision=precise)
    blocks = inputs.reshape(windows, counts, SEG, channels)
    inside = jnp.einsum('tsc,wksc->wktc', toeplitz, blocks, precision=precise)
    tail_gain = jnp.flip(powers, 0) * gain_in[None]
    pushed = jnp.einsum('scn,wksc->wkcn', tail_gain, blocks, precision=precise)
    jump_decay = jnp.exp(-rate * SEG)

    def advance(state_now, pushed_in):
        return (jump_decay * state_now + pushed_in, state_now)
    _, starts = lax.scan(advance, initial, jnp.moveaxis(pushed, 1, 0))
    starts = jnp.moveaxis(starts, 0, 1)
    reader = shifted * gain_out[None]
    carried = jnp.einsum('tcn,wkcn->wktc', reader, starts, precision=precise)
    return (inside + carried).reshape(windows, LEN, channels)

def context_rows(recur):
    channels = recur.shape[-1]
    block_tails = recur.reshape(-1, BLK, channels)[:, BLK - CTX:, :]
    return jnp.concatenate([jnp.zeros_like(block_tails[:1]), block_tails[:-1]], axis=0)

def attend(packed):
    queries, self_keys, self_values, ctx_keys, ctx_values, opened = packed
    keys_all = jnp.concatenate([ctx_keys, self_keys], 0)
    values_all = jnp.concatenate([ctx_values, self_values], 0)
    scores = low_back(jnp.einsum('qhd,khd->hqk', queries, keys_all, precision=precise) * HD ** (-0.5))
    row_index = jnp.arange(BLK, dtype=jnp.int32)[:, None]
    col_index = jnp.arange(CTX + BLK, dtype=jnp.int32)[None, :]
    allowed = jnp.where(col_index < CTX, opened, col_index - CTX <= row_index)
    scores = jnp.where(allowed[None], scores, -jnp.inf)
    peak_score = lax.optimization_barrier(jnp.max(scores, -1, keepdims=True))
    lifted = jnp.exp(scores - peak_score)
    attn_prob = lifted / lax.optimization_barrier(jnp.sum(lifted, -1, keepdims=True))
    return jnp.einsum('hqk,khd->qhd', low(attn_prob), values_all, precision=precise)

def reference(tokens, cotangent, first_gain, second_gain, w_query, w_key, w_value, w_out, w_up, w_down, state_rate, state_in, state_out, state_bank, prev_link):
    block_count = TOKENS // BLK

    def project(values, weight):
        return low_back(low(jnp.dot(values, weight, precision=precise)))

    def forward(token_f, gain_one, gain_two, query_w, key_w, value_w, out_w, up_w, down_w, rate, gain_in, gain_out, bank):
        gain_one = low(gain_one)
        gain_two = low(gain_two)
        query_w = low(query_w)
        key_w = low(key_w)
        value_w = low(value_w)
        out_w = low(out_w)
        up_w = low(up_w)
        down_w = low(down_w)
        normed_b = low(layer_norm(token_f, gain_one))
        sent = low_back(normed_b)
        initial = bank[prev_link]
        recur = recurrence(sent.reshape(WINDOWS, LEN, D), rate, gain_in, gain_out, initial)
        context = low_back(low(context_rows(recur))).reshape(-1, D)
        queries = project(normed_b, query_w).reshape(block_count, BLK, H, HD)
        self_keys = project(normed_b, key_w).reshape(block_count, BLK, H, HD)
        self_values = project(normed_b, value_w).reshape(block_count, BLK, H, HD)
        ctx_keys = project(context, key_w).reshape(block_count, CTX, H, HD)
        ctx_values = project(context, value_w).reshape(block_count, CTX, H, HD)
        opened = jnp.arange(block_count, dtype=jnp.int32) * BLK % LEN != 0
        mixed_heads = lax.map(jax.checkpoint(attend), (queries, self_keys, self_values, ctx_keys, ctx_values, opened))
        attended = low_back(low(mixed_heads.reshape(TOKENS, D)))
        middle = token_f + low_back(jnp.dot(attended, out_w, precision=precise))
        second_b = low(layer_norm(middle, gain_two))
        hidden = low_back(jnp.dot(second_b, up_w, precision=precise))
        active_b = low(jax.nn.gelu(hidden, approximate=False))
        return middle + low_back(jnp.dot(active_b, down_w, precision=precise))
    primal = (tokens.astype(jnp.float32), first_gain, second_gain, w_query, w_key, w_value, w_out, w_up, w_down, state_rate, state_in, state_out, state_bank)
    result, pullback = jax.vjp(forward, *primal)
    grads = pullback(cotangent.astype(jnp.float32))
    return (result.astype(jnp.bfloat16), grads[0].astype(jnp.bfloat16), grads[1], grads[2], grads[3], grads[4], grads[5], grads[6], grads[7], grads[8], grads[9], grads[10], grads[11], grads[12])
```

```python
import functools

import jax
import jax.numpy as jnp
from jax import lax
from jax.experimental import pallas as pl
from jax.experimental.pallas import tpu as pltpu
from jax.sharding import PartitionSpec as P

D = 1024
H = 8
HD = 128
FF = 4096
NS = 16
LEN = 4096
BLK = 512
CTX = 128
OWN = BLK - CTX
HALF = D // 2
SCALE = HD ** (-0.5)
AXES = ("dp", "mp")
f32 = jnp.float32
bf16 = jnp.bfloat16
VMEM = pl.BlockSpec(memory_space=pltpu.VMEM)
SMEM = pl.BlockSpec(memory_space=pltpu.SMEM)
ANY = pl.BlockSpec(memory_space=pl.ANY)
NT = (((1,), (1,)), ((), ()))
TN = (((0,), (0,)), ((), ()))


def params(mib):
    return pltpu.CompilerParams(vmem_limit_bytes=mib * 1024 * 1024)


def cost(flops, bytes_accessed, trans=0):
    return pl.CostEstimate(flops=flops, bytes_accessed=bytes_accessed, transcendentals=trans)


def bits_of(n):
    return n.bit_length() - 1


def swap_bits(word, count):
    out = 0
    for i in range(count):
        out = out | (((word >> i) & 1) << (count - 1 - i))
    return out


class Links:
    def __init__(self):
        self.ndp = lax.axis_size("dp")
        self.nmp = lax.axis_size("mp")
        self.nz = self.nmp // 2
        self.dp = lax.axis_index("dp")
        self.mp = lax.axis_index("mp")
        self.z = self.mp // 2
        self.core = self.mp % 2
        self.dp_bits = bits_of(self.ndp)
        self.mp_bits = bits_of(self.nmp)

    def send(self, values, target):
        pairs = []
        for d in range(self.ndp):
            for m in range(self.nmp):
                to = target(d, m)
                if to is not None:
                    pairs.append((d * self.nmp + m, to[0] * self.nmp + to[1]))
        return lax.ppermute(values, AXES, pairs)

    def mp_swap(self, values, bit):
        return self.send(values, lambda d, m: (d, m ^ (1 << bit)))

    def dp_swap(self, values, bit):
        return self.send(values, lambda d, m: (d ^ (1 << bit), m))

    def core_swap(self, values):
        return self.mp_swap(values, 0)

    def fan(self, values, level):
        other = self.dp_bits - 1 - level
        return self.send(
            values, lambda d, m: (d ^ (1 << (other if m % 2 else level)), m)
        )

    def block_at(self, position):
        mirrored = swap_bits(position, self.dp_bits)
        return self.dp ^ jnp.where(self.core == 0, mirrored, position)

    def window_shift(self, values, step):
        per = LEN // BLK

        def target(d, m):
            inside = m % per + step
            return (d, m + step) if 0 <= inside < per else None

        return self.send(values, target)


def by_core(links, first, second, axis):
    return jnp.where(
        links.core == 0,
        jnp.concatenate([first, second], axis),
        jnp.concatenate([second, first], axis),
    )


def spread_rows(src_ref, dst_ref, rows, start=0):
    for r in range(0, rows, 16):
        block = src_ref[start + r : start + r + 16, :].astype(f32)
        for j in range(8):
            dst_ref[r : r + 16, j, :] = block[:, j * 128 : (j + 1) * 128]


def gather_rows(src_ref, dst_ref, rows):
    for r in range(0, rows, 16):
        for j in range(8):
            dst_ref[r : r + 16, j * 128 : (j + 1) * 128] = src_ref[r : r + 16, j, :].astype(
                dst_ref.dtype
            )


def scan_kernel(rows, x_ref, rate_ref, out_ref, xs):
    spread_rows(x_ref, xs, rows)
    decay = jnp.exp(-rate_ref[...])
    zero = jnp.zeros((NS, 8, 128), f32)

    def step(i, carry):
        u, v = carry
        for k in range(8):
            v = decay * v + u
            u = decay * u + xs[i * 8 + k][None]
        return u, v

    u, v = lax.fori_loop(0, rows // 8, step, (zero, zero))
    out_ref[0] = u
    out_ref[1] = v


def state_scan(values, rate):
    rows = values.shape[0]
    return pl.pallas_call(
        functools.partial(scan_kernel, rows),
        out_shape=jax.ShapeDtypeStruct((2, NS, 8, 128), f32),
        in_specs=[VMEM, VMEM],
        out_specs=VMEM,
        scratch_shapes=[pltpu.VMEM((rows, 8, 128), f32)],
        compiler_params=params(24),
        cost_estimate=cost(rows * 64 * 1024, rows * 2048),
        name="state_scan",
    )(values, rate)


def context_kernel(x_ref, start_ref, decay_ref, weight_ref, out_ref, xs, ys):
    spread_rows(x_ref, xs, CTX)
    decay = decay_ref[...]
    weight = weight_ref[...]

    def step(i, y):
        for k in range(8):
            y = decay * y + weight * xs[i * 8 + k][None]
            ys[i * 8 + k] = jnp.sum(y, axis=0)
        return y

    lax.fori_loop(0, CTX // 8, step, start_ref[...])
    gather_rows(ys, out_ref, CTX)


def context_states(tail, start, decay, weight):
    return pl.pallas_call(
        context_kernel,
        out_shape=jax.ShapeDtypeStruct((CTX, D), bf16),
        in_specs=[VMEM] * 4,
        out_specs=VMEM,
        scratch_shapes=[pltpu.VMEM((CTX, 8, 128), f32)] * 2,
        compiler_params=params(16),
        cost_estimate=cost(CTX * 64 * 1024, CTX * 4096),
        name="context_states",
    )(tail, start, decay, weight)


def state_sums_kernel(g_ref, x_ref, start_ref, decay_ref, sums_ref, gs, xs):
    spread_rows(g_ref, gs, CTX)
    spread_rows(x_ref, xs, CTX)
    part = NS // 2
    for n in range(0, NS, part):
        decay = decay_ref[n : n + part]
        zero = jnp.zeros((part, 8, 128), f32)

        def step(i, carry):
            u, v, su, sv = carry
            for k in range(4):
                v = decay * v + u
                u = decay * u + xs[i * 4 + k][None]
                g = gs[i * 4 + k][None]
                su = su + g * u
                sv = sv + g * v
            return u, v, su, sv

        _, _, su, sv = lax.fori_loop(
            0,
            CTX // 4,
            step,
            (start_ref[0, n : n + part], start_ref[1, n : n + part], zero, zero),
        )
        sums_ref[0, n : n + part] = su
        sums_ref[1, n : n + part] = sv
    decay = decay_ref[...]
    zero = jnp.zeros((NS, 8, 128), f32)

    def back(i, carry):
        low, slope = carry
        for k in range(8):
            slope = decay * slope + low
            low = decay * low + gs[CTX - 1 - (i * 8 + k)][None]
        return low, slope

    low, slope = lax.fori_loop(0, CTX // 8, back, (zero, zero))
    sums_ref[2] = low
    sums_ref[3] = slope


def state_sums(grad_context, tail, start, decay):
    return pl.pallas_call(
        state_sums_kernel,
        out_shape=jax.ShapeDtypeStruct((4, NS, 8, 128), f32),
        in_specs=[VMEM] * 4,
        out_specs=VMEM,
        scratch_shapes=[pltpu.VMEM((CTX, 8, 128), f32)] * 2,
        compiler_params=params(16),
        cost_estimate=cost(CTX * 192 * 1024, CTX * 4096),
        name="state_sums",
    )(grad_context, tail, start, decay)


def sent_tail_kernel(g_ref, start_ref, decay_ref, weight_ref, out_ref, gs, ys):
    spread_rows(g_ref, gs, CTX)
    decay = decay_ref[...]
    weight = weight_ref[...]

    def back(i, y):
        for k in range(8):
            t = CTX - 1 - (i * 8 + k)
            y = decay * y + weight * gs[t][None]
            ys[t] = jnp.sum(y, axis=0)
        return y

    lax.fori_loop(0, CTX // 8, back, start_ref[...])
    gather_rows(ys, out_ref, CTX)


def sent_tail(grad_context, start, decay, weight):
    return pl.pallas_call(
        sent_tail_kernel,
        out_shape=jax.ShapeDtypeStruct((CTX, D), bf16),
        in_specs=[VMEM] * 4,
        out_specs=VMEM,
        scratch_shapes=[pltpu.VMEM((CTX, 8, 128), f32)] * 2,
        compiler_params=params(16),
        cost_estimate=cost(CTX * 64 * 1024, CTX * 4096),
        name="sent_tail",
    )(grad_context, start, decay, weight)


def sent_own_kernel(start_ref, decay_ref, out_ref, ys):
    decay = decay_ref[...]

    def back(i, y):
        for k in range(8):
            y = decay * y
            ys[OWN - 1 - (i * 8 + k)] = jnp.sum(y, axis=0)
        return y

    lax.fori_loop(0, OWN // 8, back, start_ref[...])
    gather_rows(ys, out_ref, OWN)


def sent_own(start, decay):
    return pl.pallas_call(
        sent_own_kernel,
        out_shape=jax.ShapeDtypeStruct((OWN, D), bf16),
        in_specs=[VMEM] * 2,
        out_specs=VMEM,
        scratch_shapes=[pltpu.VMEM((OWN, 8, 128), f32)],
        compiler_params=params(16),
        cost_estimate=cost(OWN * 32 * 1024, OWN * 2048),
        name="sent_own",
    )(start, decay)


def attention_mask(keys, queries, first_query, opened):
    row = lax.broadcasted_iota(jnp.int32, (keys, queries), 0)
    col = lax.broadcasted_iota(jnp.int32, (keys, queries), 1) + first_query
    return jnp.where(row < CTX, (1 - opened) * BLK, row - CTX) <= col


def head_parts(own_ref, ctx_ref, offset):
    q = own_ref[:, pl.ds(offset, HD)]
    k = jnp.concatenate(
        [ctx_ref[:, pl.ds(offset, HD)], own_ref[:, pl.ds(HALF + offset, HD)]], 0
    )
    v = jnp.concatenate(
        [ctx_ref[:, pl.ds(HALF + offset, HD)], own_ref[:, pl.ds(2 * HALF + offset, HD)]], 0
    )
    return q, k, v


def probabilities(k, q, first_query, opened):
    scores = lax.dot_general(k, q, NT, preferred_element_type=f32) * SCALE
    scores = jnp.where(
        attention_mask(k.shape[0], q.shape[0], first_query, opened), scores, -jnp.inf
    )
    lifted = jnp.exp(scores - jnp.max(scores, axis=0, keepdims=True))
    return lifted * (1.0 / jnp.sum(lifted, axis=0, keepdims=True))


QT = BLK // 2


def attend_kernel(info, own_ref, other_ref, ctx_own_ref, ctx_other_ref, out_ref):
    opened = info[1]
    sides = ((own_ref, ctx_own_ref), (other_ref, ctx_other_ref))

    @pl.loop(0, H // 2)
    def _(h):
        offset = pl.multiple_of(h * HD, HD)
        for side, (qkv, ctx) in enumerate(sides):
            q, k, v = head_parts(qkv, ctx, offset)
            v_t = v.T
            home = pl.multiple_of((side ^ info[0]) * HALF + h * HD, HD)
            for first in range(0, BLK, QT):
                keys = CTX + first + QT
                p = probabilities(k[:keys], q[first : first + QT], first, opened).astype(bf16)
                mixed = jnp.dot(v_t[:, :keys], p, preferred_element_type=f32)
                out_ref[first : first + QT, pl.ds(home, HD)] = mixed.T.astype(bf16)


def attend(info, own, other, ctx_own, ctx_other):
    return pl.pallas_call(
        attend_kernel,
        out_shape=jax.ShapeDtypeStruct((BLK, D), bf16),
        in_specs=[SMEM] + [VMEM] * 4,
        out_specs=VMEM,
        compiler_params=params(32),
        cost_estimate=cost(4 * BLK * 640 * D, 6 * 2**20, H * 640 * BLK),
        name="attend",
    )(info, own, other, ctx_own, ctx_other)


def attend_back_kernel(
    info, own_ref, other_ref, ctx_own_ref, ctx_other_ref, grad_ref, g_own_ref, g_other_ref, acc
):
    opened = info[1]
    sides = ((own_ref, ctx_own_ref, g_own_ref), (other_ref, ctx_other_ref, g_other_ref))
    for _, _, g in sides:
        g[:CTX, :HALF] = jnp.zeros((CTX, HALF), bf16)

    @pl.loop(0, H // 2)
    def _(h):
        offset = pl.multiple_of(h * HD, HD)
        for side, (qkv, ctx, g) in enumerate(sides):
            q, k, v = head_parts(qkv, ctx, offset)
            k_t = k.T
            home = pl.multiple_of((side ^ info[0]) * HALF + h * HD, HD)
            for first in range(0, BLK, QT):
                keys = CTX + first + QT
                q_now = q[first : first + QT]
                go = grad_ref[first : first + QT, pl.ds(home, HD)]
                p = probabilities(k[:keys], q_now, first, opened)
                gp = lax.dot_general(v[:keys], go, NT, preferred_element_type=f32)
                mean = jnp.sum(p * gp, axis=0, keepdims=True)
                gs = (p * (gp - mean)).astype(bf16)
                gq_t = jnp.dot(k_t[:, :keys], gs, preferred_element_type=f32) * SCALE
                g[CTX + first : CTX + first + QT, pl.ds(offset, HD)] = gq_t.T.astype(bf16)
                gk = jnp.dot(gs, q_now, preferred_element_type=f32)
                gv = jnp.dot(p.astype(bf16), go, preferred_element_type=f32)
                if first == 0:
                    acc[0, :keys] = gk
                    acc[1, :keys] = gv
                else:
                    early = CTX + QT
                    gk_all = jnp.concatenate([gk[:early] + acc[0, :early], gk[early:]], 0)
                    gv_all = jnp.concatenate([gv[:early] + acc[1, :early], gv[early:]], 0)
                    g[:, pl.ds(HALF + offset, HD)] = (gk_all * SCALE).astype(bf16)
                    g[:, pl.ds(2 * HALF + offset, HD)] = gv_all.astype(bf16)


def attend_back(info, own, other, ctx_own, ctx_other, grad):
    out = jax.ShapeDtypeStruct((CTX + BLK, 3 * HALF), bf16)
    return pl.pallas_call(
        attend_back_kernel,
        out_shape=(out, out),
        in_specs=[SMEM] + [VMEM] * 5,
        out_specs=(VMEM, VMEM),
        scratch_shapes=[pltpu.VMEM((2, CTX + QT, HD), f32)],
        compiler_params=params(32),
        cost_estimate=cost(10 * BLK * 640 * D, 10 * 2**20, H * 640 * BLK),
        name="attend_back",
    )(info, own, other, ctx_own, ctx_other, grad)


def gelu_parts(x):
    cdf = 0.5 * (1.0 + lax.erf(x * 0.7071067811865476))
    slope = cdf + x * (jnp.exp(-0.5 * x * x) * 0.3989422804014327)
    return x * cdf, slope


def feed_kernel(
    ndp, nz, width, earlier, last, info, s_own, s_par, c_own, c_par, st_own, st_par, ct_own, ct_par,
    w_low, w_high, *rest
):
    rows = s_own.shape[0]
    tokens = 2 * rows
    block = D // ndp
    group = nz * width
    half = ndp // 2
    if earlier:
        m_in, g_in, *rest = rest
    if last:
        m_own, m_par, g_own, g_par, keep_out, send_out, *rest = rest
    else:
        m_out, g_out, keep_out, send_out, *rest = rest
    s, c, st, ct, w, act, gh, acc_m, acc_g, keep, send, sems, out_sems = rest
    at = [pl.multiple_of(info[p] * block, block) for p in range(ndp)]
    z = info[ndp]
    copies = {}
    count = [0]

    def start(name, src, dst):
        sem = sems.at[count[0]]
        count[0] += 1
        copy = pltpu.make_async_copy(src, dst, sem)
        copy.start()
        copies.setdefault(name, []).append(copy)

    def wait(name):
        for copy in copies.pop(name):
            copy.wait()

    def columns(name, own, par, dst):
        for p in range(ndp):
            for i, src in enumerate((own, par)):
                start(
                    name,
                    src.at[:, pl.ds(at[p], block)],
                    dst.at[i * rows : (i + 1) * rows, p * block : (p + 1) * block],
                )

    def rows_of(name, own, par, dst):
        for p in range(ndp):
            for i, src in enumerate((own, par)):
                start(
                    name,
                    src.at[pl.ds(at[p], block), :],
                    dst.at[p * block : (p + 1) * block, i * rows : (i + 1) * rows],
                )

    columns("s", s_own, s_par, s)
    for p in range(ndp):
        src = w_low if p < half else w_high
        start("w", src.at[p % half], w.at[p * block : (p + 1) * block, :])
    columns("c", c_own, c_par, c)
    rows_of("st", st_own, st_par, st)
    rows_of("ct", ct_own, ct_par, ct)
    if earlier:
        start("m", m_in, acc_m)
        start("g", g_in, acc_g)
    wait("s")
    wait("w")
    wait("c")

    @pl.loop(0, nz)
    def _(b):
        up = pl.ds(pl.multiple_of(b * width, width), width)
        down = pl.ds(pl.multiple_of(group + b * width, width), width)
        for i in range(2):
            part = slice(i * rows, (i + 1) * rows)
            hidden = jnp.dot(s[part, :], w[:, up], preferred_element_type=f32)
            grad = jnp.dot(c[part, :], w[:, down], preferred_element_type=f32)
            active, slope = gelu_parts(hidden)
            act[part, up] = active.astype(bf16)
            gh[part, up] = (grad * slope).astype(bf16)

    wait("st")
    wait("ct")

    @pl.loop(0, nz)
    def _(r):
        cols = pl.ds(pl.multiple_of((z ^ r) * width, width), width)
        for part, dst in ((0, keep), (1, send)):
            span = slice(part * half * block, (part + 1) * half * block)
            up = jnp.dot(st[span, :], gh[:, cols], preferred_element_type=f32).astype(bf16)
            down = jnp.dot(ct[span, :], act[:, cols], preferred_element_type=f32).astype(bf16)
            for p in range(half):
                dst[p, r, 0] = up[p * block : (p + 1) * block]
                dst[p, r, 1] = down[p * block : (p + 1) * block]

    outs = [
        pltpu.make_async_copy(keep, keep_out, out_sems.at[0]),
        pltpu.make_async_copy(send, send_out, out_sems.at[1]),
    ]
    for copy in outs:
        copy.start()
    if earlier:
        wait("m")
        wait("g")
    for name, left, acc, first in (("g", gh, acc_g, 0), ("m", act, acc_m, group)):
        for p in range(ndp):
            right = w[p * block : (p + 1) * block, first : first + group]
            for i in range(2):
                part = slice(i * rows, (i + 1) * rows)
                value = lax.dot_general(left[part, :], right, NT, preferred_element_type=f32)
                cols = pl.ds(at[p], block)
                if earlier:
                    value = value + acc[part, cols]
                if not last:
                    acc[part, cols] = value
                elif i == 0:
                    (g_own if name == "g" else m_own)[:, cols] = value
                else:
                    (g_par if name == "g" else m_par)[:, cols] = value.astype(bf16)
    if not last:
        outs.append(pltpu.make_async_copy(acc_m, m_out, out_sems.at[2]))
        outs.append(pltpu.make_async_copy(acc_g, g_out, out_sems.at[3]))
        for copy in outs[2:]:
            copy.start()
    for copy in outs:
        copy.wait()


def feed(links, info, acts, weights, earlier, last):
    ndp, nz = links.ndp, links.nz
    rows = acts[0].shape[0]
    tokens = 2 * rows
    block = D // ndp
    group = weights[0].shape[2] // 2
    width = group // nz
    half = ndp // 2
    full = jax.ShapeDtypeStruct((tokens, D), f32)
    own = jax.ShapeDtypeStruct((rows, D), f32)
    par = jax.ShapeDtypeStruct((rows, D), bf16)
    grads = jax.ShapeDtypeStruct((half, nz, 2, block, width), bf16)
    out_shape = (own, par, own, par, grads, grads) if last else (full, full, grads, grads)
    out_specs = (VMEM,) * 4 + (ANY,) * 2 if last else (ANY,) * 4
    inputs = (info, *acts, *weights) + (tuple(earlier) if earlier else ())
    n_copies = 8 * ndp + ndp + 2
    return pl.pallas_call(
        functools.partial(feed_kernel, ndp, nz, width, bool(earlier), last),
        out_shape=out_shape,
        in_specs=[SMEM] + [ANY] * (len(inputs) - 1),
        out_specs=out_specs,
        scratch_shapes=[
            pltpu.VMEM((tokens, D), bf16),
            pltpu.VMEM((tokens, D), bf16),
            pltpu.VMEM((D, tokens), bf16),
            pltpu.VMEM((D, tokens), bf16),
            pltpu.VMEM((D, 2 * group), bf16),
            pltpu.VMEM((tokens, group), bf16),
            pltpu.VMEM((tokens, group), bf16),
            pltpu.VMEM((tokens, D), f32),
            pltpu.VMEM((tokens, D), f32),
            pltpu.VMEM((half, nz, 2, block, width), bf16),
            pltpu.VMEM((half, nz, 2, block, width), bf16),
            pltpu.SemaphoreType.DMA((n_copies,)),
            pltpu.SemaphoreType.DMA((4,)),
        ],
        compiler_params=params(58),
        cost_estimate=cost(12 * tokens * D * group, 30 * 2**20, 2 * tokens * group),
        name="feed_last" if last else "feed_first",
    )(*inputs)


def place_kernel(ndp, half, block, info, low, high, out, sems):
    copies = []
    for p in range(ndp):
        src = low if p < half else high
        row = pl.multiple_of(info[p] * block, block)
        copies.append(
            pltpu.make_async_copy(src.at[p % half], out.at[pl.ds(row, block), :], sems.at[p])
        )
    for copy in copies:
        copy.start()
    for copy in copies:
        copy.wait()


def place(links, info, low, high):
    half, block, cols = low.shape
    ndp = links.ndp
    return pl.pallas_call(
        functools.partial(place_kernel, ndp, half, block),
        out_shape=jax.ShapeDtypeStruct((ndp * block, cols), low.dtype),
        in_specs=[SMEM, ANY, ANY],
        out_specs=ANY,
        scratch_shapes=[pltpu.SemaphoreType.DMA((ndp,))],
        cost_estimate=cost(0, 4 * ndp * block * cols),
        name="place",
    )(info, low, high)


def gather_z(links, values):
    current = values[None]
    for bit in reversed(range(1, links.mp_bits)):
        received = links.mp_swap(current, bit)
        mine = (links.mp >> bit) & 1
        current = jnp.where(
            mine == 0,
            jnp.stack([current, received], 1),
            jnp.stack([received, current], 1),
        )
        current = current.reshape(-1, *values.shape)
    return current.reshape(-1, values.shape[1])


def gather_dp(links, values):
    current = values[None]
    for level in reversed(range(links.dp_bits)):
        received = links.fan(current, level)
        if level == 0:
            return current, received
        current = jnp.concatenate([current, received], 0)


def add_b(left, right):
    return (left.astype(f32) + right.astype(f32)).astype(bf16)


def scatter_dp(links, keep, send):
    for level in range(links.dp_bits):
        received = links.fan(send, level)
        current = add_b(keep, received)
        half = current.shape[0] // 2
        if level < links.dp_bits - 1:
            keep, send = current[:half], current[half:]
    return current[0]


def scatter_z(links, values, relative):
    for bit in range(1, links.mp_bits):
        split = values.reshape(-1, 2, *values.shape[1:])
        if relative:
            keep, send = split[:, 0], split[:, 1]
        else:
            mine = (links.mp >> bit) & 1
            keep = jnp.where(mine == 0, split[:, 0], split[:, 1])
            send = jnp.where(mine == 0, split[:, 1], split[:, 0])
        received = links.mp_swap(send, bit)
        if bit == links.mp_bits - 1:
            return (keep.astype(f32) + received.astype(f32))[0]
        values = add_b(keep, received)


def gather_small(links, values):
    current = values[None]
    for bit in range(links.mp_bits):
        received = links.mp_swap(current, bit)
        current = jnp.where(
            (links.mp >> bit) & 1 == 0,
            jnp.concatenate([current, received], 0),
            jnp.concatenate([received, current], 0),
        )
    for bit in range(links.dp_bits):
        received = links.dp_swap(current, bit)
        current = jnp.where(
            (links.dp >> bit) & 1 == 0,
            jnp.concatenate([current, received], 0),
            jnp.concatenate([received, current], 0),
        )
    return current.reshape(links.ndp, links.nmp, -1)


def norm_parts(values):
    center = values - jnp.mean(values, axis=-1, keepdims=True)
    spread = jnp.mean(center * center, axis=-1, keepdims=True)
    inverse = lax.rsqrt(spread + 1e-05)
    return center * inverse, inverse


def norm_back(grad, unit, inverse, gain):
    scaled = grad * gain
    return (
        scaled
        - jnp.mean(scaled, axis=-1, keepdims=True)
        - unit * jnp.mean(scaled * unit, axis=-1, keepdims=True)
    ) * inverse


def dot(left, right):
    return jnp.dot(left, right, preferred_element_type=f32)


def dot_nt(left, right):
    return lax.dot_general(left, right, NT, preferred_element_type=f32)


def dot_tn(left, right):
    return lax.dot_general(left, right, TN, preferred_element_type=f32)


def body(
    tokens, cotangent, first_gain, second_gain, w_query, w_key, w_value, w_out, w_up, w_down,
    state_rate, state_in, state_out, state_bank, prev_link,
):
    links = Links()
    ndp, nmp, nz = links.ndp, links.nmp, links.nz
    rows = tokens.shape[0]
    per_window = LEN // BLK
    place_in = links.mp % per_window
    window = links.dp * (nmp // per_window) + links.mp // per_window
    link = lax.dynamic_index_in_dim(prev_link, window, keepdims=False)
    info = jnp.stack([links.block_at(p) for p in range(ndp)] + [links.z]).astype(jnp.int32)
    attend_info = jnp.stack([links.core, (place_in != 0).astype(jnp.int32)]).astype(jnp.int32)

    channels = state_rate.shape[0]
    maps_here = state_rate.shape[1]
    banks_here = state_bank.shape[0]
    pieces = [
        first_gain,
        second_gain,
        state_rate.T.reshape(-1),
        state_in.T.reshape(-1),
        state_out.T.reshape(-1),
        state_bank.transpose(0, 2, 1).reshape(-1),
    ]
    sizes = [piece.shape[0] for piece in pieces]
    packed = jnp.concatenate(pieces)
    packed = jnp.pad(packed, (0, -packed.shape[0] % 128)).reshape(-1, 128)
    small = gather_small(links, packed)
    starts = [sum(sizes[:i]) for i in range(len(sizes))]
    parts = [small[:, :, a : a + n] for a, n in zip(starts, sizes)]
    gain_one = lax.reduce_precision(parts[0].reshape(1, D), 8, 7)
    gain_two = lax.reduce_precision(parts[1].reshape(1, D), 8, 7)

    def full_map(values):
        values = values.reshape(ndp, nmp, maps_here, channels).transpose(0, 2, 1, 3)
        return values.reshape(NS, 8, 128)

    rate, gain_in, gain_out = (full_map(part) for part in parts[2:5])
    banks = parts[5].reshape(ndp, nmp, banks_here, NS, channels)
    bank = lax.dynamic_index_in_dim(banks, link // banks_here, 0, keepdims=False)
    bank = lax.dynamic_index_in_dim(bank, link % banks_here, 1, keepdims=False)
    initial = bank.transpose(1, 0, 2).reshape(NS, 8, 128)

    mats = jnp.stack([w_query, w_key, w_value, w_out], 1).astype(bf16)
    mats = mats.reshape(mats.shape[0], 4, 2, HALF)
    mats_keep = jnp.where(links.core == 0, mats[:, :, 0], mats[:, :, 1])
    mats_send = jnp.where(links.core == 0, mats[:, :, 1], mats[:, :, 0])
    mats_keep = mats_keep.reshape(-1, 4 * HALF)
    mats_send = mats_send.reshape(-1, 4 * HALF)
    mats_pair = by_core(links, mats_keep, links.core_swap(mats_send), 0)
    w_own = place(links, info, *gather_dp(links, gather_z(links, mats_pair)))
    w_other = links.core_swap(w_own)

    chunk = FF // nmp
    groups = 2 if chunk >= 256 else 1
    width = chunk // groups
    both = jnp.stack([w_up, w_down.T], 1).astype(bf16)
    both = both.reshape(both.shape[0], 2, nz, 2, groups, width)
    ff_keep = jnp.where(links.core == 0, both[:, :, :, 0], both[:, :, :, 1])
    ff_send = jnp.where(links.core == 0, both[:, :, :, 1], both[:, :, :, 0])

    def feed_group(values, g):
        return values[:, :, :, g].reshape(-1, 2 * nz * width)

    ff_pair = [
        by_core(links, feed_group(ff_keep, g), links.core_swap(feed_group(ff_send, g)), 0)
        for g in range(groups)
    ]
    ff_weights = [gather_dp(links, gather_z(links, pair)) for pair in ff_pair]

    token_f = tokens.astype(f32)
    unit_one, inverse_one = norm_parts(token_f)
    normed_b = (unit_one * gain_one).astype(bf16)
    tail = links.window_shift(normed_b[OWN:], 1)
    scan_own = state_scan(normed_b[:OWN], rate)
    scan_tail = state_scan(tail, rate)

    def decay_by(steps):
        return jnp.exp(-rate * steps)

    def forward(state, steps):
        far = decay_by(steps)
        near = decay_by(steps - 1.0) * steps
        return jnp.stack([far * state[0], far * state[1] + near * state[0]])

    total = forward(scan_tail, float(OWN)) + scan_own
    before = jnp.zeros_like(total)
    for bit in range(bits_of(per_window)):
        received = links.mp_swap(total, bit)
        mine = (links.mp >> bit) & 1
        inside = (place_in % (1 << bit)).astype(f32) * BLK
        before = before + jnp.where(mine == 1, forward(received, inside), 0.0)
        low = jnp.where(mine == 1, received, total)
        high = jnp.where(mine == 1, total, received)
        total = forward(low, float(BLK << bit)) + high
    decay = decay_by(1.0)
    tail_start = place_in.astype(f32) * BLK - CTX
    inside_window = (place_in != 0).astype(f32)
    carried = decay_by(tail_start) * initial * inside_window
    context = context_states(
        tail, gain_out * (gain_in * before[0] + carried), decay, gain_out * gain_in
    )

    qkv_own = dot(normed_b, w_own[:, : 3 * HALF]).astype(bf16)
    qkv_other = dot(normed_b, w_other[:, : 3 * HALF]).astype(bf16)
    ctx_own = dot(context, w_own[:, HALF : 3 * HALF]).astype(bf16)
    ctx_other = dot(context, w_other[:, HALF : 3 * HALF]).astype(bf16)
    attended = attend(attend_info, qkv_own, qkv_other, ctx_own, ctx_other)
    out_own = w_own[:, 3 * HALF :]
    out_other = w_other[:, 3 * HALF :]
    middle = token_f + by_core(links, dot(attended, out_own), dot(attended, out_other), 1)
    unit_two, inverse_two = norm_parts(middle)
    second_b = (unit_two * gain_two).astype(bf16)

    second_par = links.core_swap(second_b)
    cot_par = links.core_swap(cotangent)
    acts = (
        second_b, second_par, cotangent, cot_par, second_b.T, second_par.T, cotangent.T, cot_par.T,
    )
    scattered = []
    earlier = None
    for g in range(groups):
        last = g == groups - 1
        *sums, keep, send = feed(links, info, acts, ff_weights[g], earlier, last)
        earlier = sums
        scattered.append((keep, send))
    mix_own, mix_par, back_own, back_par = earlier
    mixed = (middle + (mix_own + links.core_swap(mix_par).astype(f32))).astype(bf16)
    grad_second = back_own + links.core_swap(back_par).astype(f32)
    ff_shares = [
        scatter_z(links, scatter_dp(links, keep, send), True) for keep, send in scattered
    ]
    grad_up = jnp.concatenate([share[0] for share in ff_shares], 1)
    grad_down = jnp.concatenate([share[1] for share in ff_shares], 1).T

    grad_gain_two = jnp.sum(grad_second * unit_two, axis=0)
    grad_middle = cotangent.astype(f32) + norm_back(grad_second, unit_two, inverse_two, gain_two)
    grad_branch = grad_middle.astype(bf16)
    branch_halves = grad_branch.reshape(rows, 2, HALF)
    branch_own = jnp.where(links.core == 0, branch_halves[:, 0], branch_halves[:, 1])
    branch_other = jnp.where(links.core == 0, branch_halves[:, 1], branch_halves[:, 0])
    grad_attended = (dot_nt(branch_own, out_own) + dot_nt(branch_other, out_other)).astype(bf16)
    g_own, g_other = attend_back(
        attend_info, qkv_own, qkv_other, ctx_own, ctx_other, grad_attended
    )
    grad_context = (
        dot_nt(g_own[:CTX, HALF:], w_own[:, HALF : 3 * HALF])
        + dot_nt(g_other[:CTX, HALF:], w_other[:, HALF : 3 * HALF])
    ).astype(bf16)

    sums = state_sums(grad_context, tail, before, decay)
    far = decay_by(tail_start)
    sum_init = far * decay * sums[2]
    sum_slope = far * ((tail_start + 1.0) * sums[2] + decay * sums[3])
    init_here = initial * inside_window
    grad_in = gain_out * sums[0]
    grad_out_map = gain_in * sums[0] + init_here * sum_init
    grad_rate = -decay * gain_out * (gain_in * sums[1] + init_here * sum_slope)
    grad_initial = gain_out * sum_init * inside_window

    total_back = sums[2]
    after = jnp.zeros_like(total_back)
    for bit in range(bits_of(per_window)):
        received = links.mp_swap(total_back, bit)
        mine = (links.mp >> bit) & 1
        inside = ((1 << bit) - 1 - place_in % (1 << bit)).astype(f32) * BLK
        after = after + jnp.where(mine == 0, decay_by(inside) * received, 0.0)
        low = jnp.where(mine == 1, received, total_back)
        high = jnp.where(mine == 1, total_back, received)
        total_back = low + decay_by(float(BLK << bit)) * high
    weight = gain_in * gain_out
    back_start = weight * after
    tail_sent = sent_tail(grad_context, decay_by(float(OWN)) * back_start, decay, weight)
    own_sent = sent_own(back_start, decay)
    last_sent = links.window_shift(tail_sent, -1)
    grad_sent = jnp.concatenate([own_sent, last_sent], 0)

    def by_owner(values):
        values = values.reshape(ndp, maps_here, nmp, channels).transpose(0, 2, 1, 3)
        return values.reshape(ndp, nmp, -1)

    chosen = jnp.arange(ndp * banks_here, dtype=jnp.int32) == link
    bank_share = grad_initial.reshape(NS, nmp, channels).transpose(1, 0, 2)[None]
    bank_share = jnp.where(chosen[:, None, None, None], bank_share, 0.0)
    bank_share = bank_share.reshape(ndp, banks_here, nmp, NS * channels).transpose(0, 2, 1, 3)
    shares = jnp.concatenate(
        [
            by_owner(grad_rate),
            by_owner(grad_in),
            by_owner(grad_out_map),
            bank_share.reshape(ndp, nmp, -1),
            grad_gain_two.reshape(ndp, nmp, -1),
        ],
        2,
    ).astype(bf16)
    share_len = shares.shape[2]
    line = 4 * HALF
    shares = jnp.pad(shares, ((0, 0), (0, 0), (0, -share_len % line)))
    shares = shares.reshape(ndp, nz, 2, -1, line)
    shares_keep = jnp.where(links.core == 0, shares[:, :, 0], shares[:, :, 1])
    shares_send = jnp.where(links.core == 0, shares[:, :, 1], shares[:, :, 0])
    shares = add_b(shares_keep, links.core_swap(shares_send))

    inputs_kv = jnp.concatenate([context, normed_b], 0)
    inputs_par = links.core_swap(inputs_kv)
    attended_par = links.core_swap(attended)
    g_par = links.core_swap(g_other)
    branch_par = links.core_swap(branch_other)
    grad_qkv = (dot_tn(inputs_kv, g_own) + dot_tn(inputs_par, g_par)).astype(bf16)
    grad_out = (dot_tn(attended, branch_own) + dot_tn(attended_par, branch_par)).astype(bf16)
    mat_rows = D // (ndp * nz)
    grad_mats = jnp.concatenate([grad_qkv, grad_out], 1).reshape(ndp, nz, mat_rows, line)
    grad_mats = jnp.concatenate([grad_mats, shares], 2)

    def blocks(first, count):
        return jnp.concatenate(
            [
                lax.dynamic_slice_in_dim(grad_mats, links.block_at(first + p), 1, 0)
                for p in range(count)
            ],
            0,
        )

    half = ndp // 2
    mats_share = scatter_z(
        links, scatter_dp(links, blocks(0, half), blocks(half, half)), False
    )
    flat = mats_share[mat_rows:].reshape(-1)[:share_len]
    map_size = maps_here * channels
    grad_maps = [
        flat[i * map_size : (i + 1) * map_size].reshape(maps_here, channels).T for i in range(3)
    ]
    bank_end = share_len - D // (ndp * nmp)
    grad_bank = flat[3 * map_size : bank_end].reshape(banks_here, NS, channels)
    grad_bank = grad_bank.transpose(0, 2, 1)
    share_two = flat[bank_end:]
    mine_rows = mats_share[:mat_rows].reshape(2, mat_rows // 2, 4, HALF)
    rows_keep = jnp.where(links.core == 0, mine_rows[0], mine_rows[1])
    rows_send = jnp.where(links.core == 0, mine_rows[1], mine_rows[0])
    grad_rows = by_core(links, rows_keep, links.core_swap(rows_send), 2)

    grad_normed = (
        dot_nt(g_own[CTX:], w_own[:, : 3 * HALF])
        + dot_nt(g_other[CTX:], w_other[:, : 3 * HALF])
        + grad_sent.astype(f32)
    )
    grad_gain_one = jnp.sum(grad_normed * unit_one, axis=0)
    grad_tokens = (grad_middle + norm_back(grad_normed, unit_one, inverse_one, gain_one)).astype(bf16)
    gain_parts = lax.all_to_all(
        grad_gain_one.reshape(ndp * nmp, -1), AXES, split_axis=0, concat_axis=0, tiled=True
    )
    share_one = jnp.sum(gain_parts, axis=0)
    return (
        mixed, grad_tokens, share_one, share_two,
        grad_rows[:, 0], grad_rows[:, 1], grad_rows[:, 2], grad_rows[:, 3],
        grad_up, grad_down, grad_maps[0], grad_maps[1], grad_maps[2], grad_bank,
    )


def solution(mesh):
    split = P(AXES, None)
    gain = P(AXES)
    maps = P("mp", "dp")
    bank = P("dp", "mp", None)
    return jax.shard_map(
        body,
        mesh=mesh,
        in_specs=(
            split, split, gain, gain, split, split, split, split, split, P(None, AXES),
            maps, maps, maps, bank, P(),
        ),
        out_specs=(
            split, split, gain, gain, split, split, split, split, P("dp", "mp"), P("mp", "dp"),
            maps, maps, maps, bank,
        ),
        check_vma=False,
    )
```

```python
import functools

import jax
import jax.numpy as jnp
from jax import lax
from jax.experimental import pallas as pl
from jax.experimental.pallas import tpu as pltpu
from jax.sharding import PartitionSpec as P

D = 1024
H = 8
HD = 128
FF = 4096
NS = 16
LEN = 4096
BLK = 512
CTX = 128
OWN = BLK - CTX
HALF = D // 2
SCALE = HD ** (-0.5)
AXES = ("dp", "mp")
f32 = jnp.float32
bf16 = jnp.bfloat16
VMEM = pl.BlockSpec(memory_space=pltpu.VMEM)
SMEM = pl.BlockSpec(memory_space=pltpu.SMEM)
ANY = pl.BlockSpec(memory_space=pl.ANY)
QKV_COLS = pl.BlockSpec((D, 3 * HALF), lambda i: (0, 0))
OUT_COLS = pl.BlockSpec((D, HALF), lambda i: (0, 3))
NT = (((1,), (1,)), ((), ()))
TN = (((0,), (0,)), ((), ()))


def params(mib):
    return pltpu.CompilerParams(vmem_limit_bytes=mib * 1024 * 1024)


COST = pl.CostEstimate(flops=1, bytes_accessed=1, transcendentals=0)


def bits_of(n):
    return n.bit_length() - 1


def swap_bits(word, count):
    out = 0
    for i in range(count):
        out = out | (((word >> i) & 1) << (count - 1 - i))
    return out


class Links:
    def __init__(self):
        self.ndp = lax.axis_size("dp")
        self.nmp = lax.axis_size("mp")
        self.nz = self.nmp // 2
        self.dp = lax.axis_index("dp")
        self.mp = lax.axis_index("mp")
        self.z = self.mp // 2
        self.core = self.mp % 2
        self.dp_bits = bits_of(self.ndp)
        self.mp_bits = bits_of(self.nmp)

    def send(self, values, target):
        pairs = []
        for d in range(self.ndp):
            for m in range(self.nmp):
                to = target(d, m)
                if to is not None:
                    pairs.append((d * self.nmp + m, to[0] * self.nmp + to[1]))
        return lax.ppermute(values, AXES, pairs)

    def mp_swap(self, values, bit):
        return self.send(values, lambda d, m: (d, m ^ (1 << bit)))

    def dp_swap(self, values, bit):
        return self.send(values, lambda d, m: (d ^ (1 << bit), m))

    def core_swap(self, values):
        return self.mp_swap(values, 0)

    def fan(self, values, level):
        other = self.dp_bits - 1 - level
        return self.send(
            values, lambda d, m: (d ^ (1 << (other if m % 2 else level)), m)
        )

    def block_at(self, position):
        mirrored = swap_bits(position, self.dp_bits)
        return self.dp ^ jnp.where(self.core == 0, mirrored, position)

    def window_shift(self, values, step):
        per = LEN // BLK

        def target(d, m):
            inside = m % per + step
            return (d, m + step) if 0 <= inside < per else None

        return self.send(values, target)


def by_core(links, first, second, axis):
    return jnp.where(
        links.core == 0,
        jnp.concatenate([first, second], axis),
        jnp.concatenate([second, first], axis),
    )


def spread_rows(src_ref, dst_ref, rows, start=0):
    for r in range(0, rows, 16):
        block = src_ref[start + r : start + r + 16, :].astype(f32)
        for j in range(8):
            dst_ref[r : r + 16, j, :] = block[:, j * 128 : (j + 1) * 128]


def gather_rows(src_ref, dst_ref, rows):
    for r in range(0, rows, 16):
        for j in range(8):
            dst_ref[r : r + 16, j * 128 : (j + 1) * 128] = src_ref[r : r + 16, j, :].astype(
                dst_ref.dtype
            )


def move_on(state, rate, steps):
    far = jnp.exp(-rate * steps)
    near = jnp.exp(-rate * (steps - 1.0)) * steps
    return far * state[0], far * state[1] + near * state[0]


def scan_rows(xs, rows, decay):
    zero = jnp.zeros((NS, 8, 128), f32)

    def step(i, carry):
        u, v = carry
        for k in range(8):
            v = decay * v + u
            u = decay * u + xs[i * 8 + k][None]
        return u, v

    return lax.fori_loop(0, rows // 8, step, (zero, zero))


def scan_own_kernel(x_ref, rate_ref, out_ref, xs):
    spread_rows(x_ref, xs, OWN)
    u, v = scan_rows(xs, OWN, jnp.exp(-rate_ref[...]))
    out_ref[0] = u
    out_ref[1] = v


def scan_tail_kernel(x_ref, own_ref, rate_ref, out_ref, xs):
    spread_rows(x_ref, xs, CTX)
    state = scan_rows(xs, CTX, jnp.exp(-rate_ref[...]))
    u, v = move_on(state, rate_ref[...], float(OWN))
    out_ref[0] = u + own_ref[0]
    out_ref[1] = v + own_ref[1]


STATE = jax.ShapeDtypeStruct((2, NS, 8, 128), f32)


def scan_own(values, rate):
    return pl.pallas_call(
        scan_own_kernel,
        out_shape=STATE,
        in_specs=[VMEM, VMEM],
        out_specs=VMEM,
        scratch_shapes=[pltpu.VMEM((OWN, 8, 128), f32)],
        compiler_params=params(24),
        cost_estimate=COST,
        name="scan_own",
    )(values, rate)


def scan_tail(values, own, rate):
    return pl.pallas_call(
        scan_tail_kernel,
        out_shape=STATE,
        in_specs=[VMEM] * 3,
        out_specs=VMEM,
        scratch_shapes=[pltpu.VMEM((CTX, 8, 128), f32)],
        compiler_params=params(24),
        cost_estimate=COST,
        name="scan_tail",
    )(values, own, rate)


def exchange_kernel(scal, total_ref, recv_ref, before_ref, rate_ref, total_out, before_out):
    mine, inside, span = scal[0], scal[1], scal[2]
    rate = rate_ref[...]
    recv = (recv_ref[0], recv_ref[1])
    total = (total_ref[0], total_ref[1])
    moved = move_on(recv, rate, inside)
    low = tuple(mine * r + (1.0 - mine) * t for r, t in zip(recv, total))
    high = tuple(mine * t + (1.0 - mine) * r for r, t in zip(recv, total))
    far = move_on(low, rate, span)
    for i in range(2):
        before_out[i] = before_ref[i] + mine * moved[i]
        total_out[i] = far[i] + high[i]


def exchange_step(scal, total, received, before, rate):
    return pl.pallas_call(
        exchange_kernel,
        out_shape=(STATE, STATE),
        in_specs=[SMEM] + [VMEM] * 4,
        out_specs=(VMEM, VMEM),
        compiler_params=params(16),
        cost_estimate=COST,
        name="exchange_step",
    )(scal, total, received, before, rate)


def exchange_back_kernel(scal, total_ref, recv_ref, after_ref, rate_ref, total_out, after_out):
    mine, inside, span = scal[0], scal[1], scal[2]
    rate = rate_ref[...]
    recv, total = recv_ref[...], total_ref[...]
    after_out[...] = after_ref[...] + (1.0 - mine) * (jnp.exp(-rate * inside) * recv)
    low = mine * recv + (1.0 - mine) * total
    high = mine * total + (1.0 - mine) * recv
    total_out[...] = low + jnp.exp(-rate * span) * high


def exchange_back_step(scal, total, received, after, rate):
    one = jax.ShapeDtypeStruct((NS, 8, 128), f32)
    return pl.pallas_call(
        exchange_back_kernel,
        out_shape=(one, one),
        in_specs=[SMEM] + [VMEM] * 4,
        out_specs=(VMEM, VMEM),
        compiler_params=params(16),
        cost_estimate=COST,
        name="exchange_back_step",
    )(scal, total, received, after, rate)


def context_kernel(
    scal, x_ref, own_ref, before_ref, initial_ref, rate_ref, in_ref, out_map_ref, out_ref, xs, ys
):
    out_ref[CTX:, :] = own_ref[...]
    spread_rows(x_ref, xs, CTX)
    rate = rate_ref[...]
    decay = jnp.exp(-rate)
    weight = in_ref[...] * out_map_ref[...]
    carried = jnp.exp(-rate * scal[0]) * initial_ref[...] * scal[1]
    start = out_map_ref[...] * (in_ref[...] * before_ref[0] + carried)

    def step(i, y):
        for k in range(8):
            y = decay * y + weight * xs[i * 8 + k][None]
            ys[i * 8 + k] = jnp.sum(y, axis=0)
        return y

    lax.fori_loop(0, CTX // 8, step, start)
    gather_rows(ys, out_ref, CTX)


def context_states(scal, tail, own, before, initial, rate, gain_in, gain_out):
    return pl.pallas_call(
        context_kernel,
        out_shape=jax.ShapeDtypeStruct((CTX + BLK, D), bf16),
        in_specs=[SMEM] + [VMEM] * 7,
        out_specs=VMEM,
        scratch_shapes=[pltpu.VMEM((CTX, 8, 128), f32)] * 2,
        compiler_params=params(24),
        cost_estimate=COST,
        name="context_states",
    )(scal, tail, own, before, initial, rate, gain_in, gain_out)


def state_low_kernel(g_ref, rate_ref, out_ref, gs):
    spread_rows(g_ref, gs, CTX)
    decay = jnp.exp(-rate_ref[...])
    zero = jnp.zeros((NS, 8, 128), f32)

    def back(i, carry):
        low, slope = carry
        for k in range(8):
            slope = decay * slope + low
            low = decay * low + gs[CTX - 1 - (i * 8 + k)][None]
        return low, slope

    low, slope = lax.fori_loop(0, CTX // 8, back, (zero, zero))
    out_ref[0] = low
    out_ref[1] = slope


def state_low(grad_context, rate):
    return pl.pallas_call(
        state_low_kernel,
        out_shape=jax.ShapeDtypeStruct((2, NS, 8, 128), f32),
        in_specs=[VMEM] * 2,
        out_specs=VMEM,
        scratch_shapes=[pltpu.VMEM((CTX, 8, 128), f32)],
        compiler_params=params(16),
        cost_estimate=COST,
        name="state_low",
    )(grad_context, rate)


def state_sums_kernel(
    scal, g_ref, x_ref, start_ref, lows_ref, initial_ref, rate_ref, in_ref, out_map_ref, out_ref,
    gs, xs,
):
    spread_rows(g_ref, gs, CTX)
    spread_rows(x_ref, xs, CTX)
    part = NS // 2
    for n in range(0, NS, part):
        span = slice(n, n + part)
        rate = rate_ref[span]
        decay = jnp.exp(-rate)
        zero = jnp.zeros((part, 8, 128), f32)

        def step(i, carry):
            u, v, su, sv = carry
            for k in range(4):
                v = decay * v + u
                u = decay * u + xs[i * 4 + k][None]
                g = gs[i * 4 + k][None]
                su = su + g * u
                sv = sv + g * v
            return u, v, su, sv

        _, _, su, sv = lax.fori_loop(
            0, CTX // 4, step, (start_ref[0, span], start_ref[1, span], zero, zero)
        )
        far = jnp.exp(-rate * scal[0])
        low, slope = lows_ref[0, span], lows_ref[1, span]
        sum_init = far * decay * low
        sum_slope = far * ((scal[0] + 1.0) * low + decay * slope)
        initial = initial_ref[span] * scal[1]
        gain_in, gain_out = in_ref[span], out_map_ref[span]
        out_ref[0, span] = -decay * gain_out * (gain_in * sv + initial * sum_slope)
        out_ref[1, span] = gain_out * su
        out_ref[2, span] = gain_in * su + initial * sum_init
        out_ref[3, span] = gain_out * sum_init * scal[1]


def state_sums(scal, grad_context, tail, start, lows, initial, rate, gain_in, gain_out):
    return pl.pallas_call(
        state_sums_kernel,
        out_shape=jax.ShapeDtypeStruct((4, NS, 8, 128), f32),
        in_specs=[SMEM] + [VMEM] * 8,
        out_specs=VMEM,
        scratch_shapes=[pltpu.VMEM((CTX, 8, 128), f32)] * 2,
        compiler_params=params(24),
        cost_estimate=COST,
        name="state_sums",
    )(scal, grad_context, tail, start, lows, initial, rate, gain_in, gain_out)


def sent_tail_kernel(g_ref, after_ref, rate_ref, in_ref, out_map_ref, out_ref, gs, ys):
    spread_rows(g_ref, gs, CTX)
    rate = rate_ref[...]
    decay = jnp.exp(-rate)
    weight = in_ref[...] * out_map_ref[...]
    start = jnp.exp(-rate * float(OWN)) * weight * after_ref[...]

    def back(i, y):
        for k in range(8):
            t = CTX - 1 - (i * 8 + k)
            y = decay * y + weight * gs[t][None]
            ys[t] = jnp.sum(y, axis=0)
        return y

    lax.fori_loop(0, CTX // 8, back, start)
    gather_rows(ys, out_ref, CTX)


def sent_tail(grad_context, after, rate, gain_in, gain_out):
    return pl.pallas_call(
        sent_tail_kernel,
        out_shape=jax.ShapeDtypeStruct((CTX, D), bf16),
        in_specs=[VMEM] * 5,
        out_specs=VMEM,
        scratch_shapes=[pltpu.VMEM((CTX, 8, 128), f32)] * 2,
        compiler_params=params(24),
        cost_estimate=COST,
        name="sent_tail",
    )(grad_context, after, rate, gain_in, gain_out)


def sent_own_kernel(after_ref, rate_ref, in_ref, out_map_ref, out_ref, ys):
    decay = jnp.exp(-rate_ref[...])

    def back(i, y):
        for k in range(8):
            y = decay * y
            ys[OWN - 1 - (i * 8 + k)] = jnp.sum(y, axis=0)
        return y

    lax.fori_loop(0, OWN // 8, back, in_ref[...] * out_map_ref[...] * after_ref[...])
    gather_rows(ys, out_ref, OWN)


def sent_own(after, rate, gain_in, gain_out):
    return pl.pallas_call(
        sent_own_kernel,
        out_shape=jax.ShapeDtypeStruct((OWN, D), bf16),
        in_specs=[VMEM] * 4,
        out_specs=VMEM,
        scratch_shapes=[pltpu.VMEM((OWN, 8, 128), f32)],
        compiler_params=params(24),
        cost_estimate=COST,
        name="sent_own",
    )(after, rate, gain_in, gain_out)


def attention_mask(keys, queries, first_query, opened):
    row = lax.broadcasted_iota(jnp.int32, (keys, queries), 0)
    col = lax.broadcasted_iota(jnp.int32, (keys, queries), 1) + first_query
    return jnp.where(row < CTX, (1 - opened) * BLK, row - CTX) <= col


def head_parts(ref, offset):
    q = ref[CTX:, pl.ds(offset, HD)]
    k = ref[:, pl.ds(HALF + offset, HD)]
    v = ref[:, pl.ds(2 * HALF + offset, HD)]
    return q, k, v


def probabilities(k, q, first_query, opened):
    scores = lax.dot_general(k, q, NT, preferred_element_type=f32) * SCALE
    scores = jnp.where(
        attention_mask(k.shape[0], q.shape[0], first_query, opened), scores, -jnp.inf
    )
    lifted = jnp.exp(scores - jnp.max(scores, axis=0, keepdims=True))
    return lifted * (1.0 / jnp.sum(lifted, axis=0, keepdims=True))


QT = BLK // 2


def attend_kernel(info, own_ref, other_ref, out_ref):
    opened = info[1]

    @pl.loop(0, H // 2)
    def _(h):
        offset = pl.multiple_of(h * HD, HD)
        for side, qkv in enumerate((own_ref, other_ref)):
            q, k, v = head_parts(qkv, offset)
            v_t = v.T
            home = pl.multiple_of((side ^ info[0]) * HALF + h * HD, HD)
            for first in range(0, BLK, QT):
                keys = CTX + first + QT
                p = probabilities(k[:keys], q[first : first + QT], first, opened).astype(bf16)
                mixed = jnp.dot(v_t[:, :keys], p, preferred_element_type=f32)
                out_ref[first : first + QT, pl.ds(home, HD)] = mixed.T.astype(bf16)


def attend(info, own, other):
    return pl.pallas_call(
        attend_kernel,
        out_shape=jax.ShapeDtypeStruct((BLK, D), bf16),
        in_specs=[SMEM] + [VMEM] * 2,
        out_specs=VMEM,
        compiler_params=params(32),
        cost_estimate=COST,
        name="attend",
    )(info, own, other)


def attend_back_kernel(
    info, own_ref, other_ref, grad_ref, g_own_ref, g_other_ref, acc
):
    opened = info[1]
    sides = ((own_ref, g_own_ref), (other_ref, g_other_ref))
    for _, g in sides:
        g[:CTX, :HALF] = jnp.zeros((CTX, HALF), bf16)

    @pl.loop(0, H // 2)
    def _(h):
        offset = pl.multiple_of(h * HD, HD)
        for side, (qkv, g) in enumerate(sides):
            q, k, v = head_parts(qkv, offset)
            k_t = k.T
            home = pl.multiple_of((side ^ info[0]) * HALF + h * HD, HD)
            for first in range(0, BLK, QT):
                keys = CTX + first + QT
                q_now = q[first : first + QT]
                go = grad_ref[first : first + QT, pl.ds(home, HD)]
                p = probabilities(k[:keys], q_now, first, opened)
                gp = lax.dot_general(v[:keys], go, NT, preferred_element_type=f32)
                mean = jnp.sum(p * gp, axis=0, keepdims=True)
                gs = (p * (gp - mean)).astype(bf16)
                gq_t = jnp.dot(k_t[:, :keys], gs, preferred_element_type=f32) * SCALE
                g[CTX + first : CTX + first + QT, pl.ds(offset, HD)] = gq_t.T.astype(bf16)
                gk = jnp.dot(gs, q_now, preferred_element_type=f32)
                gv = jnp.dot(p.astype(bf16), go, preferred_element_type=f32)
                if first == 0:
                    acc[0, :keys] = gk
                    acc[1, :keys] = gv
                else:
                    early = CTX + QT
                    gk_all = jnp.concatenate([gk[:early] + acc[0, :early], gk[early:]], 0)
                    gv_all = jnp.concatenate([gv[:early] + acc[1, :early], gv[early:]], 0)
                    g[:, pl.ds(HALF + offset, HD)] = (gk_all * SCALE).astype(bf16)
                    g[:, pl.ds(2 * HALF + offset, HD)] = gv_all.astype(bf16)


def attend_back(info, own, other, grad):
    out = jax.ShapeDtypeStruct((CTX + BLK, 3 * HALF), bf16)
    return pl.pallas_call(
        attend_back_kernel,
        out_shape=(out, out),
        in_specs=[SMEM] + [VMEM] * 3,
        out_specs=(VMEM, VMEM),
        scratch_shapes=[pltpu.VMEM((2, CTX + QT, HD), f32)],
        compiler_params=params(32),
        cost_estimate=COST,
        name="attend_back",
    )(info, own, other, grad)


def gelu_parts(x):
    cdf = 0.5 * (1.0 + lax.erf(x * 0.7071067811865476))
    slope = cdf + x * (jnp.exp(-0.5 * x * x) * 0.3989422804014327)
    return x * cdf, slope


def feed_kernel(
    ndp, nz, width, index, groups, earlier, last, info, s_own, s_par, c_own, c_par, st_own, st_par, ct_own, ct_par,
    *rest
):
    rows = s_own.shape[0]
    tokens = 2 * rows
    block = D // ndp
    group = nz * width
    half = ndp // 2
    weights, *rest = rest
    if earlier:
        m_in, g_in, *rest = rest
    if last:
        m_own, m_par, g_own, g_par, keep_out, send_out, *rest = rest
    else:
        m_out, g_out, keep_out, send_out, *rest = rest
    s, c, st, ct, w, act, gh, acc_m, acc_g, keep, send, sems, out_sems = rest
    at = [pl.multiple_of(info[p] * block, block) for p in range(ndp)]
    z = info[ndp]
    copies = {}
    count = [0]

    def start(name, src, dst):
        sem = sems.at[count[0]]
        count[0] += 1
        copy = pltpu.make_async_copy(src, dst, sem)
        copy.start()
        copies.setdefault(name, []).append(copy)

    def wait(name):
        for copy in copies.pop(name):
            copy.wait()

    def rows_of(name, own, par, dst):
        for p in range(ndp):
            for i, src in enumerate((own, par)):
                start(
                    name,
                    src.at[pl.ds(at[p], block), :],
                    dst.at[p * block : (p + 1) * block, i * rows : (i + 1) * rows],
                )

    for i, src in enumerate((s_own, s_par)):
        start("s", src, s.at[i * rows : (i + 1) * rows, :])
    at_core = pl.multiple_of((info[ndp + 1] * groups + index) * 2 * group, 128)
    start("w", weights.at[:, pl.ds(at_core, 2 * group)], w)
    for i, src in enumerate((c_own, c_par)):
        start("c", src, c.at[i * rows : (i + 1) * rows, :])
    rows_of("st", st_own, st_par, st)
    rows_of("ct", ct_own, ct_par, ct)
    if earlier:
        start("m", m_in, acc_m)
        start("g", g_in, acc_g)
    wait("s")
    wait("w")
    wait("c")

    @pl.loop(0, nz)
    def _(b):
        up = pl.ds(pl.multiple_of(b * width, width), width)
        down = pl.ds(pl.multiple_of(group + b * width, width), width)
        for i in range(2):
            part = slice(i * rows, (i + 1) * rows)
            hidden = jnp.dot(s[part, :], w[:, up], preferred_element_type=f32)
            grad = jnp.dot(c[part, :], w[:, down], preferred_element_type=f32)
            active, slope = gelu_parts(hidden)
            act[part, up] = active.astype(bf16)
            gh[part, up] = (grad * slope).astype(bf16)

    wait("st")
    wait("ct")

    @pl.loop(0, nz)
    def _(r):
        cols = pl.ds(pl.multiple_of((z ^ swap_bits(r, bits_of(nz))) * width, width), width)
        for part, dst in ((0, keep), (1, send)):
            span = slice(part * half * block, (part + 1) * half * block)
            up = jnp.dot(st[span, :], gh[:, cols], preferred_element_type=f32).astype(bf16)
            down = jnp.dot(ct[span, :], act[:, cols], preferred_element_type=f32).astype(bf16)
            for p in range(half):
                dst[p, r, 0] = up[p * block : (p + 1) * block]
                dst[p, r, 1] = down[p * block : (p + 1) * block]

    outs = [
        pltpu.make_async_copy(keep, keep_out, out_sems.at[0]),
        pltpu.make_async_copy(send, send_out, out_sems.at[1]),
    ]
    for copy in outs:
        copy.start()
    if earlier:
        wait("m")
        wait("g")
    for name, left, acc, first in (("g", gh, acc_g, 0), ("m", act, acc_m, group)):
        for p in range(ndp):
            right = w[p * block : (p + 1) * block, first : first + group]
            for i in range(2):
                part = slice(i * rows, (i + 1) * rows)
                value = lax.dot_general(left[part, :], right, NT, preferred_element_type=f32)
                cols = slice(p * block, (p + 1) * block)
                if earlier:
                    value = value + acc[part, cols]
                if not last:
                    acc[part, cols] = value
                elif i == 0:
                    (g_own if name == "g" else m_own)[:, cols] = value
                else:
                    (g_par if name == "g" else m_par)[:, cols] = value.astype(bf16)
    if not last:
        outs.append(pltpu.make_async_copy(acc_m, m_out, out_sems.at[2]))
        outs.append(pltpu.make_async_copy(acc_g, g_out, out_sems.at[3]))
        for copy in outs[2:]:
            copy.start()
    for copy in outs:
        copy.wait()


def feed(links, info, acts, weights, group, index, groups, earlier, last):
    ndp, nz = links.ndp, links.nz
    rows = acts[0].shape[0]
    tokens = 2 * rows
    block = D // ndp
    width = group // nz
    half = ndp // 2
    full = jax.ShapeDtypeStruct((tokens, D), f32)
    own = jax.ShapeDtypeStruct((rows, D), f32)
    par = jax.ShapeDtypeStruct((rows, D), bf16)
    grads = jax.ShapeDtypeStruct((half, nz, 2, block, width), bf16)
    out_shape = (own, par, own, par, grads, grads) if last else (full, full, grads, grads)
    out_specs = (VMEM,) * 4 + (ANY,) * 2 if last else (ANY,) * 4
    inputs = (info, *acts, weights) + (tuple(earlier) if earlier else ())
    n_copies = 4 * ndp + 7
    return pl.pallas_call(
        functools.partial(feed_kernel, ndp, nz, width, index, groups, bool(earlier), last),
        out_shape=out_shape,
        in_specs=[SMEM] + [ANY] * (len(inputs) - 1),
        out_specs=out_specs,
        scratch_shapes=[
            pltpu.VMEM((tokens, D), bf16),
            pltpu.VMEM((tokens, D), bf16),
            pltpu.VMEM((D, tokens), bf16),
            pltpu.VMEM((D, tokens), bf16),
            pltpu.VMEM((D, 2 * group), bf16),
            pltpu.VMEM((tokens, group), bf16),
            pltpu.VMEM((tokens, group), bf16),
            pltpu.VMEM((tokens, D), f32),
            pltpu.VMEM((tokens, D), f32),
            pltpu.VMEM((half, nz, 2, block, width), bf16),
            pltpu.VMEM((half, nz, 2, block, width), bf16),
            pltpu.SemaphoreType.DMA((n_copies,)),
            pltpu.SemaphoreType.DMA((4,)),
        ],
        compiler_params=params(58),
        cost_estimate=COST,
        name="feed_last" if last else "feed_first",
    )(*inputs)


def norm_parts(values):
    center = values - jnp.mean(values, axis=-1, keepdims=True)
    spread = jnp.mean(center * center, axis=-1, keepdims=True)
    inverse = lax.rsqrt(spread + 1e-05)
    return center * inverse, inverse


def norm_back(grad, unit, inverse, gain):
    scaled = grad * gain
    return (
        scaled
        - jnp.mean(scaled, axis=-1, keepdims=True)
        - unit * jnp.mean(scaled * unit, axis=-1, keepdims=True)
    ) * inverse


def dot(left, right):
    return jnp.dot(left, right, preferred_element_type=f32)


def dot_nt(left, right):
    return lax.dot_general(left, right, NT, preferred_element_type=f32)


ROWS = 128


def norm_kernel(x_ref, gain_ref, out_ref, tail_ref):
    for r in range(0, x_ref.shape[0], ROWS):
        unit, _ = norm_parts(x_ref[r : r + ROWS, :].astype(f32))
        out_ref[r : r + ROWS, :] = (unit * gain_ref[...]).astype(bf16)
    tail_ref[...] = out_ref[OWN:, :]


def norm_first(tokens, gain):
    return pl.pallas_call(
        norm_kernel,
        out_shape=(
            jax.ShapeDtypeStruct(tokens.shape, bf16),
            jax.ShapeDtypeStruct((CTX, D), bf16),
        ),
        in_specs=[VMEM] * 2,
        out_specs=(VMEM, VMEM),
        compiler_params=params(16),
        cost_estimate=COST,
        name="norm_first",
    )(tokens, gain)


def middle_kernel(
    info, att_ref, tok_ref, o_own, o_other, gain_ref, mid_ref, second_ref, second_t_ref
):
    att = att_ref[...]
    for side, weight in enumerate((o_own, o_other)):
        cols = pl.ds(pl.multiple_of((side ^ info[0]) * HALF, HALF), HALF)
        mid_ref[:, cols] = tok_ref[:, cols].astype(f32) + dot(att, weight[...])
    for r in range(0, att_ref.shape[0], ROWS):
        unit, _ = norm_parts(mid_ref[r : r + ROWS, :])
        second = unit * gain_ref[...]
        second_ref[r : r + ROWS, :] = second.astype(bf16)
        second_t_ref[:, r : r + ROWS] = second.T.astype(bf16)


def middle_norm(info, attended, tokens, o_own, o_other, gain):
    rows = tokens.shape[0]
    return pl.pallas_call(
        middle_kernel,
        out_shape=(
            jax.ShapeDtypeStruct((rows, D), f32),
            jax.ShapeDtypeStruct((rows, D), bf16),
            jax.ShapeDtypeStruct((D, rows), bf16),
        ),
        grid=(1,),
        in_specs=[SMEM, VMEM, VMEM, OUT_COLS, OUT_COLS, VMEM],
        out_specs=(VMEM,) * 3,
        compiler_params=params(32),
        cost_estimate=COST,
        name="middle_norm",
    )(info, attended, tokens, o_own, o_other, gain)


def back_middle_kernel(
    info, mid_ref, own_ref, recv_ref, cot_ref, gain_ref, o_own, o_other,
    grad_ref, b_own_ref, b_other_ref, att_ref, gain_grad_ref, branch,
):
    total = jnp.zeros((1, D), f32)
    for r in range(0, mid_ref.shape[0], ROWS):
        span = slice(r, r + ROWS)
        unit, inverse = norm_parts(mid_ref[span, :])
        grad = own_ref[span, :] + recv_ref[span, :].astype(f32)
        total = total + jnp.sum(grad * unit, axis=0, keepdims=True)
        back = cot_ref[span, :].astype(f32) + norm_back(grad, unit, inverse, gain_ref[...])
        grad_ref[span, :] = back
        branch[span, :] = back.astype(bf16)
    gain_grad_ref[...] = total
    for side, out in enumerate((b_own_ref, b_other_ref)):
        out[...] = branch[:, pl.ds(pl.multiple_of((side ^ info[0]) * HALF, HALF), HALF)]
    att = dot_nt(b_own_ref[...], o_own[...]) + dot_nt(b_other_ref[...], o_other[...])
    att_ref[...] = att.astype(bf16)


def back_middle(info, middle, own, received, cotangent, gain, o_own, o_other):
    rows = middle.shape[0]
    part = jax.ShapeDtypeStruct((rows, HALF), bf16)
    return pl.pallas_call(
        back_middle_kernel,
        out_shape=(
            jax.ShapeDtypeStruct((rows, D), f32),
            part,
            part,
            jax.ShapeDtypeStruct((rows, D), bf16),
            jax.ShapeDtypeStruct((1, D), f32),
        ),
        grid=(1,),
        in_specs=[SMEM] + [VMEM] * 5 + [OUT_COLS] * 2,
        out_specs=(VMEM,) * 5,
        scratch_shapes=[pltpu.VMEM((rows, D), bf16)],
        compiler_params=params(40),
        cost_estimate=COST,
        name="back_middle",
    )(info, middle, own, received, cotangent, gain, o_own, o_other)


def project_kernel(x_ref, w_ref, out_ref):
    for first in range(0, 3 * HALF, HALF):
        cols = slice(first, first + HALF)
        out_ref[:, cols] = dot(x_ref[...], w_ref[:, cols]).astype(bf16)


def project(values, weights):
    return pl.pallas_call(
        project_kernel,
        out_shape=jax.ShapeDtypeStruct((values.shape[0], 3 * HALF), bf16),
        grid=(1,),
        in_specs=[VMEM, QKV_COLS],
        out_specs=VMEM,
        compiler_params=params(32),
        cost_estimate=COST,
        name="project",
    )(values, weights)


def back_project_kernel(first, g_own, g_other, w_own, w_other, out_ref):
    rows = slice(first, first + out_ref.shape[0])
    for at in range(0, D, HALF):
        cols = slice(at, at + HALF)
        value = dot_nt(g_own[rows, :], w_own[cols, :]) + dot_nt(g_other[rows, :], w_other[cols, :])
        out_ref[:, cols] = value.astype(out_ref.dtype)


def back_project(g_own, g_other, w_own, w_other, first, rows, dtype):
    return pl.pallas_call(
        functools.partial(back_project_kernel, first),
        out_shape=jax.ShapeDtypeStruct((rows, D), dtype),
        grid=(1,),
        in_specs=[VMEM, VMEM, QKV_COLS, QKV_COLS],
        out_specs=VMEM,
        compiler_params=params(40),
        cost_estimate=COST,
        name="back_project",
    )(g_own, g_other, w_own, w_other)


def back_first_kernel(
    tok_ref, part_ref, sent_ref, last_ref, mid_ref, gain_ref, out_ref, gain_grad_ref
):
    total = jnp.zeros((1, D), f32)
    for r in range(0, tok_ref.shape[0], ROWS):
        span = slice(r, r + ROWS)
        unit, inverse = norm_parts(tok_ref[span, :].astype(f32))
        sent = sent_ref[span, :] if r < OWN else last_ref[r - OWN : r - OWN + ROWS, :]
        grad = part_ref[span, :] + sent.astype(f32)
        total = total + jnp.sum(grad * unit, axis=0, keepdims=True)
        back = mid_ref[span, :] + norm_back(grad, unit, inverse, gain_ref[...])
        out_ref[span, :] = back.astype(bf16)
    gain_grad_ref[...] = total


def back_first(tokens, part, sent, last, grad_middle, gain):
    return pl.pallas_call(
        back_first_kernel,
        out_shape=(
            jax.ShapeDtypeStruct(tokens.shape, bf16),
            jax.ShapeDtypeStruct((1, D), f32),
        ),
        in_specs=[VMEM] * 6,
        out_specs=(VMEM,) * 2,
        compiler_params=params(32),
        cost_estimate=COST,
        name="back_first",
    )(tokens, part, sent, last, grad_middle, gain)


def weight_grad_kernel(
    ndp, nz, info, x_own, x_par, g_own, g_par, a_own, a_par, b_own, b_par,
    keep_ref, send_ref,
):
    block = D // ndp
    rows = block // nz
    z = info[ndp]
    half = ndp // 2
    for p in range(ndp):
        cols = pl.ds(pl.multiple_of(info[p] * block, block), block)
        qkv = dot(x_own[:, cols].T, g_own[...]) + dot(x_par[:, cols].T, g_par[...])
        out = dot(a_own[:, cols].T, b_own[...]) + dot(a_par[:, cols].T, b_par[...])
        qkv = qkv.astype(bf16)
        out = out.astype(bf16)
        dst = keep_ref if p < half else send_ref
        for b in range(nz):
            span = slice(b * rows, (b + 1) * rows)
            r = swap_bits(z ^ b, bits_of(nz))
            dst[p % half, r, :, : 3 * HALF] = qkv[span]
            dst[p % half, r, :, 3 * HALF :] = out[span]


def weight_grads(links, info, x_own, x_par, g_own, g_par, a_own, a_par, b_own, b_par):
    ndp, nz = links.ndp, links.nz
    rows = D // (ndp * nz)
    line = 4 * HALF
    out = jax.ShapeDtypeStruct((ndp // 2, nz, rows, line), bf16)
    return pl.pallas_call(
        functools.partial(weight_grad_kernel, ndp, nz),
        out_shape=(out, out),
        in_specs=[SMEM] + [VMEM] * 8,
        out_specs=(VMEM, VMEM),
        compiler_params=params(48),
        cost_estimate=COST,
        name="weight_grads",
    )(info, x_own, x_par, g_own, g_par, a_own, a_par, b_own, b_par)


def place_kernel(ndp, order, *refs):
    out = refs[ndp]
    b = pl.program_id(0)
    for p in range(ndp):

        @pl.when(order[b] == p)
        def _(p=p):
            out[...] = refs[p][...]


def place(links, order, pieces):
    block, cols = pieces[0].shape
    ndp = links.ndp
    return pl.pallas_call(
        functools.partial(place_kernel, ndp),
        out_shape=jax.ShapeDtypeStruct((ndp * block, cols), pieces[0].dtype),
        grid_spec=pltpu.PrefetchScalarGridSpec(
            num_scalar_prefetch=1,
            grid=(ndp,),
            in_specs=[VMEM] * ndp,
            out_specs=pl.BlockSpec((block, cols), lambda b, order: (b, 0)),
        ),
        compiler_params=params(16),
        cost_estimate=COST,
        name="place",
    )(order, *pieces)


def add_b(left, right):
    return (left.astype(f32) + right.astype(f32)).astype(bf16)


def in_order(links, values):
    ndp, nz = values.shape[:2]
    inner = values.shape[2:]
    bits = links.dp_bits + links.mp_bits - 1
    split = values.reshape((2,) * bits + inner)
    for axis in range(links.dp_bits):
        mine = (links.dp >> (links.dp_bits - 1 - axis)) & 1
        split = jnp.where(mine == 0, split, jnp.flip(split, axis))
    for axis in range(links.dp_bits, bits):
        mine = (links.z >> (bits - 1 - axis)) & 1
        split = jnp.where(mine == 0, split, jnp.flip(split, axis))
    dp_axes, z_axes = list(range(links.dp_bits)), list(range(links.dp_bits, bits))
    rest = list(range(bits, split.ndim))
    split = jnp.where(
        links.core == 0,
        split.transpose(dp_axes[::-1] + z_axes[::-1] + rest),
        split.transpose(dp_axes + z_axes[::-1] + rest),
    )
    return split.reshape(values.shape)


def pack(pieces):
    sizes = [piece.size for piece in pieces]
    packed = jnp.concatenate([piece.reshape(-1) for piece in pieces])
    return jnp.pad(packed, (0, -packed.shape[0] % 128)).reshape(-1, 128), sizes


def merge_kernel(inner, bit, here_ref, there_ref, out):
    count = here_ref.shape[0]
    for i in range(count):
        if inner:
            at, other = 2 * i + bit[0], 2 * i + 1 - bit[0]
        else:
            at, other = bit[0] * count + i, (1 - bit[0]) * count + i
        out[at] = here_ref[i]
        out[other] = there_ref[i]


def merge(here, there, bit, inner):
    shape = (2 * here.shape[0], *here.shape[1:])
    return pl.pallas_call(
        functools.partial(merge_kernel, inner),
        out_shape=jax.ShapeDtypeStruct(shape, here.dtype),
        in_specs=[SMEM, VMEM, VMEM],
        out_specs=VMEM,
        compiler_params=params(16),
        cost_estimate=COST,
        name="merge",
    )(bit.astype(jnp.int32).reshape(1), here, there)


def join_small(links, current, received, index, bit):
    return merge(current, received, (index >> bit) & 1, False)


class Live:
    pass


def fence(live, transfers=(), waits=()):
    held = dict(vars(live))
    tree = (held, [t.state for t in transfers], [t.received for t in waits])
    leaves, form = jax.tree.flatten(tree)
    held, states, received = jax.tree.unflatten(form, lax.optimization_barrier(leaves))
    vars(live).update(held)
    for t, state in zip(transfers, states):
        t.state = state
    for t, values in zip(waits, received):
        t.received = values
    for t in waits:
        t.join()


class Gather:
    def __init__(self, links, values):
        self.links = links
        self.state = [values[None]]
        self.kind = None

    def along_z(self, bit, first=0, last=None):
        self.kind, self.bit, self.span = "z", bit, slice(first, last)
        self.received = [self.links.mp_swap(piece, bit) for piece in self.state[self.span]]

    def along_dp(self, level):
        self.kind = "d"
        self.received = [self.links.fan(piece, level) for piece in self.state]

    def last_dp(self, first, last):
        if first == 0:
            self.count = len(self.state)
        last = self.count if last is None else last
        self.kind = "d"
        self.received = [self.links.fan(piece, 0) for piece in self.state[first:last]]

    def join(self):
        if self.kind == "d":
            self.state = self.state + self.received
        else:
            mine = (self.links.mp >> self.bit) & 1
            joined = [
                merge(piece, received, mine, True)
                for piece, received in zip(self.state[self.span], self.received)
            ]
            self.state = self.state[: self.span.start] + joined + (
                [] if self.span.stop is None else self.state[self.span.stop :]
            )
        self.received = None

    def first_z(self):
        for bit in reversed(range(2, self.links.mp_bits)):
            if self.received is not None:
                self.join()
            self.along_z(bit)

    def along_z_but_last(self, first, last):
        for bit in reversed(range(2, self.links.mp_bits)):
            if self.received is not None:
                self.join()
            self.along_z(bit, first, last)

    def first_dp(self):
        self.received = None
        for level in reversed(range(1, self.links.dp_bits)):
            if self.received is not None:
                self.join()
            self.along_dp(level)

    received = None

    def blocks(self):
        return [piece.reshape(-1, piece.shape[2]) for piece in self.state]


def add_kernel(axis, keep_ref, recv_ref, *outs):
    part = keep_ref.shape[axis] // len(outs)
    for i, out in enumerate(outs):
        span = (slice(None),) * axis + (slice(i * part, (i + 1) * part),)
        total = keep_ref[span].astype(f32) + recv_ref[span].astype(f32)
        out[...] = total.astype(out.dtype)


def add_split(keep, received, axis):
    shape = list(keep.shape)
    if axis is None:
        outs = (jax.ShapeDtypeStruct(shape, f32),)
    else:
        shape[axis] //= 2
        outs = (jax.ShapeDtypeStruct(shape, keep.dtype),) * 2
    return pl.pallas_call(
        functools.partial(add_kernel, axis or 0),
        out_shape=outs,
        in_specs=[VMEM] * 2,
        out_specs=(VMEM,) * len(outs),
        compiler_params=params(32),
        cost_estimate=COST,
        name="add_split",
    )(keep, received)


class Scatter:
    def __init__(self, links, keep, send):
        self.links = links
        self.state = [keep, send]
        self.steps = [("d", level) for level in range(links.dp_bits)]
        self.steps += [("z", bit) for bit in range(1, links.mp_bits)]
        self.result = None

    def start(self):
        kind, index = self.steps[0]
        swap = self.links.mp_swap if kind == "z" else self.links.fan
        self.received = swap(self.state[1], index)

    def join(self):
        self.steps.pop(0)
        keep, received = self.state[0], self.received
        if not self.steps:
            self.result = add_split(keep, received, None)[0][0, 0]
            self.state = []
            return
        self.state = list(add_split(keep, received, 1 if self.steps[0][0] == "z" else 0))

    def finish(self):
        while self.steps:
            self.start()
            self.join()


def body(
    tokens, cotangent, first_gain, second_gain, w_query, w_key, w_value, w_out, w_up, w_down,
    state_rate, state_in, state_out, state_bank, prev_link,
):
    links = Links()
    ndp, nmp, nz = links.ndp, links.nmp, links.nz
    rows = tokens.shape[0]
    per_window = LEN // BLK
    place_in = links.mp % per_window
    window = links.dp * (nmp // per_window) + links.mp // per_window
    link = lax.dynamic_index_in_dim(prev_link, window, keepdims=False)
    info = jnp.stack([links.block_at(p) for p in range(ndp)] + [links.z, links.core]).astype(jnp.int32)
    order = []
    for b in range(ndp):
        far = links.dp ^ b
        order.append(jnp.where(links.core == 0, swap_bits(far, links.dp_bits), far))
    order = jnp.stack(order).astype(jnp.int32)
    attend_info = jnp.stack([links.core, (place_in != 0).astype(jnp.int32)]).astype(jnp.int32)

    channels = state_rate.shape[0]
    maps_here = state_rate.shape[1]
    banks_here = state_bank.shape[0]

    def full_map(values):
        values = values.reshape(ndp, nmp, maps_here, channels).transpose(0, 2, 1, 3)
        return values.reshape(NS, 8, 128)

    def halves(values):
        values = values.reshape(values.shape[0], -1, 2, HALF)
        keep = jnp.where(links.core == 0, values[:, :, 0], values[:, :, 1])
        send = jnp.where(links.core == 0, values[:, :, 1], values[:, :, 0])
        return keep.reshape(keep.shape[0], -1), send.reshape(send.shape[0], -1)

    mats_keep, mats_send = halves(jnp.stack([w_query, w_key, w_value, w_out], 1).astype(bf16))
    chunk = FF // nmp
    groups = 2 if chunk >= 256 else 1
    width = chunk // groups
    both = jnp.stack([w_up, w_down.T], 1).astype(bf16)
    both = both.reshape(both.shape[0], 2, nz, 2, groups, width).transpose(0, 3, 4, 1, 2, 5)
    feed_rows = both.reshape(both.shape[0], -1)

    def chip_rows(keep, send):
        return by_core(links, keep, links.core_swap(send), 0)

    pieces = [
        first_gain, second_gain, state_rate.T, state_in.T, state_out.T,
        state_bank.transpose(0, 2, 1),
    ]
    small, sizes = pack(pieces)
    v = Live()
    v.tokens, v.cotangent = tokens, cotangent
    small = small[None]
    v.small = join_small(links, small, links.core_swap(small), links.mp, 0)
    attn = Gather(links, chip_rows(mats_keep, mats_send))
    v.feed_rows = feed_rows
    fence(v, [attn])

    attn.first_z()
    for bit in range(1, links.mp_bits):
        v.small = join_small(links, v.small, links.mp_swap(v.small, bit), links.mp, bit)
    fence(v, [attn], [attn])

    feed_weights = lax.all_gather(v.feed_rows, AXES, axis=0, tiled=True)
    del v.feed_rows
    attn.along_z(1)
    for bit in range(links.dp_bits):
        v.small = join_small(links, v.small, links.dp_swap(v.small, bit), links.dp, bit)
    small = v.small.reshape(ndp, nmp, -1)
    del v.small
    starts = [sum(sizes[:i]) for i in range(len(sizes))]
    gain_one, gain_two, rate, gain_in, gain_out, banks = (
        small[:, :, a : a + n] for a, n in zip(starts, sizes)
    )
    v.gain_one = lax.reduce_precision(gain_one.reshape(1, D), 8, 7)
    v.gain_two = lax.reduce_precision(gain_two.reshape(1, D), 8, 7)
    v.rate, v.gain_in, v.gain_out = full_map(rate), full_map(gain_in), full_map(gain_out)
    banks = banks.reshape(ndp, nmp, banks_here, NS, channels)
    bank = lax.dynamic_index_in_dim(banks, link // banks_here, 0, keepdims=False)
    bank = lax.dynamic_index_in_dim(bank, link % banks_here, 1, keepdims=False)
    v.initial = bank.transpose(1, 0, 2).reshape(NS, 8, 128)
    fence(v, [attn], [attn])

    half_blocks = float(BLK)
    v.scal = jnp.stack(
        [place_in.astype(f32) * half_blocks - CTX, (place_in != 0).astype(f32)]
    )
    v.steps, v.steps_back = [], []
    for bit in range(bits_of(per_window)):
        mine = ((links.mp >> bit) & 1).astype(f32)
        inside = (place_in % (1 << bit)).astype(f32)
        span = jnp.float32(half_blocks * (1 << bit))
        v.steps.append(jnp.stack([mine, inside * half_blocks, span]))
        v.steps_back.append(
            jnp.stack([mine, ((1 << bit) - 1 - inside) * half_blocks, span])
        )

    def exchange(bit):
        received = links.mp_swap(v.total, bit)
        v.total, v.before = exchange_step(v.steps[bit], v.total, received, v.before, v.rate)

    attn.first_dp()
    v.normed_b, tail = norm_first(v.tokens, v.gain_one)
    v.tail = links.window_shift(tail, 1)
    v.total = scan_tail(v.tail, scan_own(v.normed_b, v.rate), v.rate)
    v.before = jnp.zeros_like(v.total)
    exchange(0)
    fence(v, [attn], [attn])

    attn.last_dp(0, None)
    for bit in range(1, bits_of(per_window)):
        exchange(bit)
    v.inputs_kv = context_states(
        v.scal, v.tail, v.normed_b, v.before, v.initial, v.rate, v.gain_in, v.gain_out
    )
    v.cot_t = v.cotangent.T
    fence(v, [attn], [attn])

    v.w_own = place(links, order, attn.blocks())
    attn.state = []
    v.w_other = links.core_swap(v.w_own)
    v.qkv_own = project(v.inputs_kv, v.w_own)
    v.cot_par, v.cot_par_t = links.core_swap(v.cotangent), links.core_swap(v.cot_t)
    v.inputs_par = links.core_swap(v.inputs_kv)
    fence(v)
    v.qkv_other = project(v.inputs_kv, v.w_other)
    v.attended = attend(attend_info, v.qkv_own, v.qkv_other)
    v.middle, v.second_b, v.second_t = middle_norm(
        attend_info, v.attended, v.tokens, v.w_own, v.w_other, v.gain_two
    )
    v.attended_par = links.core_swap(v.attended)
    v.second_par, v.second_par_t = links.core_swap(v.second_b), links.core_swap(v.second_t)
    v.feed_weights = feed_weights
    fence(v)

    scatters = []
    earlier = None
    for g in range(groups):
        last = g == groups - 1
        acts = (
            v.second_b, v.second_par, v.cotangent, v.cot_par,
            v.second_t, v.second_par_t, v.cot_t, v.cot_par_t,
        )
        *v.sums, keep, send = feed(
            links, info, acts, v.feed_weights, nz * width, g, groups, earlier, last
        )
        waits = list(scatters)
        scatters.append(Scatter(links, keep, send))
        fence(v, scatters, waits)
        if not last:
            scatters[g].start()
        earlier = v.sums
    first, second = scatters[0], scatters[-1]
    both = [first, second] if groups > 1 else [first]
    v.mix_own, v.mix_par, v.back_own, back_par = v.sums
    del v.sums, v.feed_weights, v.cot_t, v.cot_par, v.cot_par_t, v.second_b, v.second_par
    del v.second_t, v.second_par_t

    for scatter in both:
        scatter.start()
    v.back_recv = links.core_swap(back_par)
    v.grad_middle, v.branch_own, branch_other, v.grad_attended, v.grad_gain_two = back_middle(
        attend_info, v.middle, v.back_own, v.back_recv, v.cotangent, v.gain_two, v.w_own,
        v.w_other,
    )
    v.branch_par = links.core_swap(branch_other)
    v.g_own, v.g_other = attend_back(attend_info, v.qkv_own, v.qkv_other, v.grad_attended)
    v.g_par = links.core_swap(v.g_other)
    v.grad_context = back_project(v.g_own, v.g_other, v.w_own, v.w_other, 0, CTX, bf16)
    v.lows = state_low(v.grad_context, v.rate)
    fence(v, both, both)

    def exchange_back(bit):
        received = links.mp_swap(v.total, bit)
        v.total, v.after = exchange_back_step(
            v.steps_back[bit], v.total, received, v.after, v.rate
        )

    for scatter in both:
        scatter.start()
    v.total = v.lows[0]
    v.after = jnp.zeros_like(v.total)
    exchange_back(0)
    mats = Scatter(
        links,
        *weight_grads(
            links, info, v.inputs_kv, v.inputs_par, v.g_own, v.g_par, v.attended,
            v.attended_par, v.branch_own, v.branch_par,
        ),
    )
    fence(v, [*both, mats], both)

    mats.start()
    for scatter in both:
        scatter.start()
    for bit in range(1, bits_of(per_window)):
        exchange_back(bit)
    sums = state_sums(
        v.scal, v.grad_context, v.tail, v.before, v.lows, v.initial, v.rate, v.gain_in, v.gain_out
    )

    def by_owner(values):
        values = values.reshape(ndp, maps_here, nmp, channels).transpose(0, 2, 1, 3)
        return values.reshape(ndp, nmp, -1)

    chosen = jnp.arange(ndp * banks_here, dtype=jnp.int32) == link
    bank_share = sums[3].reshape(NS, nmp, channels).transpose(1, 0, 2)[None]
    bank_share = jnp.where(chosen[:, None, None, None], bank_share, 0.0)
    bank_share = bank_share.reshape(ndp, banks_here, nmp, NS * channels).transpose(0, 2, 1, 3)
    shares = jnp.concatenate(
        [
            by_owner(sums[0]),
            by_owner(sums[1]),
            by_owner(sums[2]),
            bank_share.reshape(ndp, nmp, -1),
            v.grad_gain_two.reshape(ndp, nmp, -1),
        ],
        2,
    ).astype(bf16)
    share_len = shares.shape[2]
    mat_rows = D // (ndp * nz)
    shares = jnp.pad(shares, ((0, 0), (0, 0), (0, -share_len % (128 * mat_rows))))
    shares = shares.reshape(ndp, nz, 2, mat_rows, -1)
    shares_keep = jnp.where(links.core == 0, shares[:, :, 0], shares[:, :, 1])
    shares_send = jnp.where(links.core == 0, shares[:, :, 1], shares[:, :, 0])
    shares = in_order(links, add_b(shares_keep, links.core_swap(shares_send)))
    small = Scatter(links, shares[: ndp // 2], shares[ndp // 2 :])
    small.start()
    v.part = back_project(v.g_own, v.g_other, v.w_own, v.w_other, CTX, BLK, f32)
    fence(v, [*both, mats, small], [*both, mats, small])

    mats.state = [jnp.concatenate([a, b], -1) for a, b in zip(mats.state, small.state)]
    mats.start()
    late = [second] if second.steps else []
    for scatter in late:
        scatter.start()
    tail_sent = sent_tail(v.grad_context, v.after, v.rate, v.gain_in, v.gain_out)
    v.last_sent = links.window_shift(tail_sent, -1)
    v.own_sent = sent_own(v.after, v.rate, v.gain_in, v.gain_out)
    fence(v, [*both, mats], [mats, *late])
    mats.start()
    v.grad_tokens, grad_gain_one = back_first(
        v.tokens, v.part, v.own_sent, v.last_sent, v.grad_middle, v.gain_one
    )
    v.gain_parts = grad_gain_one.reshape(ndp * nmp, -1)
    v.mix_recv = links.core_swap(v.mix_par)
    fence(v, [*both, mats], [mats])
    gain_parts = lax.all_to_all(v.gain_parts, AXES, split_axis=0, concat_axis=0, tiled=True)
    v.share_one = jnp.sum(gain_parts, axis=0)
    mats.start()
    for scatter in both:
        scatter.finish()
    v.mixed = (v.middle + (v.mix_own + v.mix_recv.astype(f32))).astype(bf16)
    mats.join()
    mats.finish()
    grad_tokens = v.grad_tokens
    mixed, share_one = v.mixed, v.share_one
    mats_share = mats.result
    grad_up = jnp.concatenate([scatter.result[0] for scatter in both], 1)
    grad_down = jnp.concatenate([scatter.result[1] for scatter in both], 1).T

    line = 4 * HALF
    flat = mats_share[:, line:].reshape(-1)[:share_len]
    map_size = maps_here * channels
    grad_maps = [
        flat[i * map_size : (i + 1) * map_size].reshape(maps_here, channels).T for i in range(3)
    ]
    bank_end = share_len - D // (ndp * nmp)
    grad_bank = flat[3 * map_size : bank_end].reshape(banks_here, NS, channels)
    grad_bank = grad_bank.transpose(0, 2, 1)
    share_two = flat[bank_end:]
    mine_rows = mats_share[:, :line].reshape(2, mat_rows // 2, 4, HALF)
    rows_keep = jnp.where(links.core == 0, mine_rows[0], mine_rows[1])
    rows_send = jnp.where(links.core == 0, mine_rows[1], mine_rows[0])
    grad_rows = by_core(links, rows_keep, links.core_swap(rows_send), 2)
    return (
        mixed, grad_tokens, share_one, share_two,
        grad_rows[:, 0], grad_rows[:, 1], grad_rows[:, 2], grad_rows[:, 3],
        grad_up, grad_down, grad_maps[0], grad_maps[1], grad_maps[2], grad_bank,
    )


def solution(mesh):
    split = P(AXES, None)
    gain = P(AXES)
    maps = P("mp", "dp")
    bank = P("dp", "mp", None)
    return jax.shard_map(
        body,
        mesh=mesh,
        in_specs=(
            split, split, gain, gain, split, split, split, split, split, P(None, AXES),
            maps, maps, maps, bank, P(),
        ),
        out_specs=(
            split, split, gain, gain, split, split, split, split, P("dp", "mp"), P("mp", "dp"),
            maps, maps, maps, bank,
        ),
        check_vma=False,
    )
```

```python
import functools

import jax
import jax.numpy as jnp
from jax import lax
from jax.experimental import pallas as pl
from jax.experimental.pallas import tpu as pltpu
from jax.sharding import PartitionSpec as P

D = 1024
H = 8
HD = 128
FF = 4096
NS = 16
LEN = 4096
BLK = 512
CTX = 128
OWN = BLK - CTX
HALF = D // 2
SCALE = HD ** (-0.5)
AXES = ("dp", "mp")
f32 = jnp.float32
bf16 = jnp.bfloat16
VMEM = pl.BlockSpec(memory_space=pltpu.VMEM)
SMEM = pl.BlockSpec(memory_space=pltpu.SMEM)
ANY = pl.BlockSpec(memory_space=pltpu.HBM)
QKV_COLS = pl.BlockSpec((D, 3 * HALF), lambda i: (0, 0))
OUT_COLS = pl.BlockSpec((D, HALF), lambda i: (0, 3))
NT = (((1,), (1,)), ((), ()))
TN = (((0,), (0,)), ((), ()))


def params(mib):
    return pltpu.CompilerParams(vmem_limit_bytes=mib * 1024 * 1024)


def in_hbm(values):
    return pltpu.with_memory_space_constraint(values, pltpu.HBM)


def in_vmem(values):
    return pltpu.with_memory_space_constraint(values, pltpu.VMEM)


COST = pl.CostEstimate(flops=1, bytes_accessed=1, transcendentals=0)


def bits_of(n):
    return n.bit_length() - 1


def swap_bits(word, count):
    out = 0
    for i in range(count):
        out = out | (((word >> i) & 1) << (count - 1 - i))
    return out


class Links:
    def __init__(self):
        self.ndp = lax.axis_size("dp")
        self.nmp = lax.axis_size("mp")
        self.nz = self.nmp // 2
        self.dp = lax.axis_index("dp")
        self.mp = lax.axis_index("mp")
        self.z = self.mp // 2
        self.core = self.mp % 2
        self.dp_bits = bits_of(self.ndp)
        self.mp_bits = bits_of(self.nmp)

    def send(self, values, target):
        pairs = []
        for d in range(self.ndp):
            for m in range(self.nmp):
                to = target(d, m)
                if to is not None:
                    pairs.append((d * self.nmp + m, to[0] * self.nmp + to[1]))
        return lax.ppermute(values, AXES, pairs)

    def mp_swap(self, values, bit):
        return self.send(values, lambda d, m: (d, m ^ (1 << bit)))

    def dp_swap(self, values, bit):
        return self.send(values, lambda d, m: (d ^ (1 << bit), m))

    def core_swap(self, values):
        return self.mp_swap(values, 0)

    def fan(self, values, level):
        other = self.dp_bits - 1 - level
        return self.send(
            values, lambda d, m: (d ^ (1 << (other if m % 2 else level)), m)
        )

    def block_at(self, position):
        mirrored = swap_bits(position, self.dp_bits)
        return self.dp ^ jnp.where(self.core == 0, mirrored, position)

    def window_shift(self, values, step):
        per = LEN // BLK

        def target(d, m):
            inside = m % per + step
            return (d, m + step) if 0 <= inside < per else None

        return self.send(values, target)


def by_core(links, first, second, axis):
    return jnp.where(
        links.core == 0,
        jnp.concatenate([first, second], axis),
        jnp.concatenate([second, first], axis),
    )


def spread_rows(src_ref, dst_ref, rows, start=0):
    for r in range(0, rows, 16):
        block = src_ref[start + r : start + r + 16, :].astype(f32)
        for j in range(8):
            dst_ref[r : r + 16, j, :] = block[:, j * 128 : (j + 1) * 128]


def gather_rows(src_ref, dst_ref, rows):
    for r in range(0, rows, 16):
        for j in range(8):
            dst_ref[r : r + 16, j * 128 : (j + 1) * 128] = src_ref[r : r + 16, j, :].astype(
                dst_ref.dtype
            )


def move_on(state, rate, steps):
    far = jnp.exp(-rate * steps)
    near = jnp.exp(-rate * (steps - 1.0)) * steps
    return far * state[0], far * state[1] + near * state[0]


def scan_rows(xs, rows, decay):
    zero = jnp.zeros((NS, 8, 128), f32)

    def step(i, carry):
        u, v = carry
        for k in range(8):
            v = decay * v + u
            u = decay * u + xs[i * 8 + k][None]
        return u, v

    return lax.fori_loop(0, rows // 8, step, (zero, zero))


def scan_own_kernel(x_ref, rate_ref, out_ref, xs):
    spread_rows(x_ref, xs, OWN)
    u, v = scan_rows(xs, OWN, jnp.exp(-rate_ref[...]))
    out_ref[0] = u
    out_ref[1] = v


def scan_tail_kernel(x_ref, own_ref, rate_ref, out_ref, xs):
    spread_rows(x_ref, xs, CTX)
    state = scan_rows(xs, CTX, jnp.exp(-rate_ref[...]))
    u, v = move_on(state, rate_ref[...], float(OWN))
    out_ref[0] = u + own_ref[0]
    out_ref[1] = v + own_ref[1]


STATE = jax.ShapeDtypeStruct((2, NS, 8, 128), f32)


def scan_own(values, rate):
    return pl.pallas_call(
        scan_own_kernel,
        out_shape=STATE,
        in_specs=[VMEM, VMEM],
        out_specs=VMEM,
        scratch_shapes=[pltpu.VMEM((OWN, 8, 128), f32)],
        compiler_params=params(6),
        cost_estimate=COST,
        name="scan_own",
    )(values, rate)


def scan_tail(values, own, rate):
    return pl.pallas_call(
        scan_tail_kernel,
        out_shape=STATE,
        in_specs=[VMEM] * 3,
        out_specs=VMEM,
        scratch_shapes=[pltpu.VMEM((CTX, 8, 128), f32)],
        compiler_params=params(4),
        cost_estimate=COST,
        name="scan_tail",
    )(values, own, rate)


def exchange_kernel(scal, total_ref, recv_ref, before_ref, rate_ref, total_out, before_out):
    mine, inside, span = scal[0], scal[1], scal[2]
    rate = rate_ref[...]
    recv = (recv_ref[0], recv_ref[1])
    total = (total_ref[0], total_ref[1])
    moved = move_on(recv, rate, inside)
    low = tuple(mine * r + (1.0 - mine) * t for r, t in zip(recv, total))
    high = tuple(mine * t + (1.0 - mine) * r for r, t in zip(recv, total))
    far = move_on(low, rate, span)
    for i in range(2):
        before_out[i] = before_ref[i] + mine * moved[i]
        total_out[i] = far[i] + high[i]


def exchange_step(scal, total, received, before, rate):
    return pl.pallas_call(
        exchange_kernel,
        out_shape=(STATE, STATE),
        in_specs=[SMEM] + [VMEM] * 4,
        out_specs=(VMEM, VMEM),
        compiler_params=params(3),
        cost_estimate=COST,
        name="exchange_step",
    )(scal, total, received, before, rate)


def exchange_back_kernel(scal, total_ref, recv_ref, after_ref, rate_ref, total_out, after_out):
    mine, inside, span = scal[0], scal[1], scal[2]
    rate = rate_ref[...]
    recv, total = recv_ref[...], total_ref[...]
    after_out[...] = after_ref[...] + (1.0 - mine) * (jnp.exp(-rate * inside) * recv)
    low = mine * recv + (1.0 - mine) * total
    high = mine * total + (1.0 - mine) * recv
    total_out[...] = low + jnp.exp(-rate * span) * high


def exchange_back_step(scal, total, received, after, rate):
    one = jax.ShapeDtypeStruct((NS, 8, 128), f32)
    return pl.pallas_call(
        exchange_back_kernel,
        out_shape=(one, one),
        in_specs=[SMEM] + [VMEM] * 4,
        out_specs=(VMEM, VMEM),
        compiler_params=params(3),
        cost_estimate=COST,
        name="exchange_back_step",
    )(scal, total, received, after, rate)


def context_kernel(
    scal, x_ref, own_ref, before_ref, initial_ref, rate_ref, in_ref, out_map_ref, out_ref, xs, ys
):
    out_ref[CTX:, :] = own_ref[...]
    spread_rows(x_ref, xs, CTX)
    rate = rate_ref[...]
    decay = jnp.exp(-rate)
    weight = in_ref[...] * out_map_ref[...]
    carried = jnp.exp(-rate * scal[0]) * initial_ref[...] * scal[1]
    start = out_map_ref[...] * (in_ref[...] * before_ref[0] + carried)

    def step(i, y):
        for k in range(8):
            y = decay * y + weight * xs[i * 8 + k][None]
            ys[i * 8 + k] = jnp.sum(y, axis=0)
        return y

    lax.fori_loop(0, CTX // 8, step, start)
    gather_rows(ys, out_ref, CTX)


def context_states(scal, tail, own, before, initial, rate, gain_in, gain_out):
    return pl.pallas_call(
        context_kernel,
        out_shape=jax.ShapeDtypeStruct((CTX + BLK, D), bf16),
        in_specs=[SMEM] + [VMEM] * 7,
        out_specs=VMEM,
        scratch_shapes=[pltpu.VMEM((CTX, 8, 128), f32)] * 2,
        compiler_params=params(6),
        cost_estimate=COST,
        name="context_states",
    )(scal, tail, own, before, initial, rate, gain_in, gain_out)


def state_low_kernel(g_ref, rate_ref, out_ref, gs):
    spread_rows(g_ref, gs, CTX)
    decay = jnp.exp(-rate_ref[...])
    zero = jnp.zeros((NS, 8, 128), f32)

    def back(i, carry):
        low, slope = carry
        for k in range(8):
            slope = decay * slope + low
            low = decay * low + gs[CTX - 1 - (i * 8 + k)][None]
        return low, slope

    low, slope = lax.fori_loop(0, CTX // 8, back, (zero, zero))
    out_ref[0] = low
    out_ref[1] = slope


def state_low(grad_context, rate):
    return pl.pallas_call(
        state_low_kernel,
        out_shape=jax.ShapeDtypeStruct((2, NS, 8, 128), f32),
        in_specs=[VMEM] * 2,
        out_specs=VMEM,
        scratch_shapes=[pltpu.VMEM((CTX, 8, 128), f32)],
        compiler_params=params(3),
        cost_estimate=COST,
        name="state_low",
    )(grad_context, rate)


def state_sums_kernel(
    scal, g_ref, x_ref, start_ref, lows_ref, initial_ref, rate_ref, in_ref, out_map_ref, out_ref,
    gs, xs,
):
    spread_rows(g_ref, gs, CTX)
    spread_rows(x_ref, xs, CTX)
    part = NS // 2
    for n in range(0, NS, part):
        span = slice(n, n + part)
        rate = rate_ref[span]
        decay = jnp.exp(-rate)
        zero = jnp.zeros((part, 8, 128), f32)

        def step(i, carry):
            u, v, su, sv = carry
            for k in range(4):
                v = decay * v + u
                u = decay * u + xs[i * 4 + k][None]
                g = gs[i * 4 + k][None]
                su = su + g * u
                sv = sv + g * v
            return u, v, su, sv

        _, _, su, sv = lax.fori_loop(
            0, CTX // 4, step, (start_ref[0, span], start_ref[1, span], zero, zero)
        )
        far = jnp.exp(-rate * scal[0])
        low, slope = lows_ref[0, span], lows_ref[1, span]
        sum_init = far * decay * low
        sum_slope = far * ((scal[0] + 1.0) * low + decay * slope)
        initial = initial_ref[span] * scal[1]
        gain_in, gain_out = in_ref[span], out_map_ref[span]
        out_ref[0, span] = -decay * gain_out * (gain_in * sv + initial * sum_slope)
        out_ref[1, span] = gain_out * su
        out_ref[2, span] = gain_in * su + initial * sum_init
        out_ref[3, span] = gain_out * sum_init * scal[1]


def state_sums(scal, grad_context, tail, start, lows, initial, rate, gain_in, gain_out):
    return pl.pallas_call(
        state_sums_kernel,
        out_shape=jax.ShapeDtypeStruct((4, NS, 8, 128), f32),
        in_specs=[SMEM] + [VMEM] * 8,
        out_specs=VMEM,
        scratch_shapes=[pltpu.VMEM((CTX, 8, 128), f32)] * 2,
        compiler_params=params(4),
        cost_estimate=COST,
        name="state_sums",
    )(scal, grad_context, tail, start, lows, initial, rate, gain_in, gain_out)


def sent_tail_kernel(g_ref, after_ref, rate_ref, in_ref, out_map_ref, out_ref, gs, ys):
    spread_rows(g_ref, gs, CTX)
    rate = rate_ref[...]
    decay = jnp.exp(-rate)
    weight = in_ref[...] * out_map_ref[...]
    start = jnp.exp(-rate * float(OWN)) * weight * after_ref[...]

    def back(i, y):
        for k in range(8):
            t = CTX - 1 - (i * 8 + k)
            y = decay * y + weight * gs[t][None]
            ys[t] = jnp.sum(y, axis=0)
        return y

    lax.fori_loop(0, CTX // 8, back, start)
    gather_rows(ys, out_ref, CTX)


def sent_tail(grad_context, after, rate, gain_in, gain_out):
    return pl.pallas_call(
        sent_tail_kernel,
        out_shape=jax.ShapeDtypeStruct((CTX, D), bf16),
        in_specs=[VMEM] * 5,
        out_specs=VMEM,
        scratch_shapes=[pltpu.VMEM((CTX, 8, 128), f32)] * 2,
        compiler_params=params(4),
        cost_estimate=COST,
        name="sent_tail",
    )(grad_context, after, rate, gain_in, gain_out)


def sent_own_kernel(after_ref, rate_ref, in_ref, out_map_ref, out_ref, ys):
    decay = jnp.exp(-rate_ref[...])

    def back(i, y):
        for k in range(8):
            y = decay * y
            ys[OWN - 1 - (i * 8 + k)] = jnp.sum(y, axis=0)
        return y

    lax.fori_loop(0, OWN // 8, back, in_ref[...] * out_map_ref[...] * after_ref[...])
    gather_rows(ys, out_ref, OWN)


def sent_own(after, rate, gain_in, gain_out):
    return pl.pallas_call(
        sent_own_kernel,
        out_shape=jax.ShapeDtypeStruct((OWN, D), bf16),
        in_specs=[VMEM] * 4,
        out_specs=VMEM,
        scratch_shapes=[pltpu.VMEM((OWN, 8, 128), f32)],
        compiler_params=params(6),
        cost_estimate=COST,
        name="sent_own",
    )(after, rate, gain_in, gain_out)


def attention_mask(keys, queries, first_query, opened):
    row = lax.broadcasted_iota(jnp.int32, (keys, queries), 0)
    col = lax.broadcasted_iota(jnp.int32, (keys, queries), 1) + first_query
    return jnp.where(row < CTX, (1 - opened) * BLK, row - CTX) <= col


def head_parts(ref, offset):
    q = ref[CTX:, pl.ds(offset, HD)]
    k = ref[:, pl.ds(HALF + offset, HD)]
    v = ref[:, pl.ds(2 * HALF + offset, HD)]
    return q, k, v


def probabilities(k, q, first_query, opened):
    scores = lax.dot_general(k, q, NT, preferred_element_type=f32) * SCALE
    scores = jnp.where(
        attention_mask(k.shape[0], q.shape[0], first_query, opened), scores, -jnp.inf
    )
    lifted = jnp.exp(scores - jnp.max(scores, axis=0, keepdims=True))
    return lifted * (1.0 / jnp.sum(lifted, axis=0, keepdims=True))


QT = BLK // 2


def attend_kernel(info, own_ref, other_ref, out_ref):
    opened = info[1]

    @pl.loop(0, H // 2)
    def _(h):
        offset = pl.multiple_of(h * HD, HD)
        for side, qkv in enumerate((own_ref, other_ref)):
            q, k, v = head_parts(qkv, offset)
            v_t = v.T
            home = pl.multiple_of((side ^ info[0]) * HALF + h * HD, HD)
            for first in range(0, BLK, QT):
                keys = CTX + first + QT
                p = probabilities(k[:keys], q[first : first + QT], first, opened).astype(bf16)
                mixed = jnp.dot(v_t[:, :keys], p, preferred_element_type=f32)
                out_ref[first : first + QT, pl.ds(home, HD)] = mixed.T.astype(bf16)


def attend(info, own, other):
    return pl.pallas_call(
        attend_kernel,
        out_shape=jax.ShapeDtypeStruct((BLK, D), bf16),
        in_specs=[SMEM] + [VMEM] * 2,
        out_specs=VMEM,
        compiler_params=params(14),
        cost_estimate=COST,
        name="attend",
    )(info, own, other)


def attend_back_kernel(
    info, own_ref, other_ref, grad_ref, g_own_ref, g_other_ref, acc
):
    opened = info[1]
    sides = ((own_ref, g_own_ref), (other_ref, g_other_ref))
    for _, g in sides:
        g[:CTX, :HALF] = jnp.zeros((CTX, HALF), bf16)

    @pl.loop(0, H // 2)
    def _(h):
        offset = pl.multiple_of(h * HD, HD)
        for side, (qkv, g) in enumerate(sides):
            q, k, v = head_parts(qkv, offset)
            k_t = k.T
            home = pl.multiple_of((side ^ info[0]) * HALF + h * HD, HD)
            for first in range(0, BLK, QT):
                keys = CTX + first + QT
                q_now = q[first : first + QT]
                go = grad_ref[first : first + QT, pl.ds(home, HD)]
                p = probabilities(k[:keys], q_now, first, opened)
                gp = lax.dot_general(v[:keys], go, NT, preferred_element_type=f32)
                mean = jnp.sum(p * gp, axis=0, keepdims=True)
                gs = (p * (gp - mean)).astype(bf16)
                gq_t = jnp.dot(k_t[:, :keys], gs, preferred_element_type=f32) * SCALE
                g[CTX + first : CTX + first + QT, pl.ds(offset, HD)] = gq_t.T.astype(bf16)
                gk = jnp.dot(gs, q_now, preferred_element_type=f32)
                gv = jnp.dot(p.astype(bf16), go, preferred_element_type=f32)
                if first == 0:
                    acc[0, :keys] = gk
                    acc[1, :keys] = gv
                else:
                    early = CTX + QT
                    gk_all = jnp.concatenate([gk[:early] + acc[0, :early], gk[early:]], 0)
                    gv_all = jnp.concatenate([gv[:early] + acc[1, :early], gv[early:]], 0)
                    g[:, pl.ds(HALF + offset, HD)] = (gk_all * SCALE).astype(bf16)
                    g[:, pl.ds(2 * HALF + offset, HD)] = gv_all.astype(bf16)


def attend_back(info, own, other, grad):
    out = jax.ShapeDtypeStruct((CTX + BLK, 3 * HALF), bf16)
    return pl.pallas_call(
        attend_back_kernel,
        out_shape=(out, out),
        in_specs=[SMEM] + [VMEM] * 3,
        out_specs=(VMEM, VMEM),
        scratch_shapes=[pltpu.VMEM((2, CTX + QT, HD), f32)],
        compiler_params=params(18),
        cost_estimate=COST,
        name="attend_back",
    )(info, own, other, grad)


def gelu_parts(x):
    cdf = 0.5 * (1.0 + lax.erf(x * 0.7071067811865476))
    slope = cdf + x * (jnp.exp(-0.5 * x * x) * 0.3989422804014327)
    return x * cdf, slope


def feed_kernel(
    ndp, nz, width, index, groups, earlier, last, info, s_own, s_par, c_own, c_par,
    st_own, st_par, ct_own, ct_par, weights, *rest
):
    rows = s_own.shape[0]
    block = D // ndp
    group = nz * width
    half = ndp // 2
    s, c = (s_own, s_par), (c_own, c_par)
    if earlier:
        m_in, g_in, *rest = rest
    if last:
        m_own, m_par, g_own, g_par, *rest = rest
    else:
        m_out, g_out, *rest = rest
    parts, (st, ct, w, act, gh, sems) = rest[:4], rest[4:]
    at = [pl.multiple_of(info[p] * block, block) for p in range(ndp)]
    z = info[ndp]
    copies = []

    def start(src, dst):
        copy = pltpu.make_async_copy(src, dst, sems.at[len(copies)])
        copy.start()
        copies.append(copy)

    at_core = pl.multiple_of((info[ndp + 1] * groups + index) * 2 * group, 128)
    start(weights.at[:, pl.ds(at_core, 2 * group)], w)
    for own, par, dst in ((st_own, st_par, st), (ct_own, ct_par, ct)):
        for p in range(ndp):
            for i, src in enumerate((own, par)):
                start(
                    src.at[pl.ds(at[p], block), :],
                    dst.at[p * block : (p + 1) * block, i * rows : (i + 1) * rows],
                )
    copies[0].wait()

    @pl.loop(0, nz)
    def _(b):
        up = pl.ds(pl.multiple_of(b * width, width), width)
        down = pl.ds(pl.multiple_of(group + b * width, width), width)
        for i in range(2):
            part = slice(i * rows, (i + 1) * rows)
            hidden = jnp.dot(s[i][...], w[:, up], preferred_element_type=f32)
            grad = jnp.dot(c[i][...], w[:, down], preferred_element_type=f32)
            active, slope = gelu_parts(hidden)
            act[part, up] = active.astype(bf16)
            gh[part, up] = (grad * slope).astype(bf16)

    for copy in copies[1:]:
        copy.wait()

    @pl.loop(0, nz)
    def _(r):
        cols = pl.ds(pl.multiple_of((z ^ swap_bits(r, bits_of(nz))) * width, width), width)
        for part in range(2):
            span = slice(part * half * block, (part + 1) * half * block)
            up = jnp.dot(st[span, :], gh[:, cols], preferred_element_type=f32).astype(bf16)
            down = jnp.dot(ct[span, :], act[:, cols], preferred_element_type=f32).astype(bf16)
            for p in range(half):
                far = p >= half // 2
                dst = parts[2 * part + far]
                q = p - far * (half // 2)
                dst[q, r, 0] = up[p * block : (p + 1) * block]
                dst[q, r, 1] = down[p * block : (p + 1) * block]

    for name, left, first in (("g", gh, 0), ("m", act, group)):
        for p in range(ndp):
            right = w[p * block : (p + 1) * block, first : first + group]
            cols = slice(p * block, (p + 1) * block)
            for i in range(2):
                part = slice(i * rows, (i + 1) * rows)
                value = lax.dot_general(left[part, :], right, NT, preferred_element_type=f32)
                if earlier:
                    value = value + (g_in if name == "g" else m_in)[part, cols]
                if not last:
                    (g_out if name == "g" else m_out)[part, cols] = value
                elif i == 0:
                    (g_own if name == "g" else m_own)[:, cols] = value
                else:
                    (g_par if name == "g" else m_par)[:, cols] = value.astype(bf16)


def feed(links, info, acts, weights, group, index, groups, earlier, last):
    ndp, nz = links.ndp, links.nz
    rows = acts[0].shape[0]
    tokens = 2 * rows
    block = D // ndp
    width = group // nz
    half = ndp // 2
    full = pltpu.VMEM((tokens, D), f32)
    own = jax.ShapeDtypeStruct((rows, D), f32)
    par = jax.ShapeDtypeStruct((rows, D), bf16)
    grads = tuple(
        jax.ShapeDtypeStruct((count, nz, 2, block, width), bf16)
        for count in (half // 2, half - half // 2) * 2
    )
    out_shape = (own, par, own, par, *grads) if last else (full, full, *grads)
    earlier = tuple(earlier) if earlier else ()
    return pl.pallas_call(
        functools.partial(feed_kernel, ndp, nz, width, index, groups, bool(earlier), last),
        out_shape=out_shape,
        in_specs=[SMEM] + [VMEM] * len(acts) + [ANY] + [VMEM] * len(earlier),
        out_specs=(VMEM,) * len(out_shape),
        scratch_shapes=[
            pltpu.VMEM((D, tokens), bf16),
            pltpu.VMEM((D, tokens), bf16),
            pltpu.VMEM((D, 2 * group), bf16),
            pltpu.VMEM((tokens, group), bf16),
            pltpu.VMEM((tokens, group), bf16),
            pltpu.SemaphoreType.DMA((4 * ndp + 1,)),
        ],
        compiler_params=params(22),
        cost_estimate=COST,
        name="feed_last" if last else "feed_first",
    )(info, *map(in_vmem, acts), in_hbm(weights), *map(in_vmem, earlier))


def norm_parts(values):
    center = values - jnp.mean(values, axis=-1, keepdims=True)
    spread = jnp.mean(center * center, axis=-1, keepdims=True)
    inverse = lax.rsqrt(spread + 1e-05)
    return center * inverse, inverse


def norm_back(grad, unit, inverse, gain):
    scaled = grad * gain
    return (
        scaled
        - jnp.mean(scaled, axis=-1, keepdims=True)
        - unit * jnp.mean(scaled * unit, axis=-1, keepdims=True)
    ) * inverse


def dot(left, right):
    return jnp.dot(left, right, preferred_element_type=f32)


def dot_nt(left, right):
    return lax.dot_general(left, right, NT, preferred_element_type=f32)


ROWS = 128


def norm_kernel(x_ref, gain_ref, out_ref, tail_ref):
    for r in range(0, x_ref.shape[0], ROWS):
        unit, _ = norm_parts(x_ref[r : r + ROWS, :].astype(f32))
        out_ref[r : r + ROWS, :] = (unit * gain_ref[...]).astype(bf16)
    tail_ref[...] = out_ref[OWN:, :]


def norm_first(tokens, gain):
    return pl.pallas_call(
        norm_kernel,
        out_shape=(
            jax.ShapeDtypeStruct(tokens.shape, bf16),
            jax.ShapeDtypeStruct((CTX, D), bf16),
        ),
        in_specs=[VMEM] * 2,
        out_specs=(VMEM, VMEM),
        compiler_params=params(5),
        cost_estimate=COST,
        name="norm_first",
    )(tokens, gain)


def middle_kernel(
    info, att_ref, tok_ref, o_own, o_other, gain_ref, mid_ref, second_ref, second_t_ref
):
    att = att_ref[...]
    for side, weight in enumerate((o_own, o_other)):
        cols = pl.ds(pl.multiple_of((side ^ info[0]) * HALF, HALF), HALF)
        mid_ref[:, cols] = tok_ref[:, cols].astype(f32) + dot(att, weight[...])
    for r in range(0, att_ref.shape[0], ROWS):
        unit, _ = norm_parts(mid_ref[r : r + ROWS, :])
        second = unit * gain_ref[...]
        second_ref[r : r + ROWS, :] = second.astype(bf16)
        second_t_ref[:, r : r + ROWS] = second.T.astype(bf16)


def middle_norm(info, attended, tokens, o_own, o_other, gain):
    rows = tokens.shape[0]
    return pl.pallas_call(
        middle_kernel,
        out_shape=(
            jax.ShapeDtypeStruct((rows, D), f32),
            pltpu.VMEM((rows, D), bf16),
            pltpu.VMEM((D, rows), bf16),
        ),
        grid=(1,),
        in_specs=[SMEM, VMEM, VMEM, OUT_COLS, OUT_COLS, VMEM],
        out_specs=(VMEM,) * 3,
        compiler_params=params(16),
        cost_estimate=COST,
        name="middle_norm",
    )(info, attended, tokens, in_hbm(o_own), in_hbm(o_other), gain)


def back_middle_kernel(
    info, mid_ref, own_ref, recv_ref, cot_ref, gain_ref, o_own, o_other,
    grad_ref, b_own_ref, b_other_ref, att_ref, gain_grad_ref, branch,
):
    total = jnp.zeros((1, D), f32)
    for r in range(0, mid_ref.shape[0], ROWS):
        span = slice(r, r + ROWS)
        unit, inverse = norm_parts(mid_ref[span, :])
        grad = own_ref[span, :] + recv_ref[span, :].astype(f32)
        total = total + jnp.sum(grad * unit, axis=0, keepdims=True)
        back = cot_ref[span, :].astype(f32) + norm_back(grad, unit, inverse, gain_ref[...])
        grad_ref[span, :] = back
        branch[span, :] = back.astype(bf16)
    gain_grad_ref[...] = total
    for side, out in enumerate((b_own_ref, b_other_ref)):
        out[...] = branch[:, pl.ds(pl.multiple_of((side ^ info[0]) * HALF, HALF), HALF)]
    att = dot_nt(b_own_ref[...], o_own[...]) + dot_nt(b_other_ref[...], o_other[...])
    att_ref[...] = att.astype(bf16)


def back_middle(info, middle, own, received, cotangent, gain, o_own, o_other):
    rows = middle.shape[0]
    part = jax.ShapeDtypeStruct((rows, HALF), bf16)
    return pl.pallas_call(
        back_middle_kernel,
        out_shape=(
            jax.ShapeDtypeStruct((rows, D), f32),
            part,
            part,
            jax.ShapeDtypeStruct((rows, D), bf16),
            jax.ShapeDtypeStruct((1, D), f32),
        ),
        grid=(1,),
        in_specs=[SMEM] + [VMEM] * 5 + [OUT_COLS] * 2,
        out_specs=(VMEM,) * 5,
        scratch_shapes=[pltpu.VMEM((rows, D), bf16)],
        compiler_params=params(22),
        cost_estimate=COST,
        name="back_middle",
    )(info, middle, own, received, cotangent, gain, in_hbm(o_own), in_hbm(o_other))


def project_kernel(x_ref, w_ref, out_ref):
    for first in range(0, 3 * HALF, HALF):
        cols = slice(first, first + HALF)
        out_ref[:, cols] = dot(x_ref[...], w_ref[:, cols]).astype(bf16)


def project(values, weights):
    return pl.pallas_call(
        project_kernel,
        out_shape=jax.ShapeDtypeStruct((values.shape[0], 3 * HALF), bf16),
        grid=(1,),
        in_specs=[VMEM, QKV_COLS],
        out_specs=VMEM,
        compiler_params=params(16),
        cost_estimate=COST,
        name="project",
    )(values, in_hbm(weights))


def back_project_kernel(first, g_own, g_other, w_own, w_other, out_ref):
    rows = slice(first, first + out_ref.shape[0])
    for at in range(0, D, HALF):
        cols = slice(at, at + HALF)
        value = dot_nt(g_own[rows, :], w_own[cols, :]) + dot_nt(g_other[rows, :], w_other[cols, :])
        out_ref[:, cols] = value.astype(out_ref.dtype)


def back_project(g_own, g_other, w_own, w_other, first, rows, dtype):
    return pl.pallas_call(
        functools.partial(back_project_kernel, first),
        out_shape=jax.ShapeDtypeStruct((rows, D), dtype),
        grid=(1,),
        in_specs=[VMEM, VMEM, QKV_COLS, QKV_COLS],
        out_specs=VMEM,
        compiler_params=params(26),
        cost_estimate=COST,
        name="back_project",
    )(g_own, g_other, in_hbm(w_own), in_hbm(w_other))


def back_first_kernel(
    tok_ref, part_ref, sent_ref, last_ref, mid_ref, gain_ref, out_ref, gain_grad_ref
):
    total = jnp.zeros((1, D), f32)
    for r in range(0, tok_ref.shape[0], ROWS):
        span = slice(r, r + ROWS)
        unit, inverse = norm_parts(tok_ref[span, :].astype(f32))
        sent = sent_ref[span, :] if r < OWN else last_ref[r - OWN : r - OWN + ROWS, :]
        grad = part_ref[span, :] + sent.astype(f32)
        total = total + jnp.sum(grad * unit, axis=0, keepdims=True)
        back = mid_ref[span, :] + norm_back(grad, unit, inverse, gain_ref[...])
        out_ref[span, :] = back.astype(bf16)
    gain_grad_ref[...] = total


def back_first(tokens, part, sent, last, grad_middle, gain):
    return pl.pallas_call(
        back_first_kernel,
        out_shape=(
            jax.ShapeDtypeStruct(tokens.shape, bf16),
            jax.ShapeDtypeStruct((1, D), f32),
        ),
        in_specs=[VMEM] * 6,
        out_specs=(VMEM,) * 2,
        compiler_params=params(14),
        cost_estimate=COST,
        name="back_first",
    )(tokens, part, sent, last, grad_middle, gain)


def weight_grad_kernel(
    ndp, nz, info, x_own, x_par, g_own, g_par, a_own, a_par, b_own, b_par, shares,
    keep_ref, send_ref,
):
    block = D // ndp
    rows = block // nz
    z = info[ndp]
    half = ndp // 2
    for p in range(ndp):
        cols = pl.ds(pl.multiple_of(info[p] * block, block), block)
        grad = dot(x_own[:, cols].T, g_own[...]) + dot(x_par[:, cols].T, g_par[...])
        out = dot(a_own[:, cols].T, b_own[...]) + dot(a_par[:, cols].T, b_par[...])
        grad = grad.astype(bf16)
        out = out.astype(bf16)
        dst = keep_ref if p < half else send_ref
        for b in range(nz):
            r = swap_bits(z ^ b, bits_of(nz))
            span = slice(b * rows, (b + 1) * rows)
            dst[p % half, r, :, : 3 * HALF] = grad[span]
            dst[p % half, r, :, 3 * HALF : 4 * HALF] = out[span]
            dst[p % half, r, :, 4 * HALF :] = shares[p, r]


def weight_grads(links, info, x_own, x_par, g_own, g_par, a_own, a_par, b_own, b_par, shares):
    ndp, nz = links.ndp, links.nz
    line = 4 * HALF + shares.shape[3]
    out = jax.ShapeDtypeStruct((ndp // 2, nz, D // (ndp * nz), line), bf16)
    return pl.pallas_call(
        functools.partial(weight_grad_kernel, ndp, nz),
        out_shape=(out, out),
        in_specs=[SMEM] + [VMEM] * 9,
        out_specs=(VMEM, VMEM),
        compiler_params=params(24),
        cost_estimate=COST,
        name="weight_grads",
    )(info, x_own, x_par, g_own, g_par, a_own, a_par, b_own, b_par, shares)


def shares_kernel(ndp, nmp, maps, info, owner, sums_ref, gain_ref, out):
    for p in range(ndp):
        d = info[p]
        mine = (owner[0] == d).astype(f32)
        for m in range(nmp):
            r = swap_bits(info[ndp] ^ (m // 2), bits_of(nmp // 2))
            other = (m % 2) ^ info[ndp + 1]
            place_of = jnp.where(other == 0, p, swap_bits(p, bits_of(ndp)))
            to = out.at[other, place_of, r]
            for i in range(3):
                rows = sums_ref[i, pl.ds(d * maps, maps), m, :]
                to[i * maps : (i + 1) * maps, :] = rows
            to[3 * maps : 3 * maps + NS, :] = sums_ref[3, :, m, :] * mine
            to[3 * maps + NS :, :] = jnp.zeros((to.shape[0] - 3 * maps - NS, 128), f32)
            to[3 * maps + NS : 3 * maps + NS + 1, :] = gain_ref[pl.ds(d, 1), m, :]


def pack_shares(links, info, owner, sums, gain, maps, lines):
    out = jax.ShapeDtypeStruct((2, links.ndp, links.nz, lines, 128), f32)
    return pl.pallas_call(
        functools.partial(shares_kernel, links.ndp, links.nmp, maps),
        out_shape=out,
        in_specs=[SMEM, SMEM, VMEM, VMEM],
        out_specs=VMEM,
        compiler_params=params(3),
        cost_estimate=COST,
        name="pack_shares",
    )(info, owner, sums, gain)


def prepare_kernel(nz, groups, core, q_ref, k_ref, v_ref, o_ref, up_ref, down_ref, keep, send, feed):
    for i, ref in enumerate((q_ref, k_ref, v_ref, o_ref)):
        to = slice(i * HALF, (i + 1) * HALF)
        keep[:, to] = ref[:, pl.ds(pl.multiple_of(core[0] * HALF, HALF), HALF)].astype(bf16)
        send[:, to] = ref[:, pl.ds(pl.multiple_of((1 - core[0]) * HALF, HALF), HALF)].astype(bf16)
    width = FF // (2 * nz * groups)
    at = 0
    for c in range(2):
        for g in range(groups):
            for ref in (up_ref, down_ref):
                for b in range(nz):
                    first = ((b * 2 + c) * groups + g) * width
                    feed[:, at : at + width] = ref[:, first : first + width].astype(bf16)
                    at += width


def prepare(links, groups, core, mats, up, down):
    rows = up.shape[0]
    part = jax.ShapeDtypeStruct((rows, 4 * HALF), bf16)
    return pl.pallas_call(
        functools.partial(prepare_kernel, links.nz, groups),
        out_shape=(part, part, jax.ShapeDtypeStruct((rows, 2 * FF), bf16)),
        in_specs=[SMEM] + [VMEM] * 6,
        out_specs=(VMEM,) * 3,
        compiler_params=params(5),
        cost_estimate=COST,
        name="prepare",
    )(core, *(in_hbm(values) for values in (*mats, up, down)))


def place_kernel(ndp, order, *refs):
    out = refs[ndp]
    b = pl.program_id(0)
    for p in range(ndp):

        @pl.when(order[b] == p)
        def _(p=p):
            out[...] = refs[p][...]


def place(links, order, pieces):
    block, cols = pieces[0].shape
    ndp = links.ndp
    return pl.pallas_call(
        functools.partial(place_kernel, ndp),
        out_shape=pltpu.HBM((ndp * block, cols), pieces[0].dtype),
        grid_spec=pltpu.PrefetchScalarGridSpec(
            num_scalar_prefetch=1,
            grid=(ndp,),
            in_specs=[VMEM] * ndp,
            out_specs=pl.BlockSpec((block, cols), lambda b, order: (b, 0)),
        ),
        compiler_params=params(12),
        cost_estimate=COST,
        name="place",
    )(order, *pieces)


def add_b(left, right):
    return (left.astype(f32) + right.astype(f32)).astype(bf16)


def in_order(links, values, core):
    ndp, nz = values.shape[:2]
    inner = values.shape[2:]
    bits = links.dp_bits + links.mp_bits - 1
    split = values.reshape((2,) * bits + inner)
    for axis in range(links.dp_bits):
        mine = (links.dp >> (links.dp_bits - 1 - axis)) & 1
        split = jnp.where(mine == 0, split, jnp.flip(split, axis))
    for axis in range(links.dp_bits, bits):
        mine = (links.z >> (bits - 1 - axis)) & 1
        split = jnp.where(mine == 0, split, jnp.flip(split, axis))
    dp_axes, z_axes = list(range(links.dp_bits)), list(range(links.dp_bits, bits))
    rest = list(range(bits, split.ndim))
    split = split.transpose((dp_axes if core else dp_axes[::-1]) + z_axes[::-1] + rest)
    return split.reshape(values.shape)


def pack(pieces):
    sizes = [piece.size for piece in pieces]
    packed = jnp.concatenate([piece.reshape(-1) for piece in pieces])
    return jnp.pad(packed, (0, -packed.shape[0] % 128)).reshape(-1, 128), sizes


def merge_kernel(inner, bit, here_ref, there_ref, out):
    count = here_ref.shape[0]
    for i in range(count):
        if inner:
            at, other = 2 * i + bit[0], 2 * i + 1 - bit[0]
        else:
            at, other = bit[0] * count + i, (1 - bit[0]) * count + i
        out[at] = here_ref[i]
        out[other] = there_ref[i]


def merge(here, there, bit, inner):
    shape = (2 * here.shape[0], *here.shape[1:])
    return pl.pallas_call(
        functools.partial(merge_kernel, inner),
        out_shape=jax.ShapeDtypeStruct(shape, here.dtype),
        in_specs=[SMEM, VMEM, VMEM],
        out_specs=VMEM,
        compiler_params=params(6),
        cost_estimate=COST,
        name="merge",
    )(bit.astype(jnp.int32).reshape(1), here, there)


def join_small(links, current, received, index, bit):
    return merge(current, received, (index >> bit) & 1, False)


def pack_shares_plain(links, owner, row, banks_here, sums, gain, maps):
    ndp, nmp = links.ndp, links.nmp
    channels = gain.shape[2]

    def by_owner(values):
        values = values.reshape(ndp, maps, nmp, channels)
        return values.transpose(0, 2, 1, 3)

    bank = sums[3].reshape(NS, nmp, channels).transpose(1, 0, 2)
    here = jnp.arange(ndp * banks_here, dtype=jnp.int32) == owner * banks_here + row
    bank = jnp.where(here[:, None, None, None], bank[None], 0.0)
    bank = bank.reshape(ndp, banks_here, nmp, NS, channels).transpose(0, 2, 1, 3, 4)
    bank = bank.reshape(ndp, nmp, banks_here * NS, channels)
    lines = [by_owner(sums[0]), by_owner(sums[1]), by_owner(sums[2]), bank, gain[:, :, None]]
    shares = jnp.concatenate(lines, 2)
    rows = D // (ndp * links.nz)
    shares = shares.reshape(ndp, nmp, -1)
    shares = jnp.pad(shares, ((0, 0), (0, 0), (0, -shares.shape[2] % (128 * rows))))
    shares = shares.reshape(ndp, nmp // 2, 2, rows, -1)
    parts = [in_order(links, shares[:, :, c], c) for c in range(2)]
    return jnp.where(links.core == 0, jnp.stack(parts), jnp.stack(parts[::-1]))


class Live:
    pass


def fence(live, transfers=(), waits=()):
    held = dict(vars(live))
    tree = (held, [t.outgoing for t in transfers], [t.received for t in waits])
    leaves, form = jax.tree.flatten(tree)
    held, states, received = jax.tree.unflatten(form, lax.optimization_barrier(leaves))
    vars(live).update(held)
    for t, state in zip(transfers, states):
        t.outgoing = state
    for t, values in zip(waits, received):
        t.received = values
    for t in waits:
        t.join()


class Gather:
    def __init__(self, links, values):
        self.links = links
        self.state = [values[None]]
        self.kind = None

    def along_z(self, bit, first=0, last=None):
        self.kind, self.bit, self.span = "z", bit, slice(first, last)
        self.received = [self.links.mp_swap(piece, bit) for piece in self.state[self.span]]

    def along_dp(self, level):
        self.kind = "d"
        self.received = [self.links.fan(piece, level) for piece in self.state]

    def more_dp(self):
        self.count = 2 * len(self.state)
        self.ahead = [self.links.fan(piece, 0) for piece in self.state]
        self.received = self.received + self.ahead

    def last_dp(self, first, last):
        if first == 0:
            self.count = len(self.state)
        last = self.count if last is None else last
        self.kind = "d"
        self.received = [self.links.fan(piece, 0) for piece in self.state[first:last]]

    @property
    def outgoing(self):
        return self.state

    @outgoing.setter
    def outgoing(self, values):
        self.state = values

    def join(self):
        if self.kind == "d":
            self.state = self.state + self.received
        else:
            mine = (self.links.mp >> self.bit) & 1
            joined = [
                merge(piece, received, mine, True)
                for piece, received in zip(self.state[self.span], self.received)
            ]
            self.state = self.state[: self.span.start] + joined + (
                [] if self.span.stop is None else self.state[self.span.stop :]
            )
        self.received = None

    def first_z(self):
        for bit in reversed(range(2, self.links.mp_bits)):
            if self.received is not None:
                self.join()
            self.along_z(bit)

    def along_z_but_last(self, first, last):
        for bit in reversed(range(2, self.links.mp_bits)):
            if self.received is not None:
                self.join()
            self.along_z(bit, first, last)

    def first_dp(self):
        self.received = None
        for level in reversed(range(1, self.links.dp_bits)):
            if self.received is not None:
                self.join()
            self.along_dp(level)

    received = None

    def blocks(self):
        return [piece.reshape(-1, piece.shape[2]) for piece in self.state]


def add_kernel(axis, keep_ref, recv_ref, *outs):
    part = keep_ref.shape[axis] // len(outs)
    for i, out in enumerate(outs):
        span = (slice(None),) * axis + (slice(i * part, (i + 1) * part),)
        total = keep_ref[span].astype(f32) + recv_ref[span].astype(f32)
        out[...] = total.astype(out.dtype)


def mix_kernel(middle_ref, own_ref, recv_ref, out_ref):
    total = middle_ref[...] + (own_ref[...] + recv_ref[...].astype(f32))
    out_ref[...] = total.astype(bf16)


def mix(middle, own, received):
    return pl.pallas_call(
        mix_kernel,
        out_shape=jax.ShapeDtypeStruct(middle.shape, bf16),
        in_specs=[VMEM] * 3,
        out_specs=VMEM,
        compiler_params=params(10),
        cost_estimate=COST,
        name="mix",
    )(middle, own, received)


def add_split(keep, received, axis, dtype=None):
    shape = list(keep.shape)
    if axis is False:
        outs = (jax.ShapeDtypeStruct(shape, dtype or keep.dtype),)
    elif axis is None:
        outs = (jax.ShapeDtypeStruct(shape, f32),)
    else:
        shape[axis] //= 2
        outs = (jax.ShapeDtypeStruct(shape, keep.dtype),) * 2
    return pl.pallas_call(
        functools.partial(add_kernel, axis or 0),
        out_shape=outs,
        in_specs=[VMEM] * 2,
        out_specs=(VMEM,) * len(outs),
        compiler_params=params(10),
        cost_estimate=COST,
        name="add_split",
    )(keep, received)


class Scatter:
    def __init__(self, links, keep, send, *far):
        self.links = links
        self.state = [keep, send, *far]
        self.steps = [("d", level) for level in range(links.dp_bits)]
        self.steps += [("z", bit) for bit in range(1, links.mp_bits)]
        self.result = None

    def start(self):
        kind, index = self.steps[0]
        swap = self.links.mp_swap if kind == "z" else self.links.fan
        self.received = [swap(part, index) for part in self.state[1::2]]

    @property
    def outgoing(self):
        return self.state[1::2]

    @outgoing.setter
    def outgoing(self, values):
        self.state[1::2] = values

    def start_far(self):
        self.received = [self.links.fan(self.state.pop(), 0)]
        self.parts = "far"

    def start_near(self):
        self.received = [self.links.fan(self.state[1], 0)]
        self.parts = "near"

    parts = None

    def join(self):
        if self.parts == "far":
            self.parts = None
            keep_far = self.state.pop()
            self.state.append(add_split(keep_far, self.received[0], False)[0])
            return
        keep, received = self.state[0], self.received
        self.steps.pop(0)
        if self.parts == "near":
            self.parts = None
            received, far = lax.optimization_barrier((received[0], self.state[2]))
            self.state = [add_split(keep, received, False)[0], far]
        elif len(received) == 2:
            self.state = [
                add_split(keep, received[0], False)[0],
                add_split(self.state[2], received[1], False)[0],
            ]
        elif not self.steps:
            self.result = add_split(keep, received[0], None)[0][0, 0]
            self.state = []
        else:
            axis = 1 if self.steps[0][0] == "z" else 0
            self.state = list(add_split(keep, received[0], axis))

    def finish(self):
        while self.steps:
            self.start()
            self.join()


def body(
    tokens, cotangent, first_gain, second_gain, w_query, w_key, w_value, w_out, w_up, w_down,
    state_rate, state_in, state_out, state_bank, prev_link,
):
    links = Links()
    ndp, nmp, nz = links.ndp, links.nmp, links.nz
    rows = tokens.shape[0]
    per_window = LEN // BLK
    place_in = links.mp % per_window
    window = links.dp * (nmp // per_window) + links.mp // per_window
    link = lax.dynamic_index_in_dim(prev_link, window, keepdims=False)
    info = jnp.stack([links.block_at(p) for p in range(ndp)] + [links.z, links.core]).astype(jnp.int32)
    order = []
    for b in range(ndp):
        far = links.dp ^ b
        order.append(jnp.where(links.core == 0, swap_bits(far, links.dp_bits), far))
    order = jnp.stack(order).astype(jnp.int32)
    attend_info = jnp.stack([links.core, (place_in != 0).astype(jnp.int32)]).astype(jnp.int32)

    channels = state_rate.shape[0]
    maps_here = state_rate.shape[1]
    banks_here = state_bank.shape[0]

    def full_map(values):
        values = values.reshape(ndp, nmp, maps_here, channels).transpose(0, 2, 1, 3)
        return values.reshape(NS, 8, 128)

    chunk = FF // nmp
    groups = 2 if chunk >= 256 else 1
    width = chunk // groups
    mats_keep, mats_send, feed_rows = prepare(
        links, groups, links.core.astype(jnp.int32).reshape(1),
        (w_query, w_key, w_value, w_out), w_up, w_down.T,
    )

    def chip_rows(keep, send):
        return by_core(links, keep, links.core_swap(send), 0)

    pieces = [
        first_gain, second_gain, state_rate.T, state_in.T, state_out.T,
        state_bank.transpose(0, 2, 1),
    ]
    small, sizes = pack(pieces)
    v, u = Live(), Live()
    v.tokens, v.cotangent = tokens, cotangent
    small = small[None]
    v.small = join_small(links, small, links.core_swap(small), links.mp, 0)
    attn = Gather(links, chip_rows(mats_keep, mats_send))
    v.feed_rows = feed_rows
    fence(v, [attn])

    for bit in range(1, links.mp_bits):
        v.small = join_small(links, v.small, links.mp_swap(v.small, bit), links.mp, bit)
    fence(v, [attn])

    feed_weights = lax.all_gather(v.feed_rows, AXES, axis=0, tiled=True)
    del v.feed_rows
    attn.first_z()
    for bit in range(links.dp_bits):
        v.small = join_small(links, v.small, links.dp_swap(v.small, bit), links.dp, bit)
    fence(v, [attn], [attn])
    attn.along_z(1)
    small = v.small.reshape(ndp, nmp, -1)
    del v.small
    starts = [sum(sizes[:i]) for i in range(len(sizes))]
    gain_one, gain_two, rate, gain_in, gain_out, banks = (
        small[:, :, a : a + n] for a, n in zip(starts, sizes)
    )
    v.gain_one = lax.reduce_precision(gain_one.reshape(1, D), 8, 7)
    v.gain_two = lax.reduce_precision(gain_two.reshape(1, D), 8, 7)
    u.rate, u.gain_in, u.gain_out = full_map(rate), full_map(gain_in), full_map(gain_out)
    banks = banks.reshape(ndp, nmp, banks_here, NS, channels)
    bank = lax.dynamic_index_in_dim(banks, link // banks_here, 0, keepdims=False)
    bank = lax.dynamic_index_in_dim(bank, link % banks_here, 1, keepdims=False)
    u.initial = bank.transpose(1, 0, 2).reshape(NS, 8, 128)
    half_blocks = float(BLK)
    v.scal = jnp.stack(
        [place_in.astype(f32) * half_blocks - CTX, (place_in != 0).astype(f32)]
    )
    v.steps, v.steps_back = [], []
    for bit in range(bits_of(per_window)):
        mine = ((links.mp >> bit) & 1).astype(f32)
        inside = (place_in % (1 << bit)).astype(f32)
        span = jnp.float32(half_blocks * (1 << bit))
        v.steps.append(jnp.stack([mine, inside * half_blocks, span]))
        v.steps_back.append(
            jnp.stack([mine, ((1 << bit) - 1 - inside) * half_blocks, span])
        )

    def exchange(bit):
        received = links.mp_swap(v.total, bit)
        v.total, v.before = exchange_step(v.steps[bit], v.total, received, v.before, u.rate)

    u.normed_b, tail = norm_first(v.tokens, v.gain_one)
    u.tail = links.window_shift(tail, 1)
    v.total = scan_own(u.normed_b, u.rate)
    fence(v, [attn], [attn])

    attn.first_dp()
    attn.more_dp()
    v.total = scan_tail(u.tail, v.total, u.rate)
    v.before = jnp.zeros_like(v.total)
    for bit in range(2):
        exchange(bit)
    v.cot_t = v.cotangent.T
    v.cot_par = links.core_swap(v.cotangent)
    fence(v, [attn], [attn])
    attn.last_dp(max(ndp // 4, 1), None)
    for bit in range(2, bits_of(per_window)):
        exchange(bit)
    v.inputs_kv = context_states(
        v.scal, u.tail, u.normed_b, v.before, u.initial, u.rate, u.gain_in, u.gain_out
    )
    v.cot_par_t = links.core_swap(v.cot_t)
    fence(v, [attn], [attn])

    v.w_own = place(links, order, attn.blocks())
    attn.state = []
    v.w_other = links.core_swap(v.w_own)
    v.qkv_own = project(v.inputs_kv, v.w_own)
    fence(v)
    v.inputs_par = links.core_swap(v.inputs_kv)
    u.qkv_other = project(v.inputs_kv, v.w_other)
    v.attended = attend(attend_info, v.qkv_own, u.qkv_other)
    u.middle, u.second_b, u.second_t = middle_norm(
        attend_info, v.attended, v.tokens, v.w_own, v.w_other, v.gain_two
    )
    u.second_par, u.second_par_t = links.core_swap(u.second_b), links.core_swap(u.second_t)
    v.feed_weights = feed_weights
    fence(v)

    scatters = []
    earlier = None
    for g in range(groups):
        last = g == groups - 1
        acts = (
            u.second_b, u.second_par, v.cotangent, v.cot_par,
            u.second_t, u.second_par_t, v.cot_t, v.cot_par_t,
        )
        *u.sums, keep, keep_far, send, send_far = feed(
            links, info, acts, v.feed_weights, nz * width, g, groups, earlier, last
        )
        if g == 0:
            v.attended_par = links.core_swap(v.attended)
        waits = list(scatters)
        scatters.append(Scatter(links, keep, send, keep_far, send_far))
        fence(v, scatters, waits)
        if not last:
            scatters[g].start()
        earlier = u.sums
    first, second = scatters[0], scatters[-1]
    both = [first, second] if groups > 1 else [first]
    u.mix_own, v.mix_par, u.back_own, back_par = u.sums
    del v.feed_weights, v.cot_t, v.cot_par, v.cot_par_t

    split = groups > 1 and ndp >= 4
    if split:
        first.start()
        second.start_far()
    else:
        second.start()
    v.back_recv = links.core_swap(back_par)
    v.grad_middle, v.branch_own, branch_other, v.grad_attended, v.grad_gain_two = back_middle(
        attend_info, u.middle, u.back_own, v.back_recv, v.cotangent, v.gain_two, v.w_own,
        v.w_other,
    )
    v.branch_par = links.core_swap(branch_other)
    v.grad_gain_two = v.grad_gain_two.reshape(ndp, nmp, -1)
    gain_len = v.grad_gain_two.shape[2]
    v.grad_gain_two = jnp.pad(v.grad_gain_two, ((0, 0), (0, 0), (0, channels - gain_len)))
    v.g_own, v.g_other = attend_back(attend_info, v.qkv_own, u.qkv_other, v.grad_attended)
    fence(v, both, both)

    def exchange_back(bit):
        received = links.mp_swap(v.total, bit)
        v.total, v.after = exchange_back_step(
            v.steps_back[bit], v.total, received, v.after, u.rate
        )

    if split:
        second.start_near()
    v.g_par = links.core_swap(v.g_other)
    v.grad_context = back_project(v.g_own, v.g_other, v.w_own, v.w_other, 0, CTX, bf16)
    v.lows = state_low(v.grad_context, u.rate)
    v.total = v.lows[0]
    v.after = jnp.zeros_like(v.total)
    sums = state_sums(
        v.scal, v.grad_context, u.tail, v.before, v.lows, u.initial, u.rate, u.gain_in, u.gain_out
    )
    bank_owner = link // banks_here
    mat_rows = D // (ndp * nz)
    whole_lines = channels == 128 and banks_here == 1
    if whole_lines:
        shares = pack_shares(
            links, info, bank_owner.reshape(1), sums, v.grad_gain_two, maps_here, mat_rows
        )
    else:
        shares = pack_shares_plain(
            links, bank_owner, link % banks_here, banks_here, sums, v.grad_gain_two, maps_here
        )
    v.shares = add_split(shares[0], links.core_swap(shares[1].astype(bf16)), False, bf16)[0]
    for bit in range(2):
        exchange_back(bit)
    fence(v, both, [second] if split else [])

    for scatter in both:
        scatter.start()
    mats = Scatter(
        links,
        *weight_grads(
            links, info, v.inputs_kv, v.inputs_par, v.g_own, v.g_par, v.attended,
            v.attended_par, v.branch_own, v.branch_par, v.shares,
        ),
    )
    for bit in range(2, bits_of(per_window)):
        exchange_back(bit)
    fence(v, [*both, mats], both)

    mats.start()
    for scatter in both:
        scatter.start()
    tail_sent = sent_tail(v.grad_context, v.after, u.rate, u.gain_in, u.gain_out)
    v.last_sent = links.window_shift(tail_sent, -1)
    v.own_sent = sent_own(v.after, u.rate, u.gain_in, u.gain_out)
    v.part = back_project(v.g_own, v.g_other, v.w_own, v.w_other, CTX, BLK, f32)
    v.grad_tokens, grad_gain_one = back_first(
        v.tokens, v.part, v.own_sent, v.last_sent, v.grad_middle, v.gain_one
    )
    v.gain_parts = grad_gain_one.reshape(ndp * nmp, -1)
    fence(v, [*both, mats], [mats, *both])
    mats.start()
    late = [second] if second.steps else []
    for scatter in late:
        scatter.start()
    gain_parts = lax.all_to_all(v.gain_parts, AXES, split_axis=0, concat_axis=0, tiled=True)
    v.share_one = jnp.sum(gain_parts, axis=0)
    v.mix_recv = links.core_swap(v.mix_par)
    fence(v, [*both, mats], [mats, *late])
    mats.start()
    v.mixed = mix(u.middle, u.mix_own, v.mix_recv)
    for scatter in both:
        scatter.finish()
    v.results = [scatter.result for scatter in both]
    fence(v, [mats], [mats])
    mats.start()
    grad_up = jnp.concatenate([result[0] for result in v.results], 1)
    grad_down = jnp.concatenate([result[1] for result in v.results], 1).T
    mats.join()
    mats.finish()
    grad_tokens = v.grad_tokens
    mixed, share_one = v.mixed, v.share_one
    mats_share = mats.result
    line = 4 * HALF
    extra = mats_share[:, line:]
    if not whole_lines:
        lines = 3 * maps_here + banks_here * NS + 1
        extra = extra.reshape(-1)[: lines * channels].reshape(lines, channels)
    grad_maps = [
        extra[i * maps_here : (i + 1) * maps_here].T for i in range(3)
    ]
    bank_end = 3 * maps_here + banks_here * NS
    grad_bank = extra[3 * maps_here : bank_end].reshape(banks_here, NS, channels)
    grad_bank = grad_bank.transpose(0, 2, 1)
    share_two = extra[bank_end, :gain_len]
    mine_rows = mats_share[:, :line].reshape(2, mat_rows // 2, 4, HALF)
    rows_keep = jnp.where(links.core == 0, mine_rows[0], mine_rows[1])
    rows_send = jnp.where(links.core == 0, mine_rows[1], mine_rows[0])
    grad_rows = by_core(links, rows_keep, links.core_swap(rows_send), 2)
    return (
        mixed, grad_tokens, share_one, share_two,
        grad_rows[:, 0], grad_rows[:, 1], grad_rows[:, 2], grad_rows[:, 3],
        grad_up, grad_down, grad_maps[0], grad_maps[1], grad_maps[2], grad_bank,
    )


def solution(mesh):
    split = P(AXES, None)
    gain = P(AXES)
    maps = P("mp", "dp")
    bank = P("dp", "mp", None)
    return jax.shard_map(
        body,
        mesh=mesh,
        in_specs=(
            split, split, gain, gain, split, split, split, split, split, P(None, AXES),
            maps, maps, maps, bank, P(),
        ),
        out_specs=(
            split, split, gain, gain, split, split, split, split, P("dp", "mp"), P("mp", "dp"),
            maps, maps, maps, bank,
        ),
        check_vma=False,
    )
```

```python
import functools

import jax
import jax.numpy as jnp
from jax import lax
from jax.experimental import pallas as pl
from jax.experimental.pallas import tpu as pltpu
from jax.sharding import PartitionSpec as P

D = 1024
H = 8
HD = 128
FF = 4096
NS = 16
LEN = 4096
BLK = 512
CTX = 128
OWN = BLK - CTX
HALF = D // 2
SCALE = HD ** (-0.5)
AXES = ("dp", "mp")
f32 = jnp.float32
bf16 = jnp.bfloat16
VMEM = pl.BlockSpec(memory_space=pltpu.VMEM)
SMEM = pl.BlockSpec(memory_space=pltpu.SMEM)
ANY = pl.BlockSpec(memory_space=pltpu.HBM)
QKV_COLS = pl.BlockSpec((D, 3 * HALF), lambda i: (0, 0))
OUT_COLS = pl.BlockSpec((D, HALF), lambda i: (0, 3))
NT = (((1,), (1,)), ((), ()))
TN = (((0,), (0,)), ((), ()))


def params(mib):
    return pltpu.CompilerParams(vmem_limit_bytes=mib * 1024 * 1024)


def in_hbm(values):
    return pltpu.with_memory_space_constraint(values, pltpu.HBM)


def in_vmem(values):
    return pltpu.with_memory_space_constraint(values, pltpu.VMEM)


COST = pl.CostEstimate(flops=1, bytes_accessed=1, transcendentals=0)


def bits_of(n):
    return n.bit_length() - 1


def swap_bits(word, count):
    out = 0
    for i in range(count):
        out = out | (((word >> i) & 1) << (count - 1 - i))
    return out


class Links:
    def __init__(self):
        self.ndp = lax.axis_size("dp")
        self.nmp = lax.axis_size("mp")
        self.nz = self.nmp // 2
        self.dp = lax.axis_index("dp")
        self.mp = lax.axis_index("mp")
        self.z = self.mp // 2
        self.core = self.mp % 2
        self.dp_bits = bits_of(self.ndp)
        self.mp_bits = bits_of(self.nmp)

    def send(self, values, target):
        pairs = []
        for d in range(self.ndp):
            for m in range(self.nmp):
                to = target(d, m)
                if to is not None:
                    pairs.append((d * self.nmp + m, to[0] * self.nmp + to[1]))
        return lax.ppermute(values, AXES, pairs)

    def mp_swap(self, values, bit):
        return self.send(values, lambda d, m: (d, m ^ (1 << bit)))

    def dp_swap(self, values, bit):
        return self.send(values, lambda d, m: (d ^ (1 << bit), m))

    def core_swap(self, values):
        return self.mp_swap(values, 0)

    def fan(self, values, level):
        other = self.dp_bits - 1 - level
        return self.send(
            values, lambda d, m: (d ^ (1 << (other if m % 2 else level)), m)
        )

    def block_at(self, position):
        mirrored = swap_bits(position, self.dp_bits)
        return self.dp ^ jnp.where(self.core == 0, mirrored, position)

    def window_shift(self, values, step):
        per = LEN // BLK

        def target(d, m):
            inside = m % per + step
            return (d, m + step) if 0 <= inside < per else None

        return self.send(values, target)


def by_core(links, first, second, axis):
    return jnp.where(
        links.core == 0,
        jnp.concatenate([first, second], axis),
        jnp.concatenate([second, first], axis),
    )


def spread_rows(src_ref, dst_ref, rows, start=0):
    for r in range(0, rows, 16):
        block = src_ref[start + r : start + r + 16, :].astype(f32)
        for j in range(8):
            dst_ref[r : r + 16, j, :] = block[:, j * 128 : (j + 1) * 128]


def gather_rows(src_ref, dst_ref, rows):
    for r in range(0, rows, 16):
        for j in range(8):
            dst_ref[r : r + 16, j * 128 : (j + 1) * 128] = src_ref[r : r + 16, j, :].astype(
                dst_ref.dtype
            )


def move_on(state, rate, steps):
    far = jnp.exp(-rate * steps)
    near = jnp.exp(-rate * (steps - 1.0)) * steps
    return far * state[0], far * state[1] + near * state[0]


def scan_rows(xs, rows, decay):
    zero = jnp.zeros((NS, 8, 128), f32)

    def step(i, carry):
        u, v = carry
        for k in range(8):
            v = decay * v + u
            u = decay * u + xs[i * 8 + k][None]
        return u, v

    return lax.fori_loop(0, rows // 8, step, (zero, zero))


def scan_own_kernel(x_ref, rate_ref, out_ref, xs):
    spread_rows(x_ref, xs, OWN)
    u, v = scan_rows(xs, OWN, jnp.exp(-rate_ref[...]))
    out_ref[0] = u
    out_ref[1] = v


def scan_tail_kernel(x_ref, own_ref, rate_ref, out_ref, xs):
    spread_rows(x_ref, xs, CTX)
    state = scan_rows(xs, CTX, jnp.exp(-rate_ref[...]))
    u, v = move_on(state, rate_ref[...], float(OWN))
    out_ref[0] = u + own_ref[0]
    out_ref[1] = v + own_ref[1]


STATE = jax.ShapeDtypeStruct((2, NS, 8, 128), f32)


def scan_own(values, rate):
    return pl.pallas_call(
        scan_own_kernel,
        out_shape=STATE,
        in_specs=[VMEM, VMEM],
        out_specs=VMEM,
        scratch_shapes=[pltpu.VMEM((OWN, 8, 128), f32)],
        compiler_params=params(6),
        cost_estimate=COST,
        name="scan_own",
    )(values, rate)


def scan_tail(values, own, rate):
    return pl.pallas_call(
        scan_tail_kernel,
        out_shape=STATE,
        in_specs=[VMEM] * 3,
        out_specs=VMEM,
        scratch_shapes=[pltpu.VMEM((CTX, 8, 128), f32)],
        compiler_params=params(4),
        cost_estimate=COST,
        name="scan_tail",
    )(values, own, rate)


def exchange_kernel(scal, total_ref, recv_ref, before_ref, rate_ref, total_out, before_out):
    mine, inside, span = scal[0], scal[1], scal[2]
    rate = rate_ref[...]
    recv = (recv_ref[0], recv_ref[1])
    total = (total_ref[0], total_ref[1])
    moved = move_on(recv, rate, inside)
    low = tuple(mine * r + (1.0 - mine) * t for r, t in zip(recv, total))
    high = tuple(mine * t + (1.0 - mine) * r for r, t in zip(recv, total))
    far = move_on(low, rate, span)
    for i in range(2):
        before_out[i] = before_ref[i] + mine * moved[i]
        total_out[i] = far[i] + high[i]


def exchange_step(scal, total, received, before, rate):
    return pl.pallas_call(
        exchange_kernel,
        out_shape=(STATE, STATE),
        in_specs=[SMEM] + [VMEM] * 4,
        out_specs=(VMEM, VMEM),
        compiler_params=params(3),
        cost_estimate=COST,
        name="exchange_step",
    )(scal, total, received, before, rate)


def exchange_back_kernel(scal, total_ref, recv_ref, after_ref, rate_ref, total_out, after_out):
    mine, inside, span = scal[0], scal[1], scal[2]
    rate = rate_ref[...]
    recv, total = recv_ref[...], total_ref[...]
    after_out[...] = after_ref[...] + (1.0 - mine) * (jnp.exp(-rate * inside) * recv)
    low = mine * recv + (1.0 - mine) * total
    high = mine * total + (1.0 - mine) * recv
    total_out[...] = low + jnp.exp(-rate * span) * high


def exchange_back_step(scal, total, received, after, rate):
    one = jax.ShapeDtypeStruct((NS, 8, 128), f32)
    return pl.pallas_call(
        exchange_back_kernel,
        out_shape=(one, one),
        in_specs=[SMEM] + [VMEM] * 4,
        out_specs=(VMEM, VMEM),
        compiler_params=params(3),
        cost_estimate=COST,
        name="exchange_back_step",
    )(scal, total, received, after, rate)


def context_kernel(
    scal, x_ref, own_ref, before_ref, initial_ref, rate_ref, in_ref, out_map_ref, out_ref, xs, ys
):
    out_ref[CTX:, :] = own_ref[...]
    spread_rows(x_ref, xs, CTX)
    rate = rate_ref[...]
    decay = jnp.exp(-rate)
    weight = in_ref[...] * out_map_ref[...]
    carried = jnp.exp(-rate * scal[0]) * initial_ref[...] * scal[1]
    start = out_map_ref[...] * (in_ref[...] * before_ref[0] + carried)

    def step(i, y):
        for k in range(8):
            y = decay * y + weight * xs[i * 8 + k][None]
            ys[i * 8 + k] = jnp.sum(y, axis=0)
        return y

    lax.fori_loop(0, CTX // 8, step, start)
    gather_rows(ys, out_ref, CTX)


def context_states(scal, tail, own, before, initial, rate, gain_in, gain_out):
    return pl.pallas_call(
        context_kernel,
        out_shape=jax.ShapeDtypeStruct((CTX + BLK, D), bf16),
        in_specs=[SMEM] + [VMEM] * 7,
        out_specs=VMEM,
        scratch_shapes=[pltpu.VMEM((CTX, 8, 128), f32)] * 2,
        compiler_params=params(6),
        cost_estimate=COST,
        name="context_states",
    )(scal, tail, own, before, initial, rate, gain_in, gain_out)


def state_low_kernel(g_ref, rate_ref, out_ref, gs):
    spread_rows(g_ref, gs, CTX)
    decay = jnp.exp(-rate_ref[...])
    zero = jnp.zeros((NS, 8, 128), f32)

    def back(i, carry):
        low, slope = carry
        for k in range(8):
            slope = decay * slope + low
            low = decay * low + gs[CTX - 1 - (i * 8 + k)][None]
        return low, slope

    low, slope = lax.fori_loop(0, CTX // 8, back, (zero, zero))
    out_ref[0] = low
    out_ref[1] = slope


def state_low(grad_context, rate):
    return pl.pallas_call(
        state_low_kernel,
        out_shape=jax.ShapeDtypeStruct((2, NS, 8, 128), f32),
        in_specs=[VMEM] * 2,
        out_specs=VMEM,
        scratch_shapes=[pltpu.VMEM((CTX, 8, 128), f32)],
        compiler_params=params(3),
        cost_estimate=COST,
        name="state_low",
    )(grad_context, rate)


def state_sums_kernel(
    scal, g_ref, x_ref, start_ref, lows_ref, initial_ref, rate_ref, in_ref, out_map_ref, out_ref,
    gs, xs,
):
    spread_rows(g_ref, gs, CTX)
    spread_rows(x_ref, xs, CTX)
    part = NS // 2
    for n in range(0, NS, part):
        span = slice(n, n + part)
        rate = rate_ref[span]
        decay = jnp.exp(-rate)
        zero = jnp.zeros((part, 8, 128), f32)

        def step(i, carry):
            u, v, su, sv = carry
            for k in range(4):
                v = decay * v + u
                u = decay * u + xs[i * 4 + k][None]
                g = gs[i * 4 + k][None]
                su = su + g * u
                sv = sv + g * v
            return u, v, su, sv

        _, _, su, sv = lax.fori_loop(
            0, CTX // 4, step, (start_ref[0, span], start_ref[1, span], zero, zero)
        )
        far = jnp.exp(-rate * scal[0])
        low, slope = lows_ref[0, span], lows_ref[1, span]
        sum_init = far * decay * low
        sum_slope = far * ((scal[0] + 1.0) * low + decay * slope)
        initial = initial_ref[span] * scal[1]
        gain_in, gain_out = in_ref[span], out_map_ref[span]
        out_ref[0, span] = -decay * gain_out * (gain_in * sv + initial * sum_slope)
        out_ref[1, span] = gain_out * su
        out_ref[2, span] = gain_in * su + initial * sum_init
        out_ref[3, span] = gain_out * sum_init * scal[1]


def state_sums(scal, grad_context, tail, start, lows, initial, rate, gain_in, gain_out):
    return pl.pallas_call(
        state_sums_kernel,
        out_shape=jax.ShapeDtypeStruct((4, NS, 8, 128), f32),
        in_specs=[SMEM] + [VMEM] * 8,
        out_specs=VMEM,
        scratch_shapes=[pltpu.VMEM((CTX, 8, 128), f32)] * 2,
        compiler_params=params(4),
        cost_estimate=COST,
        name="state_sums",
    )(scal, grad_context, tail, start, lows, initial, rate, gain_in, gain_out)


def sent_tail_kernel(g_ref, after_ref, rate_ref, in_ref, out_map_ref, out_ref, gs, ys):
    spread_rows(g_ref, gs, CTX)
    rate = rate_ref[...]
    decay = jnp.exp(-rate)
    weight = in_ref[...] * out_map_ref[...]
    start = jnp.exp(-rate * float(OWN)) * weight * after_ref[...]

    def back(i, y):
        for k in range(8):
            t = CTX - 1 - (i * 8 + k)
            y = decay * y + weight * gs[t][None]
            ys[t] = jnp.sum(y, axis=0)
        return y

    lax.fori_loop(0, CTX // 8, back, start)
    gather_rows(ys, out_ref, CTX)


def sent_tail(grad_context, after, rate, gain_in, gain_out):
    return pl.pallas_call(
        sent_tail_kernel,
        out_shape=jax.ShapeDtypeStruct((CTX, D), bf16),
        in_specs=[VMEM] * 5,
        out_specs=VMEM,
        scratch_shapes=[pltpu.VMEM((CTX, 8, 128), f32)] * 2,
        compiler_params=params(4),
        cost_estimate=COST,
        name="sent_tail",
    )(grad_context, after, rate, gain_in, gain_out)


def sent_own_kernel(after_ref, rate_ref, in_ref, out_map_ref, out_ref, ys):
    decay = jnp.exp(-rate_ref[...])

    def back(i, y):
        for k in range(8):
            y = decay * y
            ys[OWN - 1 - (i * 8 + k)] = jnp.sum(y, axis=0)
        return y

    lax.fori_loop(0, OWN // 8, back, in_ref[...] * out_map_ref[...] * after_ref[...])
    gather_rows(ys, out_ref, OWN)


def sent_own(after, rate, gain_in, gain_out):
    return pl.pallas_call(
        sent_own_kernel,
        out_shape=jax.ShapeDtypeStruct((OWN, D), bf16),
        in_specs=[VMEM] * 4,
        out_specs=VMEM,
        scratch_shapes=[pltpu.VMEM((OWN, 8, 128), f32)],
        compiler_params=params(6),
        cost_estimate=COST,
        name="sent_own",
    )(after, rate, gain_in, gain_out)


def attention_mask(keys, queries, first_query, opened):
    row = lax.broadcasted_iota(jnp.int32, (keys, queries), 0)
    col = lax.broadcasted_iota(jnp.int32, (keys, queries), 1) + first_query
    return jnp.where(row < CTX, (1 - opened) * BLK, row - CTX) <= col


def head_parts(ref, offset):
    q = ref[CTX:, pl.ds(offset, HD)]
    k = ref[:, pl.ds(HALF + offset, HD)]
    v = ref[:, pl.ds(2 * HALF + offset, HD)]
    return q, k, v


def probabilities(k, q, first_query, opened):
    scores = lax.dot_general(k, q, NT, preferred_element_type=f32) * SCALE
    scores = jnp.where(
        attention_mask(k.shape[0], q.shape[0], first_query, opened), scores, -jnp.inf
    )
    lifted = jnp.exp(scores - jnp.max(scores, axis=0, keepdims=True))
    return lifted * (1.0 / jnp.sum(lifted, axis=0, keepdims=True))


QT = BLK // 2


def attend_kernel(info, own_ref, other_ref, out_ref):
    opened = info[1]

    @pl.loop(0, H // 2)
    def _(h):
        offset = pl.multiple_of(h * HD, HD)
        for side, qkv in enumerate((own_ref, other_ref)):
            q, k, v = head_parts(qkv, offset)
            v_t = v.T
            home = pl.multiple_of((side ^ info[0]) * HALF + h * HD, HD)
            for first in range(0, BLK, QT):
                keys = CTX + first + QT
                p = probabilities(k[:keys], q[first : first + QT], first, opened).astype(bf16)
                mixed = jnp.dot(v_t[:, :keys], p, preferred_element_type=f32)
                out_ref[first : first + QT, pl.ds(home, HD)] = mixed.T.astype(bf16)


def attend(info, own, other):
    return pl.pallas_call(
        attend_kernel,
        out_shape=jax.ShapeDtypeStruct((BLK, D), bf16),
        in_specs=[SMEM] + [VMEM] * 2,
        out_specs=VMEM,
        compiler_params=params(14),
        cost_estimate=COST,
        name="attend",
    )(info, own, other)


def attend_back_kernel(
    info, own_ref, other_ref, grad_ref, g_own_ref, g_other_ref, acc
):
    opened = info[1]
    sides = ((own_ref, g_own_ref), (other_ref, g_other_ref))
    for _, g in sides:
        g[:CTX, :HALF] = jnp.zeros((CTX, HALF), bf16)

    @pl.loop(0, H // 2)
    def _(h):
        offset = pl.multiple_of(h * HD, HD)
        for side, (qkv, g) in enumerate(sides):
            q, k, v = head_parts(qkv, offset)
            k_t = k.T
            home = pl.multiple_of((side ^ info[0]) * HALF + h * HD, HD)
            for first in range(0, BLK, QT):
                keys = CTX + first + QT
                q_now = q[first : first + QT]
                go = grad_ref[first : first + QT, pl.ds(home, HD)]
                p = probabilities(k[:keys], q_now, first, opened)
                gp = lax.dot_general(v[:keys], go, NT, preferred_element_type=f32)
                mean = jnp.sum(p * gp, axis=0, keepdims=True)
                gs = (p * (gp - mean)).astype(bf16)
                gq_t = jnp.dot(k_t[:, :keys], gs, preferred_element_type=f32) * SCALE
                g[CTX + first : CTX + first + QT, pl.ds(offset, HD)] = gq_t.T.astype(bf16)
                gk = jnp.dot(gs, q_now, preferred_element_type=f32)
                gv = jnp.dot(p.astype(bf16), go, preferred_element_type=f32)
                if first == 0:
                    acc[0, :keys] = gk
                    acc[1, :keys] = gv
                else:
                    early = CTX + QT
                    gk_all = jnp.concatenate([gk[:early] + acc[0, :early], gk[early:]], 0)
                    gv_all = jnp.concatenate([gv[:early] + acc[1, :early], gv[early:]], 0)
                    g[:, pl.ds(HALF + offset, HD)] = (gk_all * SCALE).astype(bf16)
                    g[:, pl.ds(2 * HALF + offset, HD)] = gv_all.astype(bf16)


def attend_back(info, own, other, grad):
    out = jax.ShapeDtypeStruct((CTX + BLK, 3 * HALF), bf16)
    return pl.pallas_call(
        attend_back_kernel,
        out_shape=(out, out),
        in_specs=[SMEM] + [VMEM] * 3,
        out_specs=(VMEM, VMEM),
        scratch_shapes=[pltpu.VMEM((2, CTX + QT, HD), f32)],
        compiler_params=params(18),
        cost_estimate=COST,
        name="attend_back",
    )(info, own, other, grad)


def gelu_parts(x):
    cdf = 0.5 * (1.0 + lax.erf(x * 0.7071067811865476))
    slope = cdf + x * (jnp.exp(-0.5 * x * x) * 0.3989422804014327)
    return x * cdf, slope


def feed_kernel(
    ndp, nz, width, index, groups, earlier, last, info, s_own, s_par, c_own, c_par,
    st_own, st_par, ct_own, ct_par, *rest
):
    rows = s_own.shape[0]
    block = D // ndp
    group = nz * width
    half = ndp // 2
    s, c = (s_own, s_par), (c_own, c_par)
    count = ndp if index else 1
    weights, rest = rest[:count], rest[count:]
    if earlier:
        m_in, g_in, *rest = rest
    if last:
        m_own, m_par, g_own, g_par, *rest = rest
    else:
        m_out, g_out, *rest = rest
    parts, (st, ct, w, act, gh, sems) = rest[:4], rest[4:]
    at = [pl.multiple_of(info[p] * block, block) for p in range(ndp)]
    z = info[ndp]
    copies = []

    def start(src, dst):
        copy = pltpu.make_async_copy(src, dst, sems.at[len(copies)])
        copy.start()
        copies.append(copy)

    if index:
        for p in range(ndp):
            start(weights[p], w.at[pl.ds(at[p], block), :])
    else:
        at_core = pl.multiple_of(info[ndp + 1] * 2 * group, 128)
        start(weights[0].at[:, pl.ds(at_core, 2 * group)], w)
    for own, par, dst in ((st_own, st_par, st), (ct_own, ct_par, ct)):
        for p in range(ndp):
            for i, src in enumerate((own, par)):
                start(
                    src.at[pl.ds(at[p], block), :],
                    dst.at[p * block : (p + 1) * block, i * rows : (i + 1) * rows],
                )
    for copy in copies[:count]:
        copy.wait()

    @pl.loop(0, nz)
    def _(b):
        up = pl.ds(pl.multiple_of(b * width, width), width)
        down = pl.ds(pl.multiple_of(group + b * width, width), width)
        for i in range(2):
            part = slice(i * rows, (i + 1) * rows)
            hidden = jnp.dot(s[i][...], w[:, up], preferred_element_type=f32)
            grad = jnp.dot(c[i][...], w[:, down], preferred_element_type=f32)
            active, slope = gelu_parts(hidden)
            act[part, up] = active.astype(bf16)
            gh[part, up] = (grad * slope).astype(bf16)

    for copy in copies[count:]:
        copy.wait()

    @pl.loop(0, nz)
    def _(r):
        cols = pl.ds(pl.multiple_of((z ^ swap_bits(r, bits_of(nz))) * width, width), width)
        for part in range(2):
            span = slice(part * half * block, (part + 1) * half * block)
            up = jnp.dot(st[span, :], gh[:, cols], preferred_element_type=f32).astype(bf16)
            down = jnp.dot(ct[span, :], act[:, cols], preferred_element_type=f32).astype(bf16)
            for p in range(half):
                far = p >= half // 2
                dst = parts[2 * part + far]
                q = p - far * (half // 2)
                dst[q, r, 0] = up[p * block : (p + 1) * block]
                dst[q, r, 1] = down[p * block : (p + 1) * block]

    for name, left, first in (("g", gh, 0), ("m", act, group)):
        for p in range(ndp):
            right = w[p * block : (p + 1) * block, first : first + group]
            cols = slice(p * block, (p + 1) * block)
            for i in range(2):
                part = slice(i * rows, (i + 1) * rows)
                value = lax.dot_general(left[part, :], right, NT, preferred_element_type=f32)
                if earlier:
                    value = value + (g_in if name == "g" else m_in)[part, cols]
                if not last:
                    (g_out if name == "g" else m_out)[part, cols] = value
                elif i == 0:
                    (g_own if name == "g" else m_own)[:, cols] = value
                else:
                    (g_par if name == "g" else m_par)[:, cols] = value.astype(bf16)


def feed(links, info, acts, weights, group, index, groups, earlier, last):
    ndp, nz = links.ndp, links.nz
    rows = acts[0].shape[0]
    tokens = 2 * rows
    block = D // ndp
    width = group // nz
    half = ndp // 2
    full = pltpu.VMEM((tokens, D), f32)
    own = jax.ShapeDtypeStruct((rows, D), f32)
    par = jax.ShapeDtypeStruct((rows, D), bf16)
    grads = tuple(
        jax.ShapeDtypeStruct((count, nz, 2, block, width), bf16)
        for count in (half // 2, half - half // 2) * 2
    )
    out_shape = (own, par, own, par, *grads) if last else (full, full, *grads)
    earlier = tuple(earlier) if earlier else ()
    return pl.pallas_call(
        functools.partial(feed_kernel, ndp, nz, width, index, groups, bool(earlier), last),
        out_shape=out_shape,
        in_specs=[SMEM] + [VMEM] * len(acts) + [ANY] * len(weights) + [VMEM] * len(earlier),
        out_specs=(VMEM,) * len(out_shape),
        scratch_shapes=[
            pltpu.VMEM((D, tokens), bf16),
            pltpu.VMEM((D, tokens), bf16),
            pltpu.VMEM((D, 2 * group), bf16),
            pltpu.VMEM((tokens, group), bf16),
            pltpu.VMEM((tokens, group), bf16),
            pltpu.SemaphoreType.DMA((5 * ndp,)),
        ],
        compiler_params=params(30),
        cost_estimate=COST,
        name="feed_last" if last else "feed_first",
    )(info, *map(in_vmem, acts), *map(in_hbm, weights), *map(in_vmem, earlier))


def norm_parts(values):
    center = values - jnp.mean(values, axis=-1, keepdims=True)
    spread = jnp.mean(center * center, axis=-1, keepdims=True)
    inverse = lax.rsqrt(spread + 1e-05)
    return center * inverse, inverse


def norm_back(grad, unit, inverse, gain):
    scaled = grad * gain
    return (
        scaled
        - jnp.mean(scaled, axis=-1, keepdims=True)
        - unit * jnp.mean(scaled * unit, axis=-1, keepdims=True)
    ) * inverse


def dot(left, right):
    return jnp.dot(left, right, preferred_element_type=f32)


def dot_nt(left, right):
    return lax.dot_general(left, right, NT, preferred_element_type=f32)


ROWS = 128


def norm_kernel(x_ref, gain_ref, out_ref, tail_ref):
    for r in range(0, x_ref.shape[0], ROWS):
        unit, _ = norm_parts(x_ref[r : r + ROWS, :].astype(f32))
        out_ref[r : r + ROWS, :] = (unit * gain_ref[...]).astype(bf16)
    tail_ref[...] = out_ref[OWN:, :]


def norm_first(tokens, gain):
    return pl.pallas_call(
        norm_kernel,
        out_shape=(
            jax.ShapeDtypeStruct(tokens.shape, bf16),
            jax.ShapeDtypeStruct((CTX, D), bf16),
        ),
        in_specs=[VMEM] * 2,
        out_specs=(VMEM, VMEM),
        compiler_params=params(5),
        cost_estimate=COST,
        name="norm_first",
    )(tokens, gain)


def middle_kernel(
    info, att_ref, tok_ref, o_own, o_other, gain_ref, mid_ref, second_ref, second_t_ref
):
    att = att_ref[...]
    for side, weight in enumerate((o_own, o_other)):
        cols = pl.ds(pl.multiple_of((side ^ info[0]) * HALF, HALF), HALF)
        mid_ref[:, cols] = tok_ref[:, cols].astype(f32) + dot(att, weight[...])
    for r in range(0, att_ref.shape[0], ROWS):
        unit, _ = norm_parts(mid_ref[r : r + ROWS, :])
        second = unit * gain_ref[...]
        second_ref[r : r + ROWS, :] = second.astype(bf16)
        second_t_ref[:, r : r + ROWS] = second.T.astype(bf16)


def middle_norm(info, attended, tokens, o_own, o_other, gain):
    rows = tokens.shape[0]
    return pl.pallas_call(
        middle_kernel,
        out_shape=(
            jax.ShapeDtypeStruct((rows, D), f32),
            pltpu.VMEM((rows, D), bf16),
            pltpu.VMEM((D, rows), bf16),
        ),
        grid=(1,),
        in_specs=[SMEM, VMEM, VMEM, OUT_COLS, OUT_COLS, VMEM],
        out_specs=(VMEM,) * 3,
        compiler_params=params(16),
        cost_estimate=COST,
        name="middle_norm",
    )(info, attended, tokens, in_hbm(o_own), in_hbm(o_other), gain)


def back_middle_kernel(
    info, mid_ref, own_ref, recv_ref, cot_ref, gain_ref, o_own, o_other,
    grad_ref, b_own_ref, b_other_ref, att_ref, gain_grad_ref, branch,
):
    total = jnp.zeros((1, D), f32)
    for r in range(0, mid_ref.shape[0], ROWS):
        span = slice(r, r + ROWS)
        unit, inverse = norm_parts(mid_ref[span, :])
        grad = own_ref[span, :] + recv_ref[span, :].astype(f32)
        total = total + jnp.sum(grad * unit, axis=0, keepdims=True)
        back = cot_ref[span, :].astype(f32) + norm_back(grad, unit, inverse, gain_ref[...])
        grad_ref[span, :] = back
        branch[span, :] = back.astype(bf16)
    gain_grad_ref[...] = total
    for side, out in enumerate((b_own_ref, b_other_ref)):
        out[...] = branch[:, pl.ds(pl.multiple_of((side ^ info[0]) * HALF, HALF), HALF)]
    att = dot_nt(b_own_ref[...], o_own[...]) + dot_nt(b_other_ref[...], o_other[...])
    att_ref[...] = att.astype(bf16)


def back_middle(info, middle, own, received, cotangent, gain, o_own, o_other):
    rows = middle.shape[0]
    part = jax.ShapeDtypeStruct((rows, HALF), bf16)
    return pl.pallas_call(
        back_middle_kernel,
        out_shape=(
            jax.ShapeDtypeStruct((rows, D), f32),
            part,
            part,
            jax.ShapeDtypeStruct((rows, D), bf16),
            jax.ShapeDtypeStruct((1, D), f32),
        ),
        grid=(1,),
        in_specs=[SMEM] + [VMEM] * 5 + [OUT_COLS] * 2,
        out_specs=(VMEM,) * 5,
        scratch_shapes=[pltpu.VMEM((rows, D), bf16)],
        compiler_params=params(30),
        cost_estimate=COST,
        name="back_middle",
    )(info, middle, own, received, cotangent, gain, in_hbm(o_own), in_hbm(o_other))


def project_kernel(x_ref, w_ref, out_ref):
    for first in range(0, 3 * HALF, HALF):
        cols = slice(first, first + HALF)
        out_ref[:, cols] = dot(x_ref[...], w_ref[:, cols]).astype(bf16)


def project(values, weights):
    return pl.pallas_call(
        project_kernel,
        out_shape=jax.ShapeDtypeStruct((values.shape[0], 3 * HALF), bf16),
        grid=(1,),
        in_specs=[VMEM, QKV_COLS],
        out_specs=VMEM,
        compiler_params=params(16),
        cost_estimate=COST,
        name="project",
    )(values, in_hbm(weights))


def back_project_kernel(first, g_own, g_other, w_own, w_other, out_ref):
    rows = slice(first, first + out_ref.shape[0])
    for at in range(0, D, HALF):
        cols = slice(at, at + HALF)
        value = dot_nt(g_own[rows, :], w_own[cols, :]) + dot_nt(g_other[rows, :], w_other[cols, :])
        out_ref[:, cols] = value.astype(out_ref.dtype)


def back_project(g_own, g_other, w_own, w_other, first, rows, dtype):
    return pl.pallas_call(
        functools.partial(back_project_kernel, first),
        out_shape=jax.ShapeDtypeStruct((rows, D), dtype),
        grid=(1,),
        in_specs=[VMEM, VMEM, QKV_COLS, QKV_COLS],
        out_specs=VMEM,
        compiler_params=params(26),
        cost_estimate=COST,
        name="back_project",
    )(g_own, g_other, in_hbm(w_own), in_hbm(w_other))


def back_first_kernel(
    tok_ref, part_ref, sent_ref, last_ref, mid_ref, gain_ref, out_ref, gain_grad_ref
):
    total = jnp.zeros((1, D), f32)
    for r in range(0, tok_ref.shape[0], ROWS):
        span = slice(r, r + ROWS)
        unit, inverse = norm_parts(tok_ref[span, :].astype(f32))
        sent = sent_ref[span, :] if r < OWN else last_ref[r - OWN : r - OWN + ROWS, :]
        grad = part_ref[span, :] + sent.astype(f32)
        total = total + jnp.sum(grad * unit, axis=0, keepdims=True)
        back = mid_ref[span, :] + norm_back(grad, unit, inverse, gain_ref[...])
        out_ref[span, :] = back.astype(bf16)
    gain_grad_ref[...] = total


def back_first(tokens, part, sent, last, grad_middle, gain):
    return pl.pallas_call(
        back_first_kernel,
        out_shape=(
            jax.ShapeDtypeStruct(tokens.shape, bf16),
            jax.ShapeDtypeStruct((1, D), f32),
        ),
        in_specs=[VMEM] * 6,
        out_specs=(VMEM,) * 2,
        compiler_params=params(14),
        cost_estimate=COST,
        name="back_first",
    )(tokens, part, sent, last, grad_middle, gain)


def weight_grad_kernel(
    ndp, nz, info, x_own, x_par, g_own, g_par, a_own, a_par, b_own, b_par, shares,
    keep_ref, send_ref,
):
    block = D // ndp
    rows = block // nz
    z = info[ndp]
    half = ndp // 2
    for p in range(ndp):
        cols = pl.ds(pl.multiple_of(info[p] * block, block), block)
        grad = dot(x_own[:, cols].T, g_own[...]) + dot(x_par[:, cols].T, g_par[...])
        out = dot(a_own[:, cols].T, b_own[...]) + dot(a_par[:, cols].T, b_par[...])
        grad = grad.astype(bf16)
        out = out.astype(bf16)
        dst = keep_ref if p < half else send_ref
        for b in range(nz):
            r = swap_bits(z ^ b, bits_of(nz))
            span = slice(b * rows, (b + 1) * rows)
            dst[p % half, r, :, : 3 * HALF] = grad[span]
            dst[p % half, r, :, 3 * HALF : 4 * HALF] = out[span]
            dst[p % half, r, :, 4 * HALF :] = shares[p, r]


def weight_grads(links, info, x_own, x_par, g_own, g_par, a_own, a_par, b_own, b_par, shares):
    ndp, nz = links.ndp, links.nz
    line = 4 * HALF + shares.shape[3]
    out = jax.ShapeDtypeStruct((ndp // 2, nz, D // (ndp * nz), line), bf16)
    return pl.pallas_call(
        functools.partial(weight_grad_kernel, ndp, nz),
        out_shape=(out, out),
        in_specs=[SMEM] + [VMEM] * 9,
        out_specs=(VMEM, VMEM),
        compiler_params=params(24),
        cost_estimate=COST,
        name="weight_grads",
    )(info, x_own, x_par, g_own, g_par, a_own, a_par, b_own, b_par, shares)


def shares_kernel(ndp, nmp, maps, info, owner, sums_ref, gain_ref, out):
    for p in range(ndp):
        d = info[p]
        mine = (owner[0] == d).astype(f32)
        for m in range(nmp):
            r = swap_bits(info[ndp] ^ (m // 2), bits_of(nmp // 2))
            other = (m % 2) ^ info[ndp + 1]
            place_of = jnp.where(other == 0, p, swap_bits(p, bits_of(ndp)))
            to = out.at[other, place_of, r]
            for i in range(3):
                rows = sums_ref[i, pl.ds(d * maps, maps), m, :]
                to[i * maps : (i + 1) * maps, :] = rows
            to[3 * maps : 3 * maps + NS, :] = sums_ref[3, :, m, :] * mine
            to[3 * maps + NS :, :] = jnp.zeros((to.shape[0] - 3 * maps - NS, 128), f32)
            to[3 * maps + NS : 3 * maps + NS + 1, :] = gain_ref[pl.ds(d, 1), m, :]


def pack_shares(links, info, owner, sums, gain, maps, lines):
    out = jax.ShapeDtypeStruct((2, links.ndp, links.nz, lines, 128), f32)
    return pl.pallas_call(
        functools.partial(shares_kernel, links.ndp, links.nmp, maps),
        out_shape=out,
        in_specs=[SMEM, SMEM, VMEM, VMEM],
        out_specs=VMEM,
        compiler_params=params(3),
        cost_estimate=COST,
        name="pack_shares",
    )(info, owner, sums, gain)


def prepare_kernel(
    nz, groups, core, q_ref, k_ref, v_ref, o_ref, up_ref, down_ref, keep, send, feed, *late
):
    for i, ref in enumerate((q_ref, k_ref, v_ref, o_ref)):
        to = slice(i * HALF, (i + 1) * HALF)
        keep[:, to] = ref[:, pl.ds(pl.multiple_of(core[0] * HALF, HALF), HALF)].astype(bf16)
        send[:, to] = ref[:, pl.ds(pl.multiple_of((1 - core[0]) * HALF, HALF), HALF)].astype(bf16)
    width = FF // (2 * nz * groups)
    at = 0
    for c in range(2):
        for ref in (up_ref, down_ref):
            for b in range(nz):
                first = (b * 2 + c) * groups * width
                feed[:, at : at + width] = ref[:, first : first + width].astype(bf16)
                at += width
    for i, out in enumerate(late):
        at = 0
        for ref in (up_ref, down_ref):
            for b in range(nz):
                first = ((b * 2 + (core[0] ^ i)) * groups + 1) * width
                span = pl.ds(pl.multiple_of(first, width), width)
                out[:, at : at + width] = ref[:, span].astype(bf16)
                at += width


def prepare(links, groups, core, mats, up, down):
    rows = up.shape[0]
    part = jax.ShapeDtypeStruct((rows, 4 * HALF), bf16)
    late = (jax.ShapeDtypeStruct((rows, FF // 2), bf16),) * 2 if groups > 1 else ()
    return pl.pallas_call(
        functools.partial(prepare_kernel, links.nz, groups),
        out_shape=(part, part, jax.ShapeDtypeStruct((rows, 2 * FF // groups), bf16), *late),
        in_specs=[SMEM] + [VMEM] * 6,
        out_specs=(VMEM,) * (3 + len(late)),
        compiler_params=params(5),
        cost_estimate=COST,
        name="prepare",
    )(core, *(in_hbm(values) for values in (*mats, up, down)))


def place_kernel(ndp, order, *refs):
    out = refs[ndp]
    b = pl.program_id(0)
    for p in range(ndp):

        @pl.when(order[b] == p)
        def _(p=p):
            out[...] = refs[p][...]


def place(links, order, pieces):
    block, cols = pieces[0].shape
    ndp = links.ndp
    return pl.pallas_call(
        functools.partial(place_kernel, ndp),
        out_shape=pltpu.HBM((ndp * block, cols), pieces[0].dtype),
        grid_spec=pltpu.PrefetchScalarGridSpec(
            num_scalar_prefetch=1,
            grid=(ndp,),
            in_specs=[VMEM] * ndp,
            out_specs=pl.BlockSpec((block, cols), lambda b, order: (b, 0)),
        ),
        compiler_params=params(12),
        cost_estimate=COST,
        name="place",
    )(order, *pieces)


def add_b(left, right):
    return (left.astype(f32) + right.astype(f32)).astype(bf16)


def in_order(links, values, core):
    ndp, nz = values.shape[:2]
    inner = values.shape[2:]
    bits = links.dp_bits + links.mp_bits - 1
    split = values.reshape((2,) * bits + inner)
    for axis in range(links.dp_bits):
        mine = (links.dp >> (links.dp_bits - 1 - axis)) & 1
        split = jnp.where(mine == 0, split, jnp.flip(split, axis))
    for axis in range(links.dp_bits, bits):
        mine = (links.z >> (bits - 1 - axis)) & 1
        split = jnp.where(mine == 0, split, jnp.flip(split, axis))
    dp_axes, z_axes = list(range(links.dp_bits)), list(range(links.dp_bits, bits))
    rest = list(range(bits, split.ndim))
    split = split.transpose((dp_axes if core else dp_axes[::-1]) + z_axes[::-1] + rest)
    return split.reshape(values.shape)


def pack(pieces):
    sizes = [piece.size for piece in pieces]
    packed = jnp.concatenate([piece.reshape(-1) for piece in pieces])
    return jnp.pad(packed, (0, -packed.shape[0] % 128)).reshape(-1, 128), sizes


def merge_kernel(inner, bit, here_ref, there_ref, out):
    count = here_ref.shape[0]
    for i in range(count):
        if inner:
            at, other = 2 * i + bit[0], 2 * i + 1 - bit[0]
        else:
            at, other = bit[0] * count + i, (1 - bit[0]) * count + i
        out[at] = here_ref[i]
        out[other] = there_ref[i]


def merge(here, there, bit, inner):
    shape = (2 * here.shape[0], *here.shape[1:])
    return pl.pallas_call(
        functools.partial(merge_kernel, inner),
        out_shape=jax.ShapeDtypeStruct(shape, here.dtype),
        in_specs=[SMEM, VMEM, VMEM],
        out_specs=VMEM,
        compiler_params=params(6),
        cost_estimate=COST,
        name="merge",
    )(bit.astype(jnp.int32).reshape(1), here, there)


def join_small(links, current, received, index, bit):
    return merge(current, received, (index >> bit) & 1, False)


def pack_shares_plain(links, owner, row, banks_here, sums, gain, maps):
    ndp, nmp = links.ndp, links.nmp
    channels = gain.shape[2]

    def by_owner(values):
        values = values.reshape(ndp, maps, nmp, channels)
        return values.transpose(0, 2, 1, 3)

    bank = sums[3].reshape(NS, nmp, channels).transpose(1, 0, 2)
    here = jnp.arange(ndp * banks_here, dtype=jnp.int32) == owner * banks_here + row
    bank = jnp.where(here[:, None, None, None], bank[None], 0.0)
    bank = bank.reshape(ndp, banks_here, nmp, NS, channels).transpose(0, 2, 1, 3, 4)
    bank = bank.reshape(ndp, nmp, banks_here * NS, channels)
    lines = [by_owner(sums[0]), by_owner(sums[1]), by_owner(sums[2]), bank, gain[:, :, None]]
    shares = jnp.concatenate(lines, 2)
    rows = D // (ndp * links.nz)
    shares = shares.reshape(ndp, nmp, -1)
    shares = jnp.pad(shares, ((0, 0), (0, 0), (0, -shares.shape[2] % (128 * rows))))
    shares = shares.reshape(ndp, nmp // 2, 2, rows, -1)
    parts = [in_order(links, shares[:, :, c], c) for c in range(2)]
    return jnp.where(links.core == 0, jnp.stack(parts), jnp.stack(parts[::-1]))


class Live:
    pass


def fence(live, transfers=(), waits=()):
    held = dict(vars(live))
    tree = (held, [t.outgoing for t in transfers], [t.received for t in waits])
    leaves, form = jax.tree.flatten(tree)
    held, states, received = jax.tree.unflatten(form, lax.optimization_barrier(leaves))
    vars(live).update(held)
    for t, state in zip(transfers, states):
        t.outgoing = state
    for t, values in zip(waits, received):
        t.received = values
    for t in waits:
        t.join()


class Gather:
    def __init__(self, links, values):
        self.links = links
        self.state = [values[None]]
        self.kind = None

    def along_z(self, bit, first=0, last=None):
        self.kind, self.bit, self.span = "z", bit, slice(first, last)
        self.received = [self.links.mp_swap(piece, bit) for piece in self.state[self.span]]

    def along_dp(self, level):
        self.kind = "d"
        self.received = [self.links.fan(piece, level) for piece in self.state]

    def more_dp(self):
        self.count = 2 * len(self.state)
        self.ahead = [self.links.fan(piece, 0) for piece in self.state]
        self.received = self.received + self.ahead

    def last_dp(self, first, last):
        if first == 0:
            self.count = len(self.state)
        last = self.count if last is None else last
        self.kind = "d"
        self.received = [self.links.fan(piece, 0) for piece in self.state[first:last]]

    @property
    def outgoing(self):
        return self.state

    @outgoing.setter
    def outgoing(self, values):
        self.state = values

    def join(self):
        if self.kind == "d":
            self.state = self.state + self.received
        else:
            mine = (self.links.mp >> self.bit) & 1
            joined = [
                merge(piece, received, mine, True)
                for piece, received in zip(self.state[self.span], self.received)
            ]
            self.state = self.state[: self.span.start] + joined + (
                [] if self.span.stop is None else self.state[self.span.stop :]
            )
        self.received = None

    def first_z(self):
        for bit in reversed(range(2, self.links.mp_bits)):
            if self.received is not None:
                self.join()
            self.along_z(bit)

    def along_z_but_last(self, first, last):
        for bit in reversed(range(2, self.links.mp_bits)):
            if self.received is not None:
                self.join()
            self.along_z(bit, first, last)

    def first_dp(self):
        self.received = None
        for level in reversed(range(1, self.links.dp_bits)):
            if self.received is not None:
                self.join()
            self.along_dp(level)

    received = None

    def blocks(self):
        return [piece.reshape(-1, piece.shape[2]) for piece in self.state]


def add_kernel(axis, keep_ref, recv_ref, *outs):
    part = keep_ref.shape[axis] // len(outs)
    for i, out in enumerate(outs):
        span = (slice(None),) * axis + (slice(i * part, (i + 1) * part),)
        total = keep_ref[span].astype(f32) + recv_ref[span].astype(f32)
        out[...] = total.astype(out.dtype)


def mix_kernel(middle_ref, own_ref, recv_ref, out_ref):
    total = middle_ref[...] + (own_ref[...] + recv_ref[...].astype(f32))
    out_ref[...] = total.astype(bf16)


def mix(middle, own, received):
    return pl.pallas_call(
        mix_kernel,
        out_shape=jax.ShapeDtypeStruct(middle.shape, bf16),
        in_specs=[VMEM] * 3,
        out_specs=VMEM,
        compiler_params=params(10),
        cost_estimate=COST,
        name="mix",
    )(middle, own, received)


def add_split(keep, received, axis, dtype=None):
    shape = list(keep.shape)
    if axis is False:
        outs = (jax.ShapeDtypeStruct(shape, dtype or keep.dtype),)
    elif axis is None:
        outs = (jax.ShapeDtypeStruct(shape, f32),)
    else:
        shape[axis] //= 2
        outs = (jax.ShapeDtypeStruct(shape, keep.dtype),) * 2
    return pl.pallas_call(
        functools.partial(add_kernel, axis or 0),
        out_shape=outs,
        in_specs=[VMEM] * 2,
        out_specs=(VMEM,) * len(outs),
        compiler_params=params(10),
        cost_estimate=COST,
        name="add_split",
    )(keep, received)


class Scatter:
    def __init__(self, links, keep, send, *far):
        self.links = links
        self.state = [keep, send, *far]
        self.steps = [("d", level) for level in range(links.dp_bits)]
        self.steps += [("z", bit) for bit in range(1, links.mp_bits)]
        self.result = None

    def start(self):
        kind, index = self.steps[0]
        swap = self.links.mp_swap if kind == "z" else self.links.fan
        self.received = [swap(part, index) for part in self.state[1::2]]

    @property
    def outgoing(self):
        return self.state[1::2]

    @outgoing.setter
    def outgoing(self, values):
        self.state[1::2] = values

    def start_far(self):
        self.received = [self.links.fan(self.state.pop(), 0)]
        self.parts = "far"

    def start_near(self):
        self.received = [self.links.fan(self.state[1], 0)]
        self.parts = "near"

    parts = None

    def join(self):
        if self.parts == "far":
            self.parts = None
            keep_far = self.state.pop()
            self.state.append(add_split(keep_far, self.received[0], False)[0])
            return
        keep, received = self.state[0], self.received
        self.steps.pop(0)
        if self.parts == "near":
            self.parts = None
            received, far = lax.optimization_barrier((received[0], self.state[2]))
            self.state = [add_split(keep, received, False)[0], far]
        elif len(received) == 2:
            self.state = [
                add_split(keep, received[0], False)[0],
                add_split(self.state[2], received[1], False)[0],
            ]
        elif not self.steps:
            self.result = add_split(keep, received[0], None)[0][0, 0]
            self.state = []
        else:
            axis = 1 if self.steps[0][0] == "z" else 0
            self.state = list(add_split(keep, received[0], axis))

    def finish(self):
        while self.steps:
            self.start()
            self.join()


def body(
    tokens, cotangent, first_gain, second_gain, w_query, w_key, w_value, w_out, w_up, w_down,
    state_rate, state_in, state_out, state_bank, prev_link,
):
    links = Links()
    ndp, nmp, nz = links.ndp, links.nmp, links.nz
    rows = tokens.shape[0]
    per_window = LEN // BLK
    place_in = links.mp % per_window
    window = links.dp * (nmp // per_window) + links.mp // per_window
    link = lax.dynamic_index_in_dim(prev_link, window, keepdims=False)
    info = jnp.stack([links.block_at(p) for p in range(ndp)] + [links.z, links.core]).astype(jnp.int32)
    order = []
    for b in range(ndp):
        far = links.dp ^ b
        order.append(jnp.where(links.core == 0, swap_bits(far, links.dp_bits), far))
    order = jnp.stack(order).astype(jnp.int32)
    attend_info = jnp.stack([links.core, (place_in != 0).astype(jnp.int32)]).astype(jnp.int32)

    channels = state_rate.shape[0]
    maps_here = state_rate.shape[1]
    banks_here = state_bank.shape[0]

    def full_map(values):
        values = values.reshape(ndp, nmp, maps_here, channels).transpose(0, 2, 1, 3)
        return values.reshape(NS, 8, 128)

    chunk = FF // nmp
    groups = 2 if chunk >= 256 else 1
    width = chunk // groups
    mats_keep, mats_send, feed_rows, *late_rows = prepare(
        links, groups, links.core.astype(jnp.int32).reshape(1),
        (w_query, w_key, w_value, w_out), w_up, w_down.T,
    )

    def chip_rows(keep, send):
        return by_core(links, keep, links.core_swap(send), 0)

    pieces = [
        first_gain, second_gain, state_rate.T, state_in.T, state_out.T,
        state_bank.transpose(0, 2, 1),
    ]
    small, sizes = pack(pieces)
    v, u = Live(), Live()
    v.tokens, v.cotangent = tokens, cotangent
    small = small[None]
    v.small = join_small(links, small, links.core_swap(small), links.mp, 0)
    attn = Gather(links, chip_rows(mats_keep, mats_send))
    v.feed_rows = feed_rows
    late_feeds = [Gather(links, chip_rows(*late_rows))] if late_rows else []
    fence(v, [attn, *late_feeds])

    for bit in range(1, links.mp_bits):
        v.small = join_small(links, v.small, links.mp_swap(v.small, bit), links.mp, bit)
    fence(v, [attn])

    feed_weights = lax.all_gather(v.feed_rows, AXES, axis=0, tiled=True)
    del v.feed_rows
    attn.first_z()
    for bit in range(links.dp_bits):
        v.small = join_small(links, v.small, links.dp_swap(v.small, bit), links.dp, bit)
    fence(v, [attn], [attn])
    attn.along_z(1)
    small = v.small.reshape(ndp, nmp, -1)
    del v.small
    starts = [sum(sizes[:i]) for i in range(len(sizes))]
    gain_one, gain_two, rate, gain_in, gain_out, banks = (
        small[:, :, a : a + n] for a, n in zip(starts, sizes)
    )
    v.gain_one = lax.reduce_precision(gain_one.reshape(1, D), 8, 7)
    v.gain_two = lax.reduce_precision(gain_two.reshape(1, D), 8, 7)
    u.rate, u.gain_in, u.gain_out = full_map(rate), full_map(gain_in), full_map(gain_out)
    banks = banks.reshape(ndp, nmp, banks_here, NS, channels)
    bank = lax.dynamic_index_in_dim(banks, link // banks_here, 0, keepdims=False)
    bank = lax.dynamic_index_in_dim(bank, link % banks_here, 1, keepdims=False)
    u.initial = bank.transpose(1, 0, 2).reshape(NS, 8, 128)
    half_blocks = float(BLK)
    v.scal = jnp.stack(
        [place_in.astype(f32) * half_blocks - CTX, (place_in != 0).astype(f32)]
    )
    v.steps, v.steps_back = [], []
    for bit in range(bits_of(per_window)):
        mine = ((links.mp >> bit) & 1).astype(f32)
        inside = (place_in % (1 << bit)).astype(f32)
        span = jnp.float32(half_blocks * (1 << bit))
        v.steps.append(jnp.stack([mine, inside * half_blocks, span]))
        v.steps_back.append(
            jnp.stack([mine, ((1 << bit) - 1 - inside) * half_blocks, span])
        )

    def exchange(bit):
        received = links.mp_swap(v.total, bit)
        v.total, v.before = exchange_step(v.steps[bit], v.total, received, v.before, u.rate)

    u.normed_b, tail = norm_first(v.tokens, v.gain_one)
    u.tail = links.window_shift(tail, 1)
    v.total = scan_own(u.normed_b, u.rate)
    fence(v, [attn], [attn])

    attn.first_dp()
    attn.more_dp()
    v.total = scan_tail(u.tail, v.total, u.rate)
    v.before = jnp.zeros_like(v.total)
    for bit in range(2):
        exchange(bit)
    v.cot_t = v.cotangent.T
    fence(v, [attn, *late_feeds], [attn])
    attn.last_dp(max(ndp // 4, 1), None)
    for bit in range(2, bits_of(per_window)):
        exchange(bit)
    v.inputs_kv = context_states(
        v.scal, u.tail, u.normed_b, v.before, u.initial, u.rate, u.gain_in, u.gain_out
    )
    fence(v, [attn, *late_feeds], [attn])

    for gather in late_feeds:
        gather.first_z()
    v.w_own = place(links, order, attn.blocks())
    attn.state = []
    v.w_other = links.core_swap(v.w_own)
    v.qkv_own = project(v.inputs_kv, v.w_own)
    u.cot_par, u.cot_par_t = links.core_swap(v.cotangent), links.core_swap(v.cot_t)
    fence(v, late_feeds, late_feeds)
    for gather in late_feeds:
        gather.along_z(1)
    v.inputs_par = links.core_swap(v.inputs_kv)
    u.qkv_other = project(v.inputs_kv, v.w_other)
    v.attended = attend(attend_info, v.qkv_own, u.qkv_other)
    fence(v, late_feeds, late_feeds)
    for gather in late_feeds:
        gather.first_dp()
    u.middle, u.second_b, u.second_t = middle_norm(
        attend_info, v.attended, v.tokens, v.w_own, v.w_other, v.gain_two
    )
    u.second_par, u.second_par_t = links.core_swap(u.second_b), links.core_swap(u.second_t)
    v.feed_weights = feed_weights
    fence(v, late_feeds, late_feeds)

    scatters = []
    earlier = None
    for g in range(groups):
        last = g == groups - 1
        acts = (
            u.second_b, u.second_par, v.cotangent, u.cot_par,
            u.second_t, u.second_par_t, v.cot_t, u.cot_par_t,
        )
        if g == 0:
            weights = [v.feed_weights]
            for gather in late_feeds:
                gather.last_dp(0, None)
        else:
            weights = late_feeds[0].blocks()
        *u.sums, keep, keep_far, send, send_far = feed(
            links, info, acts, weights, nz * width, g, groups, earlier, last
        )
        if g == 0:
            v.attended_par = links.core_swap(v.attended)
        waits = list(scatters)
        scatters.append(Scatter(links, keep, send, keep_far, send_far))
        fence(v, scatters, waits + (late_feeds if not last else []))
        if not last:
            scatters[g].start()
        earlier = u.sums
    first, second = scatters[0], scatters[-1]
    both = [first, second] if groups > 1 else [first]
    u.mix_own, v.mix_par, u.back_own, back_par = u.sums
    del v.feed_weights, v.cot_t

    split = groups > 1 and ndp >= 4
    if split:
        first.start()
        second.start_far()
    else:
        second.start()
    v.back_recv = links.core_swap(back_par)
    v.grad_middle, v.branch_own, branch_other, v.grad_attended, v.grad_gain_two = back_middle(
        attend_info, u.middle, u.back_own, v.back_recv, v.cotangent, v.gain_two, v.w_own,
        v.w_other,
    )
    v.branch_par = links.core_swap(branch_other)
    v.grad_gain_two = v.grad_gain_two.reshape(ndp, nmp, -1)
    gain_len = v.grad_gain_two.shape[2]
    v.grad_gain_two = jnp.pad(v.grad_gain_two, ((0, 0), (0, 0), (0, channels - gain_len)))
    v.g_own, v.g_other = attend_back(attend_info, v.qkv_own, u.qkv_other, v.grad_attended)
    fence(v, both, both)

    def exchange_back(bit):
        received = links.mp_swap(v.total, bit)
        v.total, v.after = exchange_back_step(
            v.steps_back[bit], v.total, received, v.after, u.rate
        )

    if split:
        second.start_near()
    v.g_par = links.core_swap(v.g_other)
    v.grad_context = back_project(v.g_own, v.g_other, v.w_own, v.w_other, 0, CTX, bf16)
    v.lows = state_low(v.grad_context, u.rate)
    v.total = v.lows[0]
    v.after = jnp.zeros_like(v.total)
    sums = state_sums(
        v.scal, v.grad_context, u.tail, v.before, v.lows, u.initial, u.rate, u.gain_in, u.gain_out
    )
    bank_owner = link // banks_here
    mat_rows = D // (ndp * nz)
    whole_lines = channels == 128 and banks_here == 1
    if whole_lines:
        shares = pack_shares(
            links, info, bank_owner.reshape(1), sums, v.grad_gain_two, maps_here, mat_rows
        )
    else:
        shares = pack_shares_plain(
            links, bank_owner, link % banks_here, banks_here, sums, v.grad_gain_two, maps_here
        )
    v.shares = add_split(shares[0], links.core_swap(shares[1].astype(bf16)), False, bf16)[0]
    for bit in range(2):
        exchange_back(bit)
    fence(v, both, [second] if split else [])

    for scatter in both:
        scatter.start()
    mats = Scatter(
        links,
        *weight_grads(
            links, info, v.inputs_kv, v.inputs_par, v.g_own, v.g_par, v.attended,
            v.attended_par, v.branch_own, v.branch_par, v.shares,
        ),
    )
    for bit in range(2, bits_of(per_window)):
        exchange_back(bit)
    fence(v, [*both, mats], both)

    mats.start()
    for scatter in both:
        scatter.start()
    tail_sent = sent_tail(v.grad_context, v.after, u.rate, u.gain_in, u.gain_out)
    v.last_sent = links.window_shift(tail_sent, -1)
    v.own_sent = sent_own(v.after, u.rate, u.gain_in, u.gain_out)
    v.part = back_project(v.g_own, v.g_other, v.w_own, v.w_other, CTX, BLK, f32)
    v.grad_tokens, grad_gain_one = back_first(
        v.tokens, v.part, v.own_sent, v.last_sent, v.grad_middle, v.gain_one
    )
    v.gain_parts = grad_gain_one.reshape(ndp * nmp, -1)
    fence(v, [*both, mats], [mats, *both])
    mats.start()
    late = [second] if second.steps else []
    for scatter in late:
        scatter.start()
    gain_parts = lax.all_to_all(v.gain_parts, AXES, split_axis=0, concat_axis=0, tiled=True)
    v.share_one = jnp.sum(gain_parts, axis=0)
    v.mix_recv = links.core_swap(v.mix_par)
    fence(v, [*both, mats], [mats, *late])
    mats.start()
    v.mixed = mix(u.middle, u.mix_own, v.mix_recv)
    for scatter in both:
        scatter.finish()
    v.results = [scatter.result for scatter in both]
    fence(v, [mats], [mats])
    mats.start()
    grad_up = jnp.concatenate([result[0] for result in v.results], 1)
    grad_down = jnp.concatenate([result[1] for result in v.results], 1).T
    mats.join()
    mats.finish()
    grad_tokens = v.grad_tokens
    mixed, share_one = v.mixed, v.share_one
    mats_share = mats.result
    line = 4 * HALF
    extra = mats_share[:, line:]
    if not whole_lines:
        lines = 3 * maps_here + banks_here * NS + 1
        extra = extra.reshape(-1)[: lines * channels].reshape(lines, channels)
    grad_maps = [
        extra[i * maps_here : (i + 1) * maps_here].T for i in range(3)
    ]
    bank_end = 3 * maps_here + banks_here * NS
    grad_bank = extra[3 * maps_here : bank_end].reshape(banks_here, NS, channels)
    grad_bank = grad_bank.transpose(0, 2, 1)
    share_two = extra[bank_end, :gain_len]
    mine_rows = mats_share[:, :line].reshape(2, mat_rows // 2, 4, HALF)
    rows_keep = jnp.where(links.core == 0, mine_rows[0], mine_rows[1])
    rows_send = jnp.where(links.core == 0, mine_rows[1], mine_rows[0])
    grad_rows = by_core(links, rows_keep, links.core_swap(rows_send), 2)
    return (
        mixed, grad_tokens, share_one, share_two,
        grad_rows[:, 0], grad_rows[:, 1], grad_rows[:, 2], grad_rows[:, 3],
        grad_up, grad_down, grad_maps[0], grad_maps[1], grad_maps[2], grad_bank,
    )


def solution(mesh):
    split = P(AXES, None)
    gain = P(AXES)
    maps = P("mp", "dp")
    bank = P("dp", "mp", None)
    return jax.shard_map(
        body,
        mesh=mesh,
        in_specs=(
            split, split, gain, gain, split, split, split, split, split, P(None, AXES),
            maps, maps, maps, bank, P(),
        ),
        out_specs=(
            split, split, gain, gain, split, split, split, split, P("dp", "mp"), P("mp", "dp"),
            maps, maps, maps, bank,
        ),
        check_vma=False,
    )
```

```python
import functools

import jax
import jax.numpy as jnp
from jax import lax
from jax.experimental import pallas as pl
from jax.experimental.pallas import tpu as pltpu
from jax.sharding import PartitionSpec as P

D = 1024
H = 8
HD = 128
FF = 4096
NS = 16
LEN = 4096
BLK = 512
CTX = 128
OWN = BLK - CTX
HALF = D // 2
SCALE = HD ** (-0.5)
AXES = ("dp", "mp")
f32 = jnp.float32
bf16 = jnp.bfloat16
VMEM = pl.BlockSpec(memory_space=pltpu.VMEM)
SMEM = pl.BlockSpec(memory_space=pltpu.SMEM)
ANY = pl.BlockSpec(memory_space=pltpu.HBM)
QKV_COLS = pl.BlockSpec((D, 3 * HALF), lambda i: (0, 0))
OUT_COLS = pl.BlockSpec((D, HALF), lambda i: (0, 3))
NT = (((1,), (1,)), ((), ()))
TN = (((0,), (0,)), ((), ()))


def params(mib):
    return pltpu.CompilerParams(vmem_limit_bytes=mib * 1024 * 1024)


def in_hbm(values):
    return pltpu.with_memory_space_constraint(values, pltpu.HBM)


def in_vmem(values):
    return pltpu.with_memory_space_constraint(values, pltpu.VMEM)


COST = pl.CostEstimate(flops=1, bytes_accessed=1, transcendentals=0)


def bits_of(n):
    return n.bit_length() - 1


def swap_bits(word, count):
    out = 0
    for i in range(count):
        out = out | (((word >> i) & 1) << (count - 1 - i))
    return out


class Links:
    def __init__(self):
        self.ndp = lax.axis_size("dp")
        self.nmp = lax.axis_size("mp")
        self.nz = self.nmp // 2
        self.dp = lax.axis_index("dp")
        self.mp = lax.axis_index("mp")
        self.z = self.mp // 2
        self.core = self.mp % 2
        self.dp_bits = bits_of(self.ndp)
        self.mp_bits = bits_of(self.nmp)

    def send(self, values, target):
        pairs = []
        for d in range(self.ndp):
            for m in range(self.nmp):
                to = target(d, m)
                if to is not None:
                    pairs.append((d * self.nmp + m, to[0] * self.nmp + to[1]))
        return lax.ppermute(values, AXES, pairs)

    def mp_swap(self, values, bit):
        return self.send(values, lambda d, m: (d, m ^ (1 << bit)))

    def dp_swap(self, values, bit):
        return self.send(values, lambda d, m: (d ^ (1 << bit), m))

    def core_swap(self, values):
        return self.mp_swap(values, 0)

    def fan(self, values, level):
        other = self.dp_bits - 1 - level
        return self.send(
            values, lambda d, m: (d ^ (1 << (other if m % 2 else level)), m)
        )

    def block_at(self, position):
        mirrored = swap_bits(position, self.dp_bits)
        return self.dp ^ jnp.where(self.core == 0, mirrored, position)

    def window_shift(self, values, step):
        per = LEN // BLK

        def target(d, m):
            inside = m % per + step
            return (d, m + step) if 0 <= inside < per else None

        return self.send(values, target)


def by_core(links, first, second, axis):
    return jnp.where(
        links.core == 0,
        jnp.concatenate([first, second], axis),
        jnp.concatenate([second, first], axis),
    )


def spread_rows(src_ref, dst_ref, rows, start=0):
    for r in range(0, rows, 16):
        block = src_ref[start + r : start + r + 16, :].astype(f32)
        for j in range(8):
            dst_ref[r : r + 16, j, :] = block[:, j * 128 : (j + 1) * 128]


def gather_rows(src_ref, dst_ref, rows):
    for r in range(0, rows, 16):
        for j in range(8):
            dst_ref[r : r + 16, j * 128 : (j + 1) * 128] = src_ref[r : r + 16, j, :].astype(
                dst_ref.dtype
            )


def move_on(state, rate, steps):
    far = jnp.exp(-rate * steps)
    near = jnp.exp(-rate * (steps - 1.0)) * steps
    return far * state[0], far * state[1] + near * state[0]


def scan_rows(xs, rows, decay):
    zero = jnp.zeros((NS, 8, 128), f32)

    def step(i, carry):
        u, v = carry
        for k in range(8):
            v = decay * v + u
            u = decay * u + xs[i * 8 + k][None]
        return u, v

    return lax.fori_loop(0, rows // 8, step, (zero, zero))


def scan_own_kernel(x_ref, rate_ref, out_ref, xs):
    spread_rows(x_ref, xs, OWN)
    u, v = scan_rows(xs, OWN, jnp.exp(-rate_ref[...]))
    out_ref[0] = u
    out_ref[1] = v


def scan_tail_kernel(x_ref, own_ref, rate_ref, out_ref, xs):
    spread_rows(x_ref, xs, CTX)
    state = scan_rows(xs, CTX, jnp.exp(-rate_ref[...]))
    u, v = move_on(state, rate_ref[...], float(OWN))
    out_ref[0] = u + own_ref[0]
    out_ref[1] = v + own_ref[1]


STATE = jax.ShapeDtypeStruct((2, NS, 8, 128), f32)


def scan_own(values, rate):
    return pl.pallas_call(
        scan_own_kernel,
        out_shape=STATE,
        in_specs=[VMEM, VMEM],
        out_specs=VMEM,
        scratch_shapes=[pltpu.VMEM((OWN, 8, 128), f32)],
        compiler_params=params(6),
        cost_estimate=COST,
        name="scan_own",
    )(values, rate)


def scan_tail(values, own, rate):
    return pl.pallas_call(
        scan_tail_kernel,
        out_shape=STATE,
        in_specs=[VMEM] * 3,
        out_specs=VMEM,
        scratch_shapes=[pltpu.VMEM((CTX, 8, 128), f32)],
        compiler_params=params(4),
        cost_estimate=COST,
        name="scan_tail",
    )(values, own, rate)


def exchange_kernel(scal, total_ref, recv_ref, before_ref, rate_ref, total_out, before_out):
    mine, inside, span = scal[0], scal[1], scal[2]
    rate = rate_ref[...]
    recv = (recv_ref[0], recv_ref[1])
    total = (total_ref[0], total_ref[1])
    moved = move_on(recv, rate, inside)
    low = tuple(mine * r + (1.0 - mine) * t for r, t in zip(recv, total))
    high = tuple(mine * t + (1.0 - mine) * r for r, t in zip(recv, total))
    far = move_on(low, rate, span)
    for i in range(2):
        before_out[i] = before_ref[i] + mine * moved[i]
        total_out[i] = far[i] + high[i]


def exchange_step(scal, total, received, before, rate):
    return pl.pallas_call(
        exchange_kernel,
        out_shape=(STATE, STATE),
        in_specs=[SMEM] + [VMEM] * 4,
        out_specs=(VMEM, VMEM),
        compiler_params=params(3),
        cost_estimate=COST,
        name="exchange_step",
    )(scal, total, received, before, rate)


def exchange_back_kernel(scal, total_ref, recv_ref, after_ref, rate_ref, total_out, after_out):
    mine, inside, span = scal[0], scal[1], scal[2]
    rate = rate_ref[...]
    recv, total = recv_ref[...], total_ref[...]
    after_out[...] = after_ref[...] + (1.0 - mine) * (jnp.exp(-rate * inside) * recv)
    low = mine * recv + (1.0 - mine) * total
    high = mine * total + (1.0 - mine) * recv
    total_out[...] = low + jnp.exp(-rate * span) * high


def exchange_back_step(scal, total, received, after, rate):
    one = jax.ShapeDtypeStruct((NS, 8, 128), f32)
    return pl.pallas_call(
        exchange_back_kernel,
        out_shape=(one, one),
        in_specs=[SMEM] + [VMEM] * 4,
        out_specs=(VMEM, VMEM),
        compiler_params=params(3),
        cost_estimate=COST,
        name="exchange_back_step",
    )(scal, total, received, after, rate)


def context_kernel(
    scal, x_ref, own_ref, before_ref, initial_ref, rate_ref, in_ref, out_map_ref, out_ref, xs, ys
):
    out_ref[CTX:, :] = own_ref[...]
    spread_rows(x_ref, xs, CTX)
    rate = rate_ref[...]
    decay = jnp.exp(-rate)
    weight = in_ref[...] * out_map_ref[...]
    carried = jnp.exp(-rate * scal[0]) * initial_ref[...] * scal[1]
    start = out_map_ref[...] * (in_ref[...] * before_ref[0] + carried)

    def step(i, y):
        for k in range(8):
            y = decay * y + weight * xs[i * 8 + k][None]
            ys[i * 8 + k] = jnp.sum(y, axis=0)
        return y

    lax.fori_loop(0, CTX // 8, step, start)
    gather_rows(ys, out_ref, CTX)


def context_states(scal, tail, own, before, initial, rate, gain_in, gain_out):
    return pl.pallas_call(
        context_kernel,
        out_shape=jax.ShapeDtypeStruct((CTX + BLK, D), bf16),
        in_specs=[SMEM] + [VMEM] * 7,
        out_specs=VMEM,
        scratch_shapes=[pltpu.VMEM((CTX, 8, 128), f32)] * 2,
        compiler_params=params(6),
        cost_estimate=COST,
        name="context_states",
    )(scal, tail, own, before, initial, rate, gain_in, gain_out)


def state_low_kernel(g_ref, rate_ref, out_ref, gs):
    spread_rows(g_ref, gs, CTX)
    decay = jnp.exp(-rate_ref[...])
    zero = jnp.zeros((NS, 8, 128), f32)

    def back(i, carry):
        low, slope = carry
        for k in range(8):
            slope = decay * slope + low
            low = decay * low + gs[CTX - 1 - (i * 8 + k)][None]
        return low, slope

    low, slope = lax.fori_loop(0, CTX // 8, back, (zero, zero))
    out_ref[0] = low
    out_ref[1] = slope


def state_low(grad_context, rate):
    return pl.pallas_call(
        state_low_kernel,
        out_shape=jax.ShapeDtypeStruct((2, NS, 8, 128), f32),
        in_specs=[VMEM] * 2,
        out_specs=VMEM,
        scratch_shapes=[pltpu.VMEM((CTX, 8, 128), f32)],
        compiler_params=params(3),
        cost_estimate=COST,
        name="state_low",
    )(grad_context, rate)


def state_sums_kernel(
    scal, g_ref, x_ref, start_ref, lows_ref, initial_ref, rate_ref, in_ref, out_map_ref, out_ref,
    gs, xs,
):
    spread_rows(g_ref, gs, CTX)
    spread_rows(x_ref, xs, CTX)
    part = NS // 2
    for n in range(0, NS, part):
        span = slice(n, n + part)
        rate = rate_ref[span]
        decay = jnp.exp(-rate)
        zero = jnp.zeros((part, 8, 128), f32)

        def step(i, carry):
            u, v, su, sv = carry
            for k in range(4):
                v = decay * v + u
                u = decay * u + xs[i * 4 + k][None]
                g = gs[i * 4 + k][None]
                su = su + g * u
                sv = sv + g * v
            return u, v, su, sv

        _, _, su, sv = lax.fori_loop(
            0, CTX // 4, step, (start_ref[0, span], start_ref[1, span], zero, zero)
        )
        far = jnp.exp(-rate * scal[0])
        low, slope = lows_ref[0, span], lows_ref[1, span]
        sum_init = far * decay * low
        sum_slope = far * ((scal[0] + 1.0) * low + decay * slope)
        initial = initial_ref[span] * scal[1]
        gain_in, gain_out = in_ref[span], out_map_ref[span]
        out_ref[0, span] = -decay * gain_out * (gain_in * sv + initial * sum_slope)
        out_ref[1, span] = gain_out * su
        out_ref[2, span] = gain_in * su + initial * sum_init
        out_ref[3, span] = gain_out * sum_init * scal[1]


def state_sums(scal, grad_context, tail, start, lows, initial, rate, gain_in, gain_out):
    return pl.pallas_call(
        state_sums_kernel,
        out_shape=jax.ShapeDtypeStruct((4, NS, 8, 128), f32),
        in_specs=[SMEM] + [VMEM] * 8,
        out_specs=VMEM,
        scratch_shapes=[pltpu.VMEM((CTX, 8, 128), f32)] * 2,
        compiler_params=params(4),
        cost_estimate=COST,
        name="state_sums",
    )(scal, grad_context, tail, start, lows, initial, rate, gain_in, gain_out)


def sent_tail_kernel(g_ref, after_ref, rate_ref, in_ref, out_map_ref, out_ref, gs, ys):
    spread_rows(g_ref, gs, CTX)
    rate = rate_ref[...]
    decay = jnp.exp(-rate)
    weight = in_ref[...] * out_map_ref[...]
    start = jnp.exp(-rate * float(OWN)) * weight * after_ref[...]

    def back(i, y):
        for k in range(8):
            t = CTX - 1 - (i * 8 + k)
            y = decay * y + weight * gs[t][None]
            ys[t] = jnp.sum(y, axis=0)
        return y

    lax.fori_loop(0, CTX // 8, back, start)
    gather_rows(ys, out_ref, CTX)


def sent_tail(grad_context, after, rate, gain_in, gain_out):
    return pl.pallas_call(
        sent_tail_kernel,
        out_shape=jax.ShapeDtypeStruct((CTX, D), bf16),
        in_specs=[VMEM] * 5,
        out_specs=VMEM,
        scratch_shapes=[pltpu.VMEM((CTX, 8, 128), f32)] * 2,
        compiler_params=params(4),
        cost_estimate=COST,
        name="sent_tail",
    )(grad_context, after, rate, gain_in, gain_out)


def sent_own_kernel(after_ref, rate_ref, in_ref, out_map_ref, out_ref, ys):
    decay = jnp.exp(-rate_ref[...])

    def back(i, y):
        for k in range(8):
            y = decay * y
            ys[OWN - 1 - (i * 8 + k)] = jnp.sum(y, axis=0)
        return y

    lax.fori_loop(0, OWN // 8, back, in_ref[...] * out_map_ref[...] * after_ref[...])
    gather_rows(ys, out_ref, OWN)


def sent_own(after, rate, gain_in, gain_out):
    return pl.pallas_call(
        sent_own_kernel,
        out_shape=jax.ShapeDtypeStruct((OWN, D), bf16),
        in_specs=[VMEM] * 4,
        out_specs=VMEM,
        scratch_shapes=[pltpu.VMEM((OWN, 8, 128), f32)],
        compiler_params=params(6),
        cost_estimate=COST,
        name="sent_own",
    )(after, rate, gain_in, gain_out)


def attention_mask(keys, queries, first_query, opened):
    row = lax.broadcasted_iota(jnp.int32, (keys, queries), 0)
    col = lax.broadcasted_iota(jnp.int32, (keys, queries), 1) + first_query
    return jnp.where(row < CTX, (1 - opened) * BLK, row - CTX) <= col


def head_parts(ref, offset):
    q = ref[CTX:, pl.ds(offset, HD)]
    k = ref[:, pl.ds(HALF + offset, HD)]
    v = ref[:, pl.ds(2 * HALF + offset, HD)]
    return q, k, v


def probabilities(k, q, first_query, opened):
    scores = lax.dot_general(k, q, NT, preferred_element_type=f32) * SCALE
    scores = jnp.where(
        attention_mask(k.shape[0], q.shape[0], first_query, opened), scores, -jnp.inf
    )
    lifted = jnp.exp(scores - jnp.max(scores, axis=0, keepdims=True))
    return lifted * (1.0 / jnp.sum(lifted, axis=0, keepdims=True))


QT = BLK // 2


def attend_kernel(info, own_ref, other_ref, out_ref):
    opened = info[1]

    @pl.loop(0, H // 2)
    def _(h):
        offset = pl.multiple_of(h * HD, HD)
        for side, qkv in enumerate((own_ref, other_ref)):
            q, k, v = head_parts(qkv, offset)
            v_t = v.T
            home = pl.multiple_of((side ^ info[0]) * HALF + h * HD, HD)
            for first in range(0, BLK, QT):
                keys = CTX + first + QT
                p = probabilities(k[:keys], q[first : first + QT], first, opened).astype(bf16)
                mixed = jnp.dot(v_t[:, :keys], p, preferred_element_type=f32)
                out_ref[first : first + QT, pl.ds(home, HD)] = mixed.T.astype(bf16)


def attend(info, own, other):
    return pl.pallas_call(
        attend_kernel,
        out_shape=jax.ShapeDtypeStruct((BLK, D), bf16),
        in_specs=[SMEM] + [VMEM] * 2,
        out_specs=VMEM,
        compiler_params=params(14),
        cost_estimate=COST,
        name="attend",
    )(info, own, other)


def attend_back_kernel(
    info, own_ref, other_ref, grad_ref, g_own_ref, g_other_ref, acc
):
    opened = info[1]
    sides = ((own_ref, g_own_ref), (other_ref, g_other_ref))
    for _, g in sides:
        g[:CTX, :HALF] = jnp.zeros((CTX, HALF), bf16)

    @pl.loop(0, H // 2)
    def _(h):
        offset = pl.multiple_of(h * HD, HD)
        for side, (qkv, g) in enumerate(sides):
            q, k, v = head_parts(qkv, offset)
            k_t = k.T
            home = pl.multiple_of((side ^ info[0]) * HALF + h * HD, HD)
            for first in range(0, BLK, QT):
                keys = CTX + first + QT
                q_now = q[first : first + QT]
                go = grad_ref[first : first + QT, pl.ds(home, HD)]
                p = probabilities(k[:keys], q_now, first, opened)
                gp = lax.dot_general(v[:keys], go, NT, preferred_element_type=f32)
                mean = jnp.sum(p * gp, axis=0, keepdims=True)
                gs = (p * (gp - mean)).astype(bf16)
                gq_t = jnp.dot(k_t[:, :keys], gs, preferred_element_type=f32) * SCALE
                g[CTX + first : CTX + first + QT, pl.ds(offset, HD)] = gq_t.T.astype(bf16)
                gk = jnp.dot(gs, q_now, preferred_element_type=f32)
                gv = jnp.dot(p.astype(bf16), go, preferred_element_type=f32)
                if first == 0:
                    acc[0, :keys] = gk
                    acc[1, :keys] = gv
                else:
                    early = CTX + QT
                    gk_all = jnp.concatenate([gk[:early] + acc[0, :early], gk[early:]], 0)
                    gv_all = jnp.concatenate([gv[:early] + acc[1, :early], gv[early:]], 0)
                    g[:, pl.ds(HALF + offset, HD)] = (gk_all * SCALE).astype(bf16)
                    g[:, pl.ds(2 * HALF + offset, HD)] = gv_all.astype(bf16)


def attend_back(info, own, other, grad):
    out = jax.ShapeDtypeStruct((CTX + BLK, 3 * HALF), bf16)
    return pl.pallas_call(
        attend_back_kernel,
        out_shape=(out, out),
        in_specs=[SMEM] + [VMEM] * 3,
        out_specs=(VMEM, VMEM),
        scratch_shapes=[pltpu.VMEM((2, CTX + QT, HD), f32)],
        compiler_params=params(18),
        cost_estimate=COST,
        name="attend_back",
    )(info, own, other, grad)


def gelu_parts(x):
    cdf = 0.5 * (1.0 + lax.erf(x * 0.7071067811865476))
    slope = cdf + x * (jnp.exp(-0.5 * x * x) * 0.3989422804014327)
    return x * cdf, slope


def feed_kernel(
    ndp, nz, width, index, groups, earlier, last, info, s_own, s_par, c_own, c_par,
    st_own, st_par, ct_own, ct_par, *rest
):
    rows = s_own.shape[0]
    block = D // ndp
    group = nz * width
    half = ndp // 2
    s, c = (s_own, s_par), (c_own, c_par)
    count = ndp if index else 1
    weights, rest = rest[:count], rest[count:]
    if earlier:
        m_in, g_in, *rest = rest
    if last:
        m_own, m_par, g_own, g_par, *rest = rest
    else:
        m_out, g_out, *rest = rest
    parts, (st, ct, w, act, gh, sems) = rest[:4], rest[4:]
    at = [pl.multiple_of(info[p] * block, block) for p in range(ndp)]
    z = info[ndp]
    copies = []

    def start(src, dst):
        copy = pltpu.make_async_copy(src, dst, sems.at[len(copies)])
        copy.start()
        copies.append(copy)

    if index:
        for p in range(ndp):
            start(weights[p], w.at[pl.ds(at[p], block), :])
    else:
        at_core = pl.multiple_of(info[ndp + 1] * 2 * group, 128)
        start(weights[0].at[:, pl.ds(at_core, 2 * group)], w)
    for own, par, dst in ((st_own, st_par, st), (ct_own, ct_par, ct)):
        for p in range(ndp):
            for i, src in enumerate((own, par)):
                start(
                    src.at[pl.ds(at[p], block), :],
                    dst.at[p * block : (p + 1) * block, i * rows : (i + 1) * rows],
                )
    for copy in copies[:count]:
        copy.wait()

    @pl.loop(0, nz)
    def _(b):
        up = pl.ds(pl.multiple_of(b * width, width), width)
        down = pl.ds(pl.multiple_of(group + b * width, width), width)
        for i in range(2):
            part = slice(i * rows, (i + 1) * rows)
            hidden = jnp.dot(s[i][...], w[:, up], preferred_element_type=f32)
            grad = jnp.dot(c[i][...], w[:, down], preferred_element_type=f32)
            active, slope = gelu_parts(hidden)
            act[part, up] = active.astype(bf16)
            gh[part, up] = (grad * slope).astype(bf16)

    for copy in copies[count:]:
        copy.wait()

    @pl.loop(0, nz)
    def _(r):
        cols = pl.ds(pl.multiple_of((z ^ swap_bits(r, bits_of(nz))) * width, width), width)
        for part in range(2):
            span = slice(part * half * block, (part + 1) * half * block)
            up = jnp.dot(st[span, :], gh[:, cols], preferred_element_type=f32).astype(bf16)
            down = jnp.dot(ct[span, :], act[:, cols], preferred_element_type=f32).astype(bf16)
            for p in range(half):
                far = p >= half // 2
                dst = parts[2 * part + far]
                q = p - far * (half // 2)
                dst[q, r, 0] = up[p * block : (p + 1) * block]
                dst[q, r, 1] = down[p * block : (p + 1) * block]

    for name, left, first in (("g", gh, 0), ("m", act, group)):
        for p in range(ndp):
            right = w[p * block : (p + 1) * block, first : first + group]
            cols = slice(p * block, (p + 1) * block)
            for i in range(2):
                part = slice(i * rows, (i + 1) * rows)
                value = lax.dot_general(left[part, :], right, NT, preferred_element_type=f32)
                if earlier:
                    value = value + (g_in if name == "g" else m_in)[part, cols]
                if not last:
                    (g_out if name == "g" else m_out)[part, cols] = value
                elif i == 0:
                    (g_own if name == "g" else m_own)[:, cols] = value
                else:
                    (g_par if name == "g" else m_par)[:, cols] = value.astype(bf16)


def feed(links, info, acts, weights, group, index, groups, earlier, last):
    ndp, nz = links.ndp, links.nz
    rows = acts[0].shape[0]
    tokens = 2 * rows
    block = D // ndp
    width = group // nz
    half = ndp // 2
    full = pltpu.VMEM((tokens, D), f32)
    own = jax.ShapeDtypeStruct((rows, D), f32)
    par = jax.ShapeDtypeStruct((rows, D), bf16)
    grads = tuple(
        jax.ShapeDtypeStruct((count, nz, 2, block, width), bf16)
        for count in (half // 2, half - half // 2) * 2
    )
    out_shape = (own, par, own, par, *grads) if last else (full, full, *grads)
    earlier = tuple(earlier) if earlier else ()
    return pl.pallas_call(
        functools.partial(feed_kernel, ndp, nz, width, index, groups, bool(earlier), last),
        out_shape=out_shape,
        in_specs=[SMEM] + [VMEM] * len(acts) + [ANY] * len(weights) + [VMEM] * len(earlier),
        out_specs=(VMEM,) * len(out_shape),
        scratch_shapes=[
            pltpu.VMEM((D, tokens), bf16),
            pltpu.VMEM((D, tokens), bf16),
            pltpu.VMEM((D, 2 * group), bf16),
            pltpu.VMEM((tokens, group), bf16),
            pltpu.VMEM((tokens, group), bf16),
            pltpu.SemaphoreType.DMA((5 * ndp,)),
        ],
        compiler_params=params(30),
        cost_estimate=COST,
        name="feed_last" if last else "feed_first",
    )(info, *map(in_vmem, acts), *map(in_hbm, weights), *map(in_vmem, earlier))


def norm_parts(values):
    center = values - jnp.mean(values, axis=-1, keepdims=True)
    spread = jnp.mean(center * center, axis=-1, keepdims=True)
    inverse = lax.rsqrt(spread + 1e-05)
    return center * inverse, inverse


def norm_back(grad, unit, inverse, gain):
    scaled = grad * gain
    return (
        scaled
        - jnp.mean(scaled, axis=-1, keepdims=True)
        - unit * jnp.mean(scaled * unit, axis=-1, keepdims=True)
    ) * inverse


def dot(left, right):
    return jnp.dot(left, right, preferred_element_type=f32)


def dot_nt(left, right):
    return lax.dot_general(left, right, NT, preferred_element_type=f32)


ROWS = 128


def norm_kernel(x_ref, gain_ref, out_ref, tail_ref):
    for r in range(0, x_ref.shape[0], ROWS):
        unit, _ = norm_parts(x_ref[r : r + ROWS, :].astype(f32))
        out_ref[r : r + ROWS, :] = (unit * gain_ref[...]).astype(bf16)
    tail_ref[...] = out_ref[OWN:, :]


def norm_first(tokens, gain):
    return pl.pallas_call(
        norm_kernel,
        out_shape=(
            jax.ShapeDtypeStruct(tokens.shape, bf16),
            jax.ShapeDtypeStruct((CTX, D), bf16),
        ),
        in_specs=[VMEM] * 2,
        out_specs=(VMEM, VMEM),
        compiler_params=params(5),
        cost_estimate=COST,
        name="norm_first",
    )(tokens, gain)


def middle_kernel(
    info, att_ref, tok_ref, o_own, o_other, gain_ref, mid_ref, second_ref, second_t_ref
):
    att = att_ref[...]
    for side, weight in enumerate((o_own, o_other)):
        cols = pl.ds(pl.multiple_of((side ^ info[0]) * HALF, HALF), HALF)
        mid_ref[:, cols] = tok_ref[:, cols].astype(f32) + dot(att, weight[...])
    for r in range(0, att_ref.shape[0], ROWS):
        unit, _ = norm_parts(mid_ref[r : r + ROWS, :])
        second = unit * gain_ref[...]
        second_ref[r : r + ROWS, :] = second.astype(bf16)
        second_t_ref[:, r : r + ROWS] = second.T.astype(bf16)


def middle_norm(info, attended, tokens, o_own, o_other, gain):
    rows = tokens.shape[0]
    return pl.pallas_call(
        middle_kernel,
        out_shape=(
            jax.ShapeDtypeStruct((rows, D), f32),
            pltpu.VMEM((rows, D), bf16),
            pltpu.VMEM((D, rows), bf16),
        ),
        grid=(1,),
        in_specs=[SMEM, VMEM, VMEM, OUT_COLS, OUT_COLS, VMEM],
        out_specs=(VMEM,) * 3,
        compiler_params=params(16),
        cost_estimate=COST,
        name="middle_norm",
    )(info, attended, tokens, in_hbm(o_own), in_hbm(o_other), gain)


def back_middle_kernel(
    info, mid_ref, own_ref, recv_ref, cot_ref, gain_ref, o_own, o_other,
    grad_ref, b_own_ref, b_other_ref, att_ref, gain_grad_ref, branch,
):
    total = jnp.zeros((1, D), f32)
    for r in range(0, mid_ref.shape[0], ROWS):
        span = slice(r, r + ROWS)
        unit, inverse = norm_parts(mid_ref[span, :])
        grad = own_ref[span, :] + recv_ref[span, :].astype(f32)
        total = total + jnp.sum(grad * unit, axis=0, keepdims=True)
        back = cot_ref[span, :].astype(f32) + norm_back(grad, unit, inverse, gain_ref[...])
        grad_ref[span, :] = back
        branch[span, :] = back.astype(bf16)
    gain_grad_ref[...] = total
    for side, out in enumerate((b_own_ref, b_other_ref)):
        out[...] = branch[:, pl.ds(pl.multiple_of((side ^ info[0]) * HALF, HALF), HALF)]
    att = dot_nt(b_own_ref[...], o_own[...]) + dot_nt(b_other_ref[...], o_other[...])
    att_ref[...] = att.astype(bf16)


def back_middle(info, middle, own, received, cotangent, gain, o_own, o_other):
    rows = middle.shape[0]
    part = jax.ShapeDtypeStruct((rows, HALF), bf16)
    return pl.pallas_call(
        back_middle_kernel,
        out_shape=(
            jax.ShapeDtypeStruct((rows, D), f32),
            part,
            part,
            jax.ShapeDtypeStruct((rows, D), bf16),
            jax.ShapeDtypeStruct((1, D), f32),
        ),
        grid=(1,),
        in_specs=[SMEM] + [VMEM] * 5 + [OUT_COLS] * 2,
        out_specs=(VMEM,) * 5,
        scratch_shapes=[pltpu.VMEM((rows, D), bf16)],
        compiler_params=params(30),
        cost_estimate=COST,
        name="back_middle",
    )(info, middle, own, received, cotangent, gain, in_hbm(o_own), in_hbm(o_other))


def project_kernel(x_ref, w_ref, out_ref):
    for first in range(0, 3 * HALF, HALF):
        cols = slice(first, first + HALF)
        out_ref[:, cols] = dot(x_ref[...], w_ref[:, cols]).astype(bf16)


def project(values, weights):
    return pl.pallas_call(
        project_kernel,
        out_shape=jax.ShapeDtypeStruct((values.shape[0], 3 * HALF), bf16),
        grid=(1,),
        in_specs=[VMEM, QKV_COLS],
        out_specs=VMEM,
        compiler_params=params(16),
        cost_estimate=COST,
        name="project",
    )(values, in_hbm(weights))


def back_project_kernel(first, g_own, g_other, w_own, w_other, out_ref):
    rows = slice(first, first + out_ref.shape[0])
    for at in range(0, D, HALF):
        cols = slice(at, at + HALF)
        value = dot_nt(g_own[rows, :], w_own[cols, :]) + dot_nt(g_other[rows, :], w_other[cols, :])
        out_ref[:, cols] = value.astype(out_ref.dtype)


def back_project(g_own, g_other, w_own, w_other, first, rows, dtype):
    return pl.pallas_call(
        functools.partial(back_project_kernel, first),
        out_shape=jax.ShapeDtypeStruct((rows, D), dtype),
        grid=(1,),
        in_specs=[VMEM, VMEM, QKV_COLS, QKV_COLS],
        out_specs=VMEM,
        compiler_params=params(26),
        cost_estimate=COST,
        name="back_project",
    )(g_own, g_other, in_hbm(w_own), in_hbm(w_other))


def back_first_kernel(
    tok_ref, part_ref, sent_ref, last_ref, mid_ref, gain_ref, out_ref, gain_grad_ref
):
    total = jnp.zeros((1, D), f32)
    for r in range(0, tok_ref.shape[0], ROWS):
        span = slice(r, r + ROWS)
        unit, inverse = norm_parts(tok_ref[span, :].astype(f32))
        sent = sent_ref[span, :] if r < OWN else last_ref[r - OWN : r - OWN + ROWS, :]
        grad = part_ref[span, :] + sent.astype(f32)
        total = total + jnp.sum(grad * unit, axis=0, keepdims=True)
        back = mid_ref[span, :] + norm_back(grad, unit, inverse, gain_ref[...])
        out_ref[span, :] = back.astype(bf16)
    gain_grad_ref[...] = total


def back_first(tokens, part, sent, last, grad_middle, gain):
    return pl.pallas_call(
        back_first_kernel,
        out_shape=(
            jax.ShapeDtypeStruct(tokens.shape, bf16),
            jax.ShapeDtypeStruct((1, D), f32),
        ),
        in_specs=[VMEM] * 6,
        out_specs=(VMEM,) * 2,
        compiler_params=params(14),
        cost_estimate=COST,
        name="back_first",
    )(tokens, part, sent, last, grad_middle, gain)


def weight_grad_kernel(
    ndp, nz, info, x_own, x_par, g_own, g_par, a_own, a_par, b_own, b_par, shares,
    keep_ref, send_ref,
):
    block = D // ndp
    rows = block // nz
    z = info[ndp]
    half = ndp // 2
    for p in range(ndp):
        cols = pl.ds(pl.multiple_of(info[p] * block, block), block)
        grad = dot(x_own[:, cols].T, g_own[...]) + dot(x_par[:, cols].T, g_par[...])
        out = dot(a_own[:, cols].T, b_own[...]) + dot(a_par[:, cols].T, b_par[...])
        grad = grad.astype(bf16)
        out = out.astype(bf16)
        dst = keep_ref if p < half else send_ref
        for b in range(nz):
            r = swap_bits(z ^ b, bits_of(nz))
            span = slice(b * rows, (b + 1) * rows)
            dst[p % half, r, :, : 3 * HALF] = grad[span]
            dst[p % half, r, :, 3 * HALF : 4 * HALF] = out[span]
            dst[p % half, r, :, 4 * HALF :] = shares[p, r]


def weight_grads(links, info, x_own, x_par, g_own, g_par, a_own, a_par, b_own, b_par, shares):
    ndp, nz = links.ndp, links.nz
    line = 4 * HALF + shares.shape[3]
    out = jax.ShapeDtypeStruct((ndp // 2, nz, D // (ndp * nz), line), bf16)
    return pl.pallas_call(
        functools.partial(weight_grad_kernel, ndp, nz),
        out_shape=(out, out),
        in_specs=[SMEM] + [VMEM] * 9,
        out_specs=(VMEM, VMEM),
        compiler_params=params(24),
        cost_estimate=COST,
        name="weight_grads",
    )(info, x_own, x_par, g_own, g_par, a_own, a_par, b_own, b_par, shares)


def shares_kernel(ndp, nmp, maps, info, owner, sums_ref, gain_ref, out):
    for p in range(ndp):
        d = info[p]
        mine = (owner[0] == d).astype(f32)
        for m in range(nmp):
            r = swap_bits(info[ndp] ^ (m // 2), bits_of(nmp // 2))
            other = (m % 2) ^ info[ndp + 1]
            place_of = jnp.where(other == 0, p, swap_bits(p, bits_of(ndp)))
            to = out.at[other, place_of, r]
            for i in range(3):
                rows = sums_ref[i, pl.ds(d * maps, maps), m, :]
                to[i * maps : (i + 1) * maps, :] = rows
            to[3 * maps : 3 * maps + NS, :] = sums_ref[3, :, m, :] * mine
            to[3 * maps + NS :, :] = jnp.zeros((to.shape[0] - 3 * maps - NS, 128), f32)
            to[3 * maps + NS : 3 * maps + NS + 1, :] = gain_ref[pl.ds(d, 1), m, :]


def pack_shares(links, info, owner, sums, gain, maps, lines):
    out = jax.ShapeDtypeStruct((2, links.ndp, links.nz, lines, 128), f32)
    return pl.pallas_call(
        functools.partial(shares_kernel, links.ndp, links.nmp, maps),
        out_shape=out,
        in_specs=[SMEM, SMEM, VMEM, VMEM],
        out_specs=VMEM,
        compiler_params=params(3),
        cost_estimate=COST,
        name="pack_shares",
    )(info, owner, sums, gain)


def prepare_kernel(
    nz, groups, core, q_ref, k_ref, v_ref, o_ref, up_ref, down_ref, keep, send, feed, *late
):
    for i, ref in enumerate((q_ref, k_ref, v_ref, o_ref)):
        to = slice(i * HALF, (i + 1) * HALF)
        keep[:, to] = ref[:, pl.ds(pl.multiple_of(core[0] * HALF, HALF), HALF)].astype(bf16)
        send[:, to] = ref[:, pl.ds(pl.multiple_of((1 - core[0]) * HALF, HALF), HALF)].astype(bf16)
    width = FF // (2 * nz * groups)
    at = 0
    for c in range(2):
        for ref in (up_ref, down_ref):
            for b in range(nz):
                first = (b * 2 + c) * groups * width
                feed[:, at : at + width] = ref[:, first : first + width].astype(bf16)
                at += width
    for i, out in enumerate(late):
        at = 0
        for ref in (up_ref, down_ref):
            for b in range(nz):
                first = ((b * 2 + (core[0] ^ i)) * groups + 1) * width
                span = pl.ds(pl.multiple_of(first, width), width)
                out[:, at : at + width] = ref[:, span].astype(bf16)
                at += width


def prepare(links, groups, core, mats, up, down):
    rows = up.shape[0]
    part = jax.ShapeDtypeStruct((rows, 4 * HALF), bf16)
    late = (jax.ShapeDtypeStruct((rows, FF // 2), bf16),) * 2 if groups > 1 else ()
    return pl.pallas_call(
        functools.partial(prepare_kernel, links.nz, groups),
        out_shape=(part, part, jax.ShapeDtypeStruct((rows, 2 * FF // groups), bf16), *late),
        in_specs=[SMEM] + [VMEM] * 6,
        out_specs=(VMEM,) * (3 + len(late)),
        compiler_params=params(5),
        cost_estimate=COST,
        name="prepare",
    )(core, *(in_hbm(values) for values in (*mats, up, down)))


def place_kernel(ndp, order, *refs):
    out = refs[ndp]
    b = pl.program_id(0)
    for p in range(ndp):

        @pl.when(order[b] == p)
        def _(p=p):
            out[...] = refs[p][...]


def place(links, order, pieces):
    block, cols = pieces[0].shape
    ndp = links.ndp
    return pl.pallas_call(
        functools.partial(place_kernel, ndp),
        out_shape=pltpu.HBM((ndp * block, cols), pieces[0].dtype),
        grid_spec=pltpu.PrefetchScalarGridSpec(
            num_scalar_prefetch=1,
            grid=(ndp,),
            in_specs=[VMEM] * ndp,
            out_specs=pl.BlockSpec((block, cols), lambda b, order: (b, 0)),
        ),
        compiler_params=params(12),
        cost_estimate=COST,
        name="place",
    )(order, *pieces)


def add_b(left, right):
    return (left.astype(f32) + right.astype(f32)).astype(bf16)


def in_order(links, values, core):
    ndp, nz = values.shape[:2]
    inner = values.shape[2:]
    bits = links.dp_bits + links.mp_bits - 1
    split = values.reshape((2,) * bits + inner)
    for axis in range(links.dp_bits):
        mine = (links.dp >> (links.dp_bits - 1 - axis)) & 1
        split = jnp.where(mine == 0, split, jnp.flip(split, axis))
    for axis in range(links.dp_bits, bits):
        mine = (links.z >> (bits - 1 - axis)) & 1
        split = jnp.where(mine == 0, split, jnp.flip(split, axis))
    dp_axes, z_axes = list(range(links.dp_bits)), list(range(links.dp_bits, bits))
    rest = list(range(bits, split.ndim))
    split = split.transpose((dp_axes if core else dp_axes[::-1]) + z_axes[::-1] + rest)
    return split.reshape(values.shape)


def pack(pieces):
    sizes = [piece.size for piece in pieces]
    packed = jnp.concatenate([piece.reshape(-1) for piece in pieces])
    return jnp.pad(packed, (0, -packed.shape[0] % 128)).reshape(-1, 128), sizes


def merge_kernel(inner, bit, here_ref, there_ref, out):
    count = here_ref.shape[0]
    for i in range(count):
        if inner:
            at, other = 2 * i + bit[0], 2 * i + 1 - bit[0]
        else:
            at, other = bit[0] * count + i, (1 - bit[0]) * count + i
        out[at] = here_ref[i]
        out[other] = there_ref[i]


def merge(here, there, bit, inner):
    shape = (2 * here.shape[0], *here.shape[1:])
    return pl.pallas_call(
        functools.partial(merge_kernel, inner),
        out_shape=jax.ShapeDtypeStruct(shape, here.dtype),
        in_specs=[SMEM, VMEM, VMEM],
        out_specs=VMEM,
        compiler_params=params(6),
        cost_estimate=COST,
        name="merge",
    )(bit.astype(jnp.int32).reshape(1), *map(in_hbm if here.dtype == bf16 else in_vmem, (here, there)))


def join_small(links, current, received, index, bit):
    return merge(current, received, (index >> bit) & 1, False)


def pack_shares_plain(links, owner, row, banks_here, sums, gain, maps):
    ndp, nmp = links.ndp, links.nmp
    channels = gain.shape[2]

    def by_owner(values):
        values = values.reshape(ndp, maps, nmp, channels)
        return values.transpose(0, 2, 1, 3)

    bank = sums[3].reshape(NS, nmp, channels).transpose(1, 0, 2)
    here = jnp.arange(ndp * banks_here, dtype=jnp.int32) == owner * banks_here + row
    bank = jnp.where(here[:, None, None, None], bank[None], 0.0)
    bank = bank.reshape(ndp, banks_here, nmp, NS, channels).transpose(0, 2, 1, 3, 4)
    bank = bank.reshape(ndp, nmp, banks_here * NS, channels)
    lines = [by_owner(sums[0]), by_owner(sums[1]), by_owner(sums[2]), bank, gain[:, :, None]]
    shares = jnp.concatenate(lines, 2)
    rows = D // (ndp * links.nz)
    shares = shares.reshape(ndp, nmp, -1)
    shares = jnp.pad(shares, ((0, 0), (0, 0), (0, -shares.shape[2] % (128 * rows))))
    shares = shares.reshape(ndp, nmp // 2, 2, rows, -1)
    parts = [in_order(links, shares[:, :, c], c) for c in range(2)]
    return jnp.where(links.core == 0, jnp.stack(parts), jnp.stack(parts[::-1]))


class Live:
    pass


def fence(live, transfers=(), waits=()):
    held = dict(vars(live))
    tree = (held, [t.outgoing for t in transfers], [t.received for t in waits])
    leaves, form = jax.tree.flatten(tree)
    held, states, received = jax.tree.unflatten(form, lax.optimization_barrier(leaves))
    vars(live).update(held)
    for t, state in zip(transfers, states):
        t.outgoing = state
    for t, values in zip(waits, received):
        t.received = values
    for t in waits:
        t.join()


class Gather:
    def __init__(self, links, values):
        self.links = links
        self.state = [values[None]]
        self.kind = None

    def along_z(self, bit, first=0, last=None):
        self.kind, self.bit, self.span = "z", bit, slice(first, last)
        self.received = [self.links.mp_swap(piece, bit) for piece in self.state[self.span]]

    def along_dp(self, level):
        self.kind = "d"
        self.received = [self.links.fan(piece, level) for piece in self.state]

    def more_dp(self):
        self.count = 2 * len(self.state)
        self.ahead = [self.links.fan(piece, 0) for piece in self.state]
        self.received = self.received + self.ahead

    def last_dp(self, first, last):
        if first == 0:
            self.count = len(self.state)
        last = self.count if last is None else last
        self.kind = "d"
        self.received = [self.links.fan(piece, 0) for piece in self.state[first:last]]

    @property
    def outgoing(self):
        return self.state

    @outgoing.setter
    def outgoing(self, values):
        self.state = values

    def join(self):
        if self.kind == "d":
            self.state = self.state + self.received
        else:
            mine = (self.links.mp >> self.bit) & 1
            joined = [
                merge(piece, received, mine, True)
                for piece, received in zip(self.state[self.span], self.received)
            ]
            self.state = self.state[: self.span.start] + joined + (
                [] if self.span.stop is None else self.state[self.span.stop :]
            )
        self.received = None

    def first_z(self):
        for bit in reversed(range(2, self.links.mp_bits)):
            if self.received is not None:
                self.join()
            self.along_z(bit)

    def along_z_but_last(self, first, last):
        for bit in reversed(range(2, self.links.mp_bits)):
            if self.received is not None:
                self.join()
            self.along_z(bit, first, last)

    def first_dp(self):
        self.received = None
        for level in reversed(range(1, self.links.dp_bits)):
            if self.received is not None:
                self.join()
            self.along_dp(level)

    received = None

    def blocks(self):
        return [piece.reshape(-1, piece.shape[2]) for piece in self.state]


def add_kernel(axis, keep_ref, recv_ref, *outs):
    part = keep_ref.shape[axis] // len(outs)
    for i, out in enumerate(outs):
        span = (slice(None),) * axis + (slice(i * part, (i + 1) * part),)
        total = keep_ref[span].astype(f32) + recv_ref[span].astype(f32)
        out[...] = total.astype(out.dtype)


def mix_kernel(middle_ref, own_ref, recv_ref, out_ref):
    total = middle_ref[...] + (own_ref[...] + recv_ref[...].astype(f32))
    out_ref[...] = total.astype(bf16)


def mix(middle, own, received):
    return pl.pallas_call(
        mix_kernel,
        out_shape=jax.ShapeDtypeStruct(middle.shape, bf16),
        in_specs=[VMEM] * 3,
        out_specs=VMEM,
        compiler_params=params(10),
        cost_estimate=COST,
        name="mix",
    )(middle, own, received)


def add_split(keep, received, axis, dtype=None):
    shape = list(keep.shape)
    if axis is False:
        outs = (jax.ShapeDtypeStruct(shape, dtype or keep.dtype),)
    elif axis is None:
        outs = (jax.ShapeDtypeStruct(shape, f32),)
    else:
        shape[axis] //= 2
        outs = (jax.ShapeDtypeStruct(shape, keep.dtype),) * 2
    return pl.pallas_call(
        functools.partial(add_kernel, axis or 0),
        out_shape=outs,
        in_specs=[VMEM] * 2,
        out_specs=(VMEM,) * len(outs),
        compiler_params=params(10),
        cost_estimate=COST,
        name="add_split",
    )(keep, received)


class Scatter:
    def __init__(self, links, keep, send, *far):
        self.links = links
        self.state = [keep, send, *far]
        self.steps = [("d", level) for level in range(links.dp_bits)]
        self.steps += [("z", bit) for bit in range(1, links.mp_bits)]
        self.result = None

    def start(self):
        kind, index = self.steps[0]
        swap = self.links.mp_swap if kind == "z" else self.links.fan
        self.received = [swap(part, index) for part in self.state[1::2]]

    @property
    def outgoing(self):
        return self.state[1::2]

    @outgoing.setter
    def outgoing(self, values):
        self.state[1::2] = values

    def start_far(self):
        self.received = [self.links.fan(self.state.pop(), 0)]
        self.parts = "far"

    def start_near(self):
        self.received = [self.links.fan(self.state[1], 0)]
        self.parts = "near"

    parts = None

    def join(self):
        if self.parts == "far":
            self.parts = None
            keep_far = self.state.pop()
            self.state.append(add_split(keep_far, self.received[0], False)[0])
            return
        keep, received = self.state[0], self.received
        self.steps.pop(0)
        if self.parts == "near":
            self.parts = None
            received, far = lax.optimization_barrier((received[0], self.state[2]))
            self.state = [add_split(keep, received, False)[0], far]
        elif len(received) == 2:
            self.state = [
                add_split(keep, received[0], False)[0],
                add_split(self.state[2], received[1], False)[0],
            ]
        elif not self.steps:
            self.result = add_split(keep, received[0], None)[0][0, 0]
            self.state = []
        else:
            axis = 1 if self.steps[0][0] == "z" else 0
            self.state = list(add_split(keep, received[0], axis))

    def finish(self):
        while self.steps:
            self.start()
            self.join()


def body(
    tokens, cotangent, first_gain, second_gain, w_query, w_key, w_value, w_out, w_up, w_down,
    state_rate, state_in, state_out, state_bank, prev_link,
):
    links = Links()
    ndp, nmp, nz = links.ndp, links.nmp, links.nz
    rows = tokens.shape[0]
    per_window = LEN // BLK
    place_in = links.mp % per_window
    window = links.dp * (nmp // per_window) + links.mp // per_window
    link = lax.dynamic_index_in_dim(prev_link, window, keepdims=False)
    info = jnp.stack([links.block_at(p) for p in range(ndp)] + [links.z, links.core]).astype(jnp.int32)
    order = []
    for b in range(ndp):
        far = links.dp ^ b
        order.append(jnp.where(links.core == 0, swap_bits(far, links.dp_bits), far))
    order = jnp.stack(order).astype(jnp.int32)
    attend_info = jnp.stack([links.core, (place_in != 0).astype(jnp.int32)]).astype(jnp.int32)

    channels = state_rate.shape[0]
    maps_here = state_rate.shape[1]
    banks_here = state_bank.shape[0]

    def full_map(values):
        values = values.reshape(ndp, nmp, maps_here, channels).transpose(0, 2, 1, 3)
        return values.reshape(NS, 8, 128)

    chunk = FF // nmp
    groups = 2 if chunk >= 256 else 1
    width = chunk // groups
    mats_keep, mats_send, feed_rows, *late_rows = prepare(
        links, groups, links.core.astype(jnp.int32).reshape(1),
        (w_query, w_key, w_value, w_out), w_up, w_down.T,
    )

    def chip_rows(keep, send):
        return by_core(links, keep, links.core_swap(send), 0)

    pieces = [
        first_gain, second_gain, state_rate.T, state_in.T, state_out.T,
        state_bank.transpose(0, 2, 1),
    ]
    small, sizes = pack(pieces)
    v, u = Live(), Live()
    v.tokens, v.cotangent = tokens, cotangent
    small = small[None]
    v.small = join_small(links, small, links.core_swap(small), links.mp, 0)
    attn = Gather(links, chip_rows(mats_keep, mats_send))
    v.feed_rows = feed_rows
    late_feeds = [Gather(links, chip_rows(*late_rows))] if late_rows else []
    fence(v, [attn, *late_feeds])

    for bit in range(1, links.mp_bits):
        v.small = join_small(links, v.small, links.mp_swap(v.small, bit), links.mp, bit)
    fence(v, [attn])

    feed_weights = lax.all_gather(v.feed_rows, AXES, axis=0, tiled=True)
    del v.feed_rows
    attn.first_z()
    for bit in range(links.dp_bits):
        v.small = join_small(links, v.small, links.dp_swap(v.small, bit), links.dp, bit)
    fence(v, [attn], [attn])
    attn.along_z(1)
    small = v.small.reshape(ndp, nmp, -1)
    del v.small
    starts = [sum(sizes[:i]) for i in range(len(sizes))]
    gain_one, gain_two, rate, gain_in, gain_out, banks = (
        small[:, :, a : a + n] for a, n in zip(starts, sizes)
    )
    v.gain_one = lax.reduce_precision(gain_one.reshape(1, D), 8, 7)
    v.gain_two = lax.reduce_precision(gain_two.reshape(1, D), 8, 7)
    u.rate, u.gain_in, u.gain_out = full_map(rate), full_map(gain_in), full_map(gain_out)
    banks = banks.reshape(ndp, nmp, banks_here, NS, channels)
    bank = lax.dynamic_index_in_dim(banks, link // banks_here, 0, keepdims=False)
    bank = lax.dynamic_index_in_dim(bank, link % banks_here, 1, keepdims=False)
    u.initial = bank.transpose(1, 0, 2).reshape(NS, 8, 128)
    half_blocks = float(BLK)
    v.scal = jnp.stack(
        [place_in.astype(f32) * half_blocks - CTX, (place_in != 0).astype(f32)]
    )
    v.steps, v.steps_back = [], []
    for bit in range(bits_of(per_window)):
        mine = ((links.mp >> bit) & 1).astype(f32)
        inside = (place_in % (1 << bit)).astype(f32)
        span = jnp.float32(half_blocks * (1 << bit))
        v.steps.append(jnp.stack([mine, inside * half_blocks, span]))
        v.steps_back.append(
            jnp.stack([mine, ((1 << bit) - 1 - inside) * half_blocks, span])
        )

    def exchange(bit):
        received = links.mp_swap(v.total, bit)
        v.total, v.before = exchange_step(v.steps[bit], v.total, received, v.before, u.rate)

    u.normed_b, tail = norm_first(v.tokens, v.gain_one)
    u.tail = links.window_shift(tail, 1)
    v.total = scan_own(u.normed_b, u.rate)
    fence(v, [attn], [attn])

    attn.first_dp()
    attn.more_dp()
    v.total = scan_tail(u.tail, v.total, u.rate)
    v.before = jnp.zeros_like(v.total)
    for bit in range(2):
        exchange(bit)
    v.cot_t = v.cotangent.T
    fence(v, [attn, *late_feeds], [attn])
    attn.last_dp(max(ndp // 4, 1), None)
    for bit in range(2, bits_of(per_window)):
        exchange(bit)
    v.inputs_kv = context_states(
        v.scal, u.tail, u.normed_b, v.before, u.initial, u.rate, u.gain_in, u.gain_out
    )
    fence(v, [attn, *late_feeds], [attn])

    for gather in late_feeds:
        gather.first_z()
    v.w_own = place(links, order, attn.blocks())
    attn.state = []
    v.w_other = links.core_swap(v.w_own)
    v.qkv_own = project(v.inputs_kv, v.w_own)
    u.cot_par, u.cot_par_t = links.core_swap(v.cotangent), links.core_swap(v.cot_t)
    fence(v, late_feeds, late_feeds)
    for gather in late_feeds:
        gather.along_z(1)
    v.inputs_par = links.core_swap(v.inputs_kv)
    u.qkv_other = project(v.inputs_kv, v.w_other)
    v.attended = attend(attend_info, v.qkv_own, u.qkv_other)
    fence(v, late_feeds, late_feeds)
    for gather in late_feeds:
        gather.first_dp()
    u.middle, u.second_b, u.second_t = middle_norm(
        attend_info, v.attended, v.tokens, v.w_own, v.w_other, v.gain_two
    )
    u.second_par, u.second_par_t = links.core_swap(u.second_b), links.core_swap(u.second_t)
    v.feed_weights = feed_weights
    fence(v, late_feeds, late_feeds)

    scatters = []
    earlier = None
    for g in range(groups):
        last = g == groups - 1
        acts = (
            u.second_b, u.second_par, v.cotangent, u.cot_par,
            u.second_t, u.second_par_t, v.cot_t, u.cot_par_t,
        )
        if g == 0:
            weights = [v.feed_weights]
            for gather in late_feeds:
                gather.last_dp(0, None)
        else:
            weights = late_feeds[0].blocks()
        *u.sums, keep, keep_far, send, send_far = feed(
            links, info, acts, weights, nz * width, g, groups, earlier, last
        )
        if g == 0:
            v.attended_par = links.core_swap(v.attended)
        waits = list(scatters)
        scatters.append(Scatter(links, keep, send, keep_far, send_far))
        fence(v, scatters, waits + (late_feeds if not last else []))
        if not last:
            scatters[g].start()
        earlier = u.sums
    first, second = scatters[0], scatters[-1]
    both = [first, second] if groups > 1 else [first]
    u.mix_own, v.mix_par, u.back_own, back_par = u.sums
    del v.feed_weights, v.cot_t

    split = groups > 1 and ndp >= 4
    if split:
        first.start()
        second.start_far()
    else:
        second.start()
    v.back_recv = links.core_swap(back_par)
    v.grad_middle, v.branch_own, branch_other, v.grad_attended, v.grad_gain_two = back_middle(
        attend_info, u.middle, u.back_own, v.back_recv, v.cotangent, v.gain_two, v.w_own,
        v.w_other,
    )
    v.branch_par = links.core_swap(branch_other)
    v.grad_gain_two = v.grad_gain_two.reshape(ndp, nmp, -1)
    gain_len = v.grad_gain_two.shape[2]
    v.grad_gain_two = jnp.pad(v.grad_gain_two, ((0, 0), (0, 0), (0, channels - gain_len)))
    u.g_own, u.g_other = attend_back(attend_info, v.qkv_own, u.qkv_other, v.grad_attended)
    fence(v, both, both)

    def exchange_back(bit):
        received = links.mp_swap(v.total, bit)
        v.total, v.after = exchange_back_step(
            v.steps_back[bit], v.total, received, v.after, u.rate
        )

    if split:
        second.start_near()
    v.g_par = links.core_swap(u.g_other)
    v.grad_context = back_project(u.g_own, u.g_other, v.w_own, v.w_other, 0, CTX, bf16)
    v.lows = state_low(v.grad_context, u.rate)
    v.total = v.lows[0]
    v.after = jnp.zeros_like(v.total)
    sums = state_sums(
        v.scal, v.grad_context, u.tail, v.before, v.lows, u.initial, u.rate, u.gain_in, u.gain_out
    )
    bank_owner = link // banks_here
    mat_rows = D // (ndp * nz)
    whole_lines = channels == 128 and banks_here == 1
    if whole_lines:
        shares = pack_shares(
            links, info, bank_owner.reshape(1), sums, v.grad_gain_two, maps_here, mat_rows
        )
    else:
        shares = pack_shares_plain(
            links, bank_owner, link % banks_here, banks_here, sums, v.grad_gain_two, maps_here
        )
    v.shares = add_split(shares[0], links.core_swap(shares[1].astype(bf16)), False, bf16)[0]
    for bit in range(2):
        exchange_back(bit)
    fence(v, both, [second] if split else [])

    u.mix_recv = links.core_swap(v.mix_par)
    for scatter in both:
        scatter.start()
    mats = Scatter(
        links,
        *weight_grads(
            links, info, v.inputs_kv, v.inputs_par, u.g_own, v.g_par, v.attended,
            v.attended_par, v.branch_own, v.branch_par, v.shares,
        ),
    )
    for bit in range(2, bits_of(per_window)):
        exchange_back(bit)
    fence(v, [*both, mats], both)

    mats.start()
    for scatter in both:
        scatter.start()
    tail_sent = sent_tail(v.grad_context, v.after, u.rate, u.gain_in, u.gain_out)
    v.last_sent = links.window_shift(tail_sent, -1)
    v.own_sent = sent_own(v.after, u.rate, u.gain_in, u.gain_out)
    v.part = back_project(u.g_own, u.g_other, v.w_own, v.w_other, CTX, BLK, f32)
    v.grad_tokens, grad_gain_one = back_first(
        v.tokens, v.part, v.own_sent, v.last_sent, v.grad_middle, v.gain_one
    )
    v.gain_parts = grad_gain_one.reshape(ndp * nmp, -1)
    fence(v, [*both, mats], [mats, *both])
    mats.start()
    late = [second] if second.steps else []
    for scatter in late:
        scatter.start()
    gain_parts = lax.all_to_all(v.gain_parts, AXES, split_axis=0, concat_axis=0, tiled=True)
    v.share_one = jnp.sum(gain_parts, axis=0)
    fence(v, [*both, mats], [mats, *late])
    mats.start()
    v.mixed = mix(u.middle, u.mix_own, u.mix_recv)
    for scatter in both:
        scatter.finish()
    v.results = [scatter.result for scatter in both]
    fence(v, [mats], [mats])
    mats.start()
    grad_up = jnp.concatenate([result[0] for result in v.results], 1)
    grad_down = jnp.concatenate([result[1] for result in v.results], 1).T
    mats.join()
    mats.finish()
    grad_tokens = v.grad_tokens
    mixed, share_one = v.mixed, v.share_one
    mats_share = mats.result
    line = 4 * HALF
    extra = mats_share[:, line:]
    if not whole_lines:
        lines = 3 * maps_here + banks_here * NS + 1
        extra = extra.reshape(-1)[: lines * channels].reshape(lines, channels)
    grad_maps = [
        extra[i * maps_here : (i + 1) * maps_here].T for i in range(3)
    ]
    bank_end = 3 * maps_here + banks_here * NS
    grad_bank = extra[3 * maps_here : bank_end].reshape(banks_here, NS, channels)
    grad_bank = grad_bank.transpose(0, 2, 1)
    share_two = extra[bank_end, :gain_len]
    mine_rows = mats_share[:, :line].reshape(2, mat_rows // 2, 4, HALF)
    rows_keep = jnp.where(links.core == 0, mine_rows[0], mine_rows[1])
    rows_send = jnp.where(links.core == 0, mine_rows[1], mine_rows[0])
    grad_rows = by_core(links, rows_keep, links.core_swap(rows_send), 2)
    return (
        mixed, grad_tokens, share_one, share_two,
        grad_rows[:, 0], grad_rows[:, 1], grad_rows[:, 2], grad_rows[:, 3],
        grad_up, grad_down, grad_maps[0], grad_maps[1], grad_maps[2], grad_bank,
    )


def solution(mesh):
    split = P(AXES, None)
    gain = P(AXES)
    maps = P("mp", "dp")
    bank = P("dp", "mp", None)
    return jax.shard_map(
        body,
        mesh=mesh,
        in_specs=(
            split, split, gain, gain, split, split, split, split, split, P(None, AXES),
            maps, maps, maps, bank, P(),
        ),
        out_specs=(
            split, split, gain, gain, split, split, split, split, P("dp", "mp"), P("mp", "dp"),
            maps, maps, maps, bank,
        ),
        check_vma=False,
    )
```
